32 devices in a mesh: dp: 8 (over y, x, core), seq: 4 (over z).
Axes of the slice: x: 2, y: 2, z: 4, core: 2. Of those that a mesh axis runs over, the one named last changes fastest.
Arguments:
- queries: bfloat16 [8, 512, 1536], P('dp', 'seq'), may hold values from -120 to 120
- keys: bfloat16 [8, 512, 1536], P('dp', 'seq'), may hold values from -4.5 to 4.5
- values: bfloat16 [8, 512, 1536], P('dp', 'seq'), may hold values from -6 to 6
- grad_out: bfloat16 [8, 512, 1536], P('dp', 'seq'), may hold values from -6 to 6
- conv_weight: float32 [31, 1536], replicated, may hold values from -2 to 2
- conv_bias: float32 [1536], replicated, may hold values from -4 to 4
- lengths: int32 [8], P('dp'), may hold values from 128 to 512, as said below
Outputs:
- query_grad: bfloat16 [8, 512, 1536], P('dp', 'seq')
- key_grad: bfloat16 [8, 512, 1536], P('dp', 'seq')
- value_grad: bfloat16 [8, 512, 1536], P('dp', 'seq')
- weight_grad: float32 [31, 1536], P(None, 'seq')
- bias_grad: float32 [1536], P('seq')
The draws below stay inside these ranges and needn't reach their ends.
Inputs may be any that keep to these rules, and one draw needn't show every extreme that they name: `lengths`: each utterance's valid frames are its first ones; in every draw some utterance has all 512 frames valid.
All inputs are finite; a program needn't handle non-finite values.
Results may differ from the reference program's by a relative error of at most 0.024.
Values may be sent and summed in bfloat16 or wider, within the bound.
No kernel may reach another device: no remote copies, remote signals or barrier semaphores. Data moves between devices by JAX's collectives and lax.ppermute only.
A program may use at most 64 MiB of HBM per device.

```python
import math
import jax
import jax.numpy as jnp
from jax import lax

D = 1536
HEADS = 16
KERNEL = 31
UTTS = 8
LENGTH = 512


def shared_keys(key):
    return jnp.clip(jax.random.normal(key, (UTTS, LENGTH, D), jnp.float32), -4.5, 4.5)


def draw_keys(key, part):
    base = shared_keys(key)
    return base.astype(jnp.bfloat16)


def draw_queries(key, part):
    key = jax.random.fold_in(key, 22)
    first = jax.random.fold_in(key, 0)
    drawn = 2.0 * jnp.clip(jax.random.normal(first, (UTTS, LENGTH, D), jnp.float32), -4.5, 4.5)
    return drawn.astype(jnp.bfloat16)


def draw_lengths(key, part):
    key = jax.random.fold_in(key, 3)
    first, second = jax.random.split(key)
    counts = jax.random.randint(first, (UTTS,), LENGTH // 4, LENGTH + 1, dtype=jnp.int32)
    full = jax.random.randint(second, (), 0, UTTS, dtype=jnp.int32)
    return jnp.where(jnp.arange(UTTS, dtype=jnp.int32) == full, LENGTH, counts).astype(jnp.int32)


def strengthened(values, stream_key, source, target, blocks, factor):
    owner, partner = [(jnp.arange(values.shape[axis_at]) // (values.shape[axis_at] // blocks)).reshape([-1 if axis == axis_at else 1 for axis in range(values.ndim)]) for axis_at in (source, target)]
    chosen = jax.random.permutation(stream_key, blocks)[partner]
    strong = (owner == chosen) | (owner == (partner + blocks // 2) % blocks)
    return jnp.where(strong, factor * values, values)


def levels(own_key, extent, cuts, smallest, high):
    level, own = 1.0, jax.random.fold_in(own_key, 6)
    for position, parts in cuts:
        steps = jnp.exp(jax.random.uniform(jax.random.fold_in(own, position), (parts,), jnp.float32, smallest / len(cuts), high / len(cuts)))
        level = level * jnp.repeat(steps, extent[position] // parts).reshape([-1 if axis == position else 1 for axis in range(len(extent))])
    return level


def centred(key, shape, scale, reach, pieces=(), kind=jnp.bfloat16):
    entries = jax.random.normal(key, shape, jnp.float32) * scale
    if len(pieces) > 0:
        entries = levels(key, shape, pieces, -0.22, 0.18) * entries
    return jnp.clip(entries, min=-reach, max=reach).astype(kind)


def gaussian_with(stream_key, dims, spread, most, pieces, heavy, kind=jnp.bfloat16):
    entries = spread * jax.random.normal(stream_key, dims, jnp.float32)
    if pieces:
        entries = entries * levels(stream_key, dims, pieces, -0.22, 0.18)
    return jnp.clip(strengthened(entries, jax.random.fold_in(stream_key, 3), *heavy), -most, most).astype(kind)


def setup_inputs(seed: int = 0) -> dict:
    key_of = jax.random.split(jax.random.key(seed), 8)
    queries = draw_queries(jax.random.fold_in(key_of[7], 71), 0)
    keys = draw_keys(jax.random.fold_in(key_of[7], 71), 0)
    values = centred(key_of[2], (UTTS, LENGTH, D), 1.0, 6.0, ((0, 8), (1, 4)))
    grad_out = gaussian_with(key_of[3], (UTTS, LENGTH, D), 1.0, 6.0, ((0, 8), (1, 4)), (1, 2, 4, 2.0))
    conv_weight = centred(key_of[4], (KERNEL, D), (KERNEL // 4) ** -0.5, 2.0, (), jnp.float32)
    conv_bias = centred(key_of[5], (D,), 1.0, 4.0, (), jnp.float32)
    lengths = draw_lengths(jax.random.fold_in(key_of[7], 71), 0)
    return {"queries": queries, "keys": keys, "values": values, "grad_out": grad_out, "conv_weight": conv_weight, "conv_bias": conv_bias, "lengths": lengths}


masked_score = -1e+30

def rounded(array):
    return lax.optimization_barrier(array.astype(jnp.bfloat16)).astype(jnp.float32)

def probs_rows(query_block, key_all, key_valid, score_scale):
    scores = jnp.einsum('qhd,khd->hqk', query_block, key_all) * score_scale
    scores = jnp.where(key_valid[None, None, :], scores, masked_score)
    row_top = lax.optimization_barrier(jnp.max(scores, axis=-1, keepdims=True))
    exped = jnp.exp(scores - row_top)
    return exped / lax.optimization_barrier(jnp.sum(exped, axis=-1, keepdims=True))

def utterance(query, keyin, value, grad, length, weight, bias):
    seq_len, width = query.shape
    head_dim = width // HEADS
    rim = KERNEL // 2
    block_rows = math.gcd(seq_len, 512)
    count = seq_len // block_rows
    score_scale = 1.0 / math.sqrt(head_dim)
    valid = jnp.arange(seq_len, dtype=jnp.int32) < length
    query_f = query.astype(jnp.float32).reshape(seq_len, HEADS, head_dim)
    key_f = keyin.astype(jnp.float32).reshape(seq_len, HEADS, head_dim)
    value_f = value.astype(jnp.float32).reshape(seq_len, HEADS, head_dim)
    query_blocks = query_f.reshape(count, block_rows, HEADS, head_dim)

    def block_out(query_block):
        probs = probs_rows(query_block, key_f, valid, score_scale)
        return jnp.einsum('hqk,khd->qhd', rounded(probs), value_f)
    attended = lax.map(block_out, query_blocks).reshape(seq_len, width)
    attended = rounded(attended * valid[:, None].astype(jnp.float32))
    padded = jnp.pad(attended, ((rim, rim), (0, 0)))
    conv_pre = jnp.zeros((seq_len, width), jnp.float32) + bias
    for j in range(KERNEL):
        conv_pre = conv_pre + weight[j] * padded[j:j + seq_len]
    sig = jax.nn.sigmoid(conv_pre)
    pre_grad = rounded(grad.astype(jnp.float32) * sig * (1.0 + conv_pre * (1.0 - sig)))
    weight_part = jnp.stack([lax.optimization_barrier(jnp.sum(pre_grad * padded[j:j + seq_len], axis=0)) for j in range(KERNEL)])
    bias_part = lax.optimization_barrier(jnp.sum(pre_grad, axis=0))
    grad_pad = jnp.pad(pre_grad, ((rim, rim), (0, 0)))
    attn_grad = grad.astype(jnp.float32)
    for j in range(KERNEL):
        attn_grad = attn_grad + weight[j] * grad_pad[2 * rim - j:2 * rim - j + seq_len]
    attn_grad = rounded(attn_grad * valid[:, None].astype(jnp.float32))
    grad_blocks = attn_grad.reshape(count, block_rows, HEADS, head_dim)

    def block_step(carry, inputs):
        key_acc, value_acc = carry
        query_block, grad_block = inputs
        probs = probs_rows(query_block, key_f, valid, score_scale)
        score_grad = jnp.einsum('qhd,khd->hqk', grad_block, value_f)
        row_delta = lax.optimization_barrier(jnp.sum(probs * score_grad, axis=-1, keepdims=True))
        diff = rounded(probs * (score_grad - row_delta))
        query_part = (jnp.einsum('hqk,khd->qhd', diff, key_f) * score_scale).astype(jnp.bfloat16)
        key_acc = key_acc + jnp.einsum('hqk,qhd->khd', diff, query_block)
        value_acc = value_acc + jnp.einsum('hqk,qhd->khd', rounded(probs), grad_block)
        return ((key_acc, value_acc), query_part)
    zeros = jnp.zeros((seq_len, HEADS, head_dim), jnp.float32)
    (key_acc, value_acc), query_parts = lax.scan(block_step, (zeros, zeros), (query_blocks, grad_blocks))
    query_out = query_parts.reshape(seq_len, width)
    key_out = (key_acc * score_scale).astype(jnp.bfloat16).reshape(seq_len, width)
    value_out = value_acc.astype(jnp.bfloat16).reshape(seq_len, width)
    return (query_out, key_out, value_out, weight_part, bias_part)

def reference(queries, keys, values, grad_out, conv_weight, conv_bias, lengths):

    def per_utterance(inputs):
        query, keyin, value, grad, length = inputs
        return utterance(query, keyin, value, grad, length, conv_weight, conv_bias)
    query_grad, key_grad, value_grad, weight_parts, bias_parts = lax.map(per_utterance, (queries, keys, values, grad_out, lengths))
    return (query_grad, key_grad, value_grad, lax.optimization_barrier(jnp.sum(weight_parts, axis=0)), lax.optimization_barrier(jnp.sum(bias_parts, axis=0)))
```

```python
import functools
import math

import jax
import jax.numpy as jnp
from jax import lax
from jax.experimental import pallas as pl
from jax.experimental.pallas import tpu as pltpu
from jax.sharding import PartitionSpec as P

HEADS = 16
KERNEL = 31
RIM = KERNEL // 2
PAD = 16
masked_score = -1e30


def head_window(head, head_dim, width):
    first = head * head_dim // 128 * 128
    last = min(-(-(head + 1) * head_dim // 128) * 128, width)
    return first, last


def kernel(
    head_dim,
    block,
    length_ref,
    x_ref,
    weight_ref,
    bias_ref,
    out_ref,
    taps_ref,
    q_t,
    k_t,
    v_t,
    a_t,
    probs,
    shifted,
    attn_grad,
    grad_pad,
    key_acc,
    value_acc,
):
    parts, _, frames, width = x_ref.shape
    rows = parts * frames
    heads = width // head_dim
    blocks = rows // block
    scale = 1.0 / math.sqrt(head_dim)
    log_scale = scale * math.log2(math.e)
    length = length_ref[0]
    f32, bf16 = jnp.float32, jnp.bfloat16

    def rows_of(which):
        return x_ref[:, which].reshape(rows, width)

    for part in range(parts):
        at = pl.ds(part * frames, frames)
        q_t[:, at] = x_ref[part, 0].T
        k_t[:, at] = x_ref[part, 1].T
        v_t[:, at] = x_ref[part, 2].T

    def masked_rows(ref, head, cols):
        first, last = head_window(head, head_dim, width)
        low, high = head * head_dim, (head + 1) * head_dim
        pieces = []
        if low > first:
            pieces.append(jnp.zeros((low - first, block), bf16))
        pieces.append(ref[low:high, cols])
        if last > high:
            pieces.append(jnp.zeros((last - high, block), bf16))
        return jnp.concatenate(pieces, axis=0) if len(pieces) > 1 else pieces[0]

    def head_lanes(array, head):
        first, last = head_window(head, head_dim, width)
        low, high = head * head_dim, (head + 1) * head_dim
        if low == first and high == last:
            return array
        lane = first + lax.broadcasted_iota(jnp.int32, array.shape, 1)
        return jnp.where((lane >= low) & (lane < high), array, jnp.zeros_like(array))

    def forward(index, head):
        cols = pl.ds(pl.multiple_of(index * block, block), block)
        first, last = head_window(head, head_dim, width)
        keys = x_ref[:, 1, :, first:last].reshape(rows, last - first)
        scores = jnp.dot(keys, masked_rows(q_t, head, cols), preferred_element_type=f32)
        key_at = lax.broadcasted_iota(jnp.int32, scores.shape, 0)
        scores = jnp.where(key_at < length, scores, masked_score)
        exped = jnp.exp2((scores - jnp.max(scores, axis=0, keepdims=True)) * log_scale)
        found = exped * (1.0 / jnp.sum(exped, axis=0, keepdims=True))
        probs[head, :, cols] = found
        low, high = head * head_dim, (head + 1) * head_dim
        out = jnp.dot(v_t[low:high, :], found.astype(bf16), preferred_element_type=f32)
        frame_at = index * block + lax.broadcasted_iota(jnp.int32, out.shape, 1)
        a_t[low:high, cols] = jnp.where(frame_at < length, out, 0.0).astype(bf16)

    def each_block(body):
        if blocks == 1:
            for head in range(heads):
                body(0, head)
        else:

            def step(index, carry):
                for head in range(heads):
                    body(index, head)
                return carry

            lax.fori_loop(0, blocks, step, 0)

    each_block(forward)

    tall = shifted.shape[1]

    def shift_all(source_rows):
        shifted[0, 0:PAD, :] = jnp.zeros((PAD, width), f32)
        shifted[0, PAD + rows : tall, :] = jnp.zeros((tall - PAD - rows, width), f32)
        for part in range(parts):
            at = part * frames
            shifted[0, PAD + at : PAD + at + frames, :] = source_rows(part)
        for s in range(1, 8):
            shifted[s, 0 : tall - 8, :] = shifted[0, s : tall - 8 + s, :]

    shift_all(lambda part: a_t[:, pl.ds(part * frames, frames)].T.astype(f32))

    chunk = 64
    lanes = [(at, min(at + 128, width)) for at in range(0, width, 128)]

    def filtered(row, low, high, reverse):
        total = None
        for offset in range(1, KERNEL + 1):
            s, a = offset % 8, offset // 8 * 8
            tap = KERNEL - offset if reverse else offset - 1
            term = weight_ref[tap : tap + 1, low:high] * shifted[s, pl.ds(row + a, chunk), low:high]
            total = term if total is None else total + term
        return total

    for low, high in lanes:

        def conv_step(index, carry, low=low, high=high):
            row = pl.multiple_of(index * chunk, chunk)
            conv_pre = filtered(row, low, high, False) + bias_ref[0:1, low:high]
            sig = 1.0 / (1.0 + jnp.exp(-conv_pre))
            part = row // frames
            grad = x_ref[part, 3, pl.ds(pl.multiple_of(row % frames, chunk), chunk), low:high]
            pre = grad.astype(f32) * (sig * (1.0 + conv_pre * (1.0 - sig)))
            pre = pre.astype(bf16).astype(f32)
            grad_pad[pl.ds(row, chunk), low:high] = pre
            new = []
            for offset in range(1, KERNEL + 1):
                s, a = offset % 8, offset // 8 * 8
                term = pre * shifted[s, pl.ds(row + a, chunk), low:high]
                new.append(carry[offset - 1] + jnp.sum(term.reshape(chunk // 8, 8, high - low), axis=0))
            new.append(carry[KERNEL] + jnp.sum(pre.reshape(chunk // 8, 8, high - low), axis=0))
            return tuple(new)

        zero = jnp.zeros((8, high - low), f32)
        sums = lax.fori_loop(0, rows // chunk, conv_step, (zero,) * (KERNEL + 1))
        for tap in range(KERNEL + 1):
            taps_ref[tap : tap + 1, low:high] = jnp.sum(sums[tap], axis=0, keepdims=True)

    shift_all(lambda part: grad_pad[pl.ds(part * frames, frames), :])

    for low, high in lanes:

        def back_step(index, carry, low=low, high=high):
            row = pl.multiple_of(index * chunk, chunk)
            part = row // frames
            grad = x_ref[part, 3, pl.ds(pl.multiple_of(row % frames, chunk), chunk), low:high]
            total = grad.astype(f32) + filtered(row, low, high, True)
            frame_at = row + lax.broadcasted_iota(jnp.int32, total.shape, 0)
            total = jnp.where(frame_at < length, total, 0.0)
            attn_grad[pl.ds(row, chunk), low:high] = total.astype(bf16)
            return carry

        lax.fori_loop(0, rows // chunk, back_step, 0)

    for part in range(parts):
        at = pl.ds(part * frames, frames)
        a_t[:, at] = attn_grad[at, :].T

    key_acc[...] = jnp.zeros_like(key_acc)
    value_acc[...] = jnp.zeros_like(value_acc)

    def backward(index, head):
        cols = pl.ds(pl.multiple_of(index * block, block), block)
        first, last = head_window(head, head_dim, width)
        low, high = head * head_dim, (head + 1) * head_dim
        values = x_ref[:, 2, :, first:last].reshape(rows, last - first)
        score_grad = jnp.dot(values, masked_rows(a_t, head, cols), preferred_element_type=f32)
        found = probs[head, :, cols]
        delta = jnp.sum(found * score_grad, axis=0, keepdims=True)
        diff = (found * (score_grad - delta)).astype(bf16)
        value_acc[:, first:last] += jnp.dot(
            found.astype(bf16),
            head_lanes(attn_grad[cols, first:last], head),
            preferred_element_type=f32,
        )
        per = block // frames
        queries = x_ref[pl.ds(index * per, per), 0, :, first:last].reshape(block, last - first)
        key_acc[:, first:last] += jnp.dot(
            diff, head_lanes(queries, head), preferred_element_type=f32
        )
        query = jnp.dot(k_t[low:high, :], diff, preferred_element_type=f32)
        q_t[low:high, cols] = (query * scale).astype(bf16)

    each_block(backward)

    for part in range(parts):
        at = pl.ds(part * frames, frames)
        out_ref[part, 0] = q_t[:, at].T
        out_ref[part, 1] = (key_acc[at, :] * scale).astype(bf16)
        out_ref[part, 2] = value_acc[at, :].astype(bf16)


def local_work(moved, weight, bias, lengths, head_dim):
    parts, _, frames, width = moved.shape
    rows = parts * frames
    heads = width // head_dim
    block = math.gcd(rows, 512)
    tall = rows + 2 * PAD + 8
    bf16, f32 = jnp.bfloat16, jnp.float32
    whole = pl.BlockSpec(memory_space=pltpu.VMEM)
    return pl.pallas_call(
        functools.partial(kernel, head_dim, block),
        out_shape=(
            jax.ShapeDtypeStruct((parts, 3, frames, width), bf16),
            jax.ShapeDtypeStruct((KERNEL + 1, width), f32),
        ),
        in_specs=[pl.BlockSpec(memory_space=pltpu.SMEM), whole, whole, whole],
        out_specs=(whole, whole),
        scratch_shapes=[
            pltpu.VMEM((width, rows), bf16),
            pltpu.VMEM((width, rows), bf16),
            pltpu.VMEM((width, rows), bf16),
            pltpu.VMEM((width, rows), bf16),
            pltpu.VMEM((heads, rows, rows), f32),
            pltpu.VMEM((8, tall, width), f32),
            pltpu.VMEM((rows, width), bf16),
            pltpu.VMEM((rows, width), f32),
            pltpu.VMEM((rows, width), f32),
            pltpu.VMEM((rows, width), f32),
        ],
        compiler_params=pltpu.CompilerParams(vmem_limit_bytes=56 * 1024 * 1024),
        cost_estimate=pl.CostEstimate(
            flops=12 * heads * rows * rows * head_dim,
            bytes_accessed=14 * rows * width,
            transcendentals=heads * rows * rows,
        ),
    )(lengths, moved, weight, bias)


def on_device(queries, keys, values, grad_out, conv_weight, conv_bias, lengths):
    seq_count = lax.axis_size("seq")
    seq_rank = lax.axis_index("seq")
    utt_count, frames, width = queries.shape
    head_dim = width // HEADS
    share = width // seq_count
    weight = lax.dynamic_slice_in_dim(conv_weight, seq_rank * share, share, axis=1)
    bias = lax.dynamic_slice_in_dim(conv_bias, seq_rank * share, share, axis=0)[None]
    stacked = jnp.stack([queries[0], keys[0], values[0], grad_out[0]])
    stacked = stacked.reshape(4, frames, seq_count, share).transpose(2, 0, 1, 3)
    moved = lax.all_to_all(stacked, "seq", split_axis=0, concat_axis=0, tiled=True)
    grads, taps = local_work(moved, weight, bias, lengths, head_dim)
    taps = lax.psum(taps, "dp")
    back = lax.all_to_all(grads, "seq", split_axis=0, concat_axis=0, tiled=True)
    back = back.transpose(1, 2, 0, 3).reshape(3, 1, frames, width)
    return back[0], back[1], back[2], taps[:KERNEL], taps[KERNEL]


def solution(mesh):
    return jax.shard_map(
        on_device,
        mesh=mesh,
        in_specs=(
            P("dp", "seq", None),
            P("dp", "seq", None),
            P("dp", "seq", None),
            P("dp", "seq", None),
            P(),
            P(),
            P("dp"),
        ),
        out_specs=(
            P("dp", "seq", None),
            P("dp", "seq", None),
            P("dp", "seq", None),
            P(None, "seq"),
            P("seq"),
        ),
        check_vma=False,
    )
```

```python
import functools
import math

import jax
import jax.numpy as jnp
from jax import lax
from jax.experimental import pallas as pl
from jax.experimental.pallas import tpu as pltpu
from jax.sharding import PartitionSpec as P

HEADS = 16
KERNEL = 31
PAD = 16
masked_score = -1e30
VMEM = pl.BlockSpec(memory_space=pltpu.VMEM)
SMEM = pl.BlockSpec(memory_space=pltpu.SMEM)
LIMIT = 56 * 1024 * 1024
bf16, f32 = jnp.bfloat16, jnp.float32


def pack_kernel(count, chunks, rank_ref, *refs):
    arrays, outs, turned = refs[:4], refs[4:-1], refs[-1]
    rank = rank_ref[0]
    high = outs[0].shape[1]
    share = high * chunks
    for which, array in enumerate(arrays):
        turned[which] = array[0].T
        for distance in range(count):
            for chunk in range(chunks):
                first = pl.multiple_of((rank ^ distance) * share + chunk * high, 16)
                outs[chunk * count + distance][which] = turned[which, pl.ds(first, high), :]


def pack(rank, arrays, count, chunks):
    _, frames, width = arrays[0].shape
    high = width // count // chunks
    piece = jax.ShapeDtypeStruct((4, high, frames), bf16)
    outs = pl.pallas_call(
        functools.partial(pack_kernel, count, chunks),
        out_shape=(piece,) * (count * chunks),
        in_specs=[SMEM] + [VMEM] * 4,
        out_specs=(VMEM,) * (count * chunks),
        scratch_shapes=[pltpu.VMEM((4, width, frames), bf16)],
        compiler_params=pltpu.CompilerParams(vmem_limit_bytes=LIMIT),
        cost_estimate=pl.CostEstimate(
            flops=0, bytes_accessed=16 * frames * width, transcendentals=0
        ),
    )(rank, *arrays)
    return [outs[chunk * count : (chunk + 1) * count] for chunk in range(chunks)]


def unpack_kernel(count, chunks, rank_ref, *refs):
    pieces, outs, turned = refs[: count * chunks], refs[-4:-1], refs[-1]
    rank = rank_ref[0]
    high = pieces[0].shape[1]
    share = high * chunks
    for which, out in enumerate(outs):
        for distance in range(count):
            for chunk in range(chunks):
                first = pl.multiple_of((rank ^ distance) * share + chunk * high, 16)
                turned[which, pl.ds(first, high), :] = pieces[chunk * count + distance][which]
        out[0] = turned[which].T


def unpack(rank, pieces, count, chunks):
    _, high, frames = pieces[0][0].shape
    width = high * count * chunks
    whole = jax.ShapeDtypeStruct((1, frames, width), bf16)
    return pl.pallas_call(
        functools.partial(unpack_kernel, count, chunks),
        out_shape=(whole,) * 3,
        in_specs=[SMEM] + [VMEM] * (count * chunks),
        out_specs=(VMEM,) * 3,
        scratch_shapes=[pltpu.VMEM((3, width, frames), bf16)],
        compiler_params=pltpu.CompilerParams(vmem_limit_bytes=LIMIT),
        cost_estimate=pl.CostEstimate(
            flops=0, bytes_accessed=12 * frames * width, transcendentals=0
        ),
    )(rank, *[piece for part in pieces for piece in part])


def core_kernel(count, block, scalars, weight_ref, bias_ref, *refs):
    pieces, outs, taps_ref = refs[:count], refs[count : 2 * count], refs[2 * count]
    q_t, k_t, v_t, a_t, q_n, k_n, v_n, g_n, a_n, probs, shifted, pre_grad = refs[2 * count + 1 :]
    heads, rows, depth = q_n.shape
    frames = pieces[0].shape[2]
    blocks = rows // block
    scale = 1.0 / math.sqrt(depth)
    log_scale = scale * math.log2(math.e)
    length, rank = scalars[0], scalars[1]

    def span(head):
        return slice(head * depth, (head + 1) * depth)

    for distance, piece in enumerate(pieces):
        at = pl.ds(pl.multiple_of((rank ^ distance) * frames, 128), frames)
        q_t[:, at] = piece[0]
        k_t[:, at] = piece[1]
        v_t[:, at] = piece[2]
        for head in range(heads):
            q_n[head, at, :] = piece[0, span(head), :].T
            k_n[head, at, :] = piece[1, span(head), :].T
            v_n[head, at, :] = piece[2, span(head), :].T
            g_n[head, at, :] = piece[3, span(head), :].T

    def forward(index, head):
        cols = pl.ds(pl.multiple_of(index * block, block), block)
        scores = jnp.dot(k_n[head], q_t[span(head), cols], preferred_element_type=f32)
        key_at = lax.broadcasted_iota(jnp.int32, scores.shape, 0)
        scores = jnp.where(key_at < length, scores, masked_score)
        exped = jnp.exp2((scores - jnp.max(scores, axis=0, keepdims=True)) * log_scale)
        found = exped * (1.0 / jnp.sum(exped, axis=0, keepdims=True))
        probs[head, :, cols] = found
        out = jnp.dot(v_t[span(head), :], found.astype(bf16), preferred_element_type=f32)
        frame_at = index * block + lax.broadcasted_iota(jnp.int32, out.shape, 1)
        a_t[span(head), cols] = jnp.where(frame_at < length, out, 0.0).astype(bf16)

    def each_block(body):
        if blocks == 1:
            for head in range(heads):
                body(0, head)
        else:

            def step(index, carry):
                for head in range(heads):
                    body(index, head)
                return carry

            lax.fori_loop(0, blocks, step, 0)

    each_block(forward)

    tall = shifted.shape[1]

    def shift_all(source_rows):
        shifted[0, 0:PAD, :] = jnp.zeros((PAD, depth), f32)
        shifted[0, PAD + rows : tall, :] = jnp.zeros((tall - PAD - rows, depth), f32)
        for first in range(0, rows, frames):
            shifted[0, PAD + first : PAD + first + frames, :] = source_rows(first)
        for s in range(1, 8):
            shifted[s, 0 : tall - 8, :] = shifted[0, s : tall - 8 + s, :]

    step_rows = 64

    def filtered(head, row, reverse):
        total = None
        for offset in range(1, KERNEL + 1):
            s, a = offset % 8, offset // 8 * 8
            tap = KERNEL - offset if reverse else offset - 1
            term = weight_ref[head, tap : tap + 1, :] * shifted[s, pl.ds(row + a, step_rows), :]
            total = term if total is None else total + term
        return total

    def eights(array):
        return jnp.sum(array.reshape(step_rows // 8, 8, depth), axis=0)

    for head in range(heads):
        shift_all(lambda first: a_t[span(head), first : first + frames].T.astype(f32))

        def conv_step(index, carry, head=head):
            row = pl.multiple_of(index * step_rows, step_rows)
            conv_pre = filtered(head, row, False) + bias_ref[head]
            sig = 1.0 / (1.0 + jnp.exp(-conv_pre))
            grad = g_n[head, pl.ds(row, step_rows), :].astype(f32)
            pre = grad * (sig * (1.0 + conv_pre * (1.0 - sig)))
            pre = pre.astype(bf16).astype(f32)
            pre_grad[pl.ds(row, step_rows), :] = pre
            new = []
            for offset in range(1, KERNEL + 1):
                s, a = offset % 8, offset // 8 * 8
                term = pre * shifted[s, pl.ds(row + a, step_rows), :]
                new.append(carry[offset - 1] + eights(term))
            new.append(carry[KERNEL] + eights(pre))
            return tuple(new)

        zero = jnp.zeros((8, depth), f32)
        sums = lax.fori_loop(0, rows // step_rows, conv_step, (zero,) * (KERNEL + 1))
        for tap in range(KERNEL + 1):
            taps_ref[head, tap : tap + 1, :] = jnp.sum(sums[tap], axis=0, keepdims=True)

        shift_all(lambda first: pre_grad[first : first + frames, :])

        def back_step(index, carry, head=head):
            row = pl.multiple_of(index * step_rows, step_rows)
            total = g_n[head, pl.ds(row, step_rows), :].astype(f32) + filtered(head, row, True)
            frame_at = row + lax.broadcasted_iota(jnp.int32, total.shape, 0)
            total = jnp.where(frame_at < length, total, 0.0)
            a_n[head, pl.ds(row, step_rows), :] = total.astype(bf16)
            return carry

        lax.fori_loop(0, rows // step_rows, back_step, 0)
        for first in range(0, rows, frames):
            a_t[span(head), first : first + frames] = a_n[head, first : first + frames, :].T

    def backward(index, head):
        cols = pl.ds(pl.multiple_of(index * block, block), block)
        score_grad = jnp.dot(v_n[head], a_t[span(head), cols], preferred_element_type=f32)
        found = probs[head, :, cols]
        delta = jnp.sum(found * score_grad, axis=0, keepdims=True)
        diff = (found * (score_grad - delta)).astype(bf16)
        value = jnp.dot(found.astype(bf16), a_n[head, cols, :], preferred_element_type=f32)
        key = jnp.dot(diff, q_n[head, cols, :], preferred_element_type=f32)
        query = jnp.dot(k_t[span(head), :], diff, preferred_element_type=f32)
        q_t[span(head), cols] = (query * scale).astype(bf16)
        return key, value

    def finish(head, key, value):
        for first in range(0, rows, frames):
            at = slice(first, first + frames)
            k_t[span(head), at] = (key[at, :] * scale).astype(bf16).T
            v_t[span(head), at] = value[at, :].astype(bf16).T

    for head in range(heads):
        if blocks == 1:
            finish(head, *backward(0, head))
        else:
            zeros = jnp.zeros((rows, depth), f32)

            def step(index, carry, head=head):
                key, value = backward(index, head)
                return carry[0] + key, carry[1] + value

            finish(head, *lax.fori_loop(0, blocks, step, (zeros, zeros)))

    for distance, out in enumerate(outs):
        at = pl.ds(pl.multiple_of((rank ^ distance) * frames, 128), frames)
        out[0] = q_t[:, at]
        out[1] = k_t[:, at]
        out[2] = v_t[:, at]


def core(scalars, weight, bias, pieces):
    count = len(pieces)
    _, high, frames = pieces[0].shape
    heads, _, depth = weight.shape
    rows = count * frames
    block = math.gcd(rows, 512)
    tall = rows + 2 * PAD + 8
    piece = jax.ShapeDtypeStruct((3, high, frames), bf16)
    turned = pltpu.VMEM((high, rows), bf16)
    plain = pltpu.VMEM((heads, rows, depth), bf16)
    outs = pl.pallas_call(
        functools.partial(core_kernel, count, block),
        out_shape=(piece,) * count + (jax.ShapeDtypeStruct((heads, KERNEL + 1, depth), f32),),
        in_specs=[SMEM] + [VMEM] * (2 + count),
        out_specs=(VMEM,) * (count + 1),
        scratch_shapes=[turned] * 4
        + [plain] * 5
        + [
            pltpu.VMEM((heads, rows, rows), f32),
            pltpu.VMEM((8, tall, depth), f32),
            pltpu.VMEM((rows, depth), f32),
        ],
        compiler_params=pltpu.CompilerParams(vmem_limit_bytes=LIMIT),
        cost_estimate=pl.CostEstimate(
            flops=24 * rows * rows * high,
            bytes_accessed=14 * rows * high,
            transcendentals=heads * rows * rows,
        ),
    )(scalars, weight, bias, *pieces)
    return outs[:count], outs[count]


def swapped(pieces):
    count = len(pieces)
    moved = [pieces[0]]
    for distance in range(1, count):
        pairs = [(i, i ^ distance) for i in range(count)]
        moved.append(lax.ppermute(pieces[distance], "seq", pairs))
    return moved


def summed(array, axis):
    count = lax.axis_size(axis)
    distance = 1
    while distance < count:
        pairs = [(i, i ^ distance) for i in range(count)]
        array = array + lax.ppermute(array, axis, pairs)
        distance *= 2
    return array


def on_device(queries, keys, values, grad_out, conv_weight, conv_bias, lengths):
    count = lax.axis_size("seq")
    rank = lax.axis_index("seq").astype(jnp.int32)
    width = queries.shape[2]
    depth = width // HEADS
    heads = HEADS // count
    chunks = math.gcd(heads, 2)
    step = heads // chunks
    by_head = conv_weight.reshape(KERNEL, HEADS, depth).transpose(1, 0, 2)
    weight = lax.dynamic_slice_in_dim(by_head, rank * heads, heads, axis=0)
    bias = lax.dynamic_slice_in_dim(conv_bias.reshape(HEADS, 1, depth), rank * heads, heads, axis=0)
    scalars = jnp.stack([lengths[0], rank])
    sent = pack(rank[None], (queries, keys, values, grad_out), count, chunks)
    arrived = [swapped(pieces) for pieces in sent]
    returned, taps = [], []
    for chunk, pieces in enumerate(arrived):
        at = slice(chunk * step, (chunk + 1) * step)
        grads, part = core(scalars, weight[at], bias[at], pieces)
        returned.append(swapped(grads))
        taps.append(part)
    taps = summed(jnp.concatenate(taps, axis=0), "dp")
    taps = taps.transpose(1, 0, 2).reshape(KERNEL + 1, heads * depth)
    query_grad, key_grad, value_grad = unpack(rank[None], returned, count, chunks)
    return query_grad, key_grad, value_grad, taps[:KERNEL], taps[KERNEL]


def solution(mesh):
    return jax.shard_map(
        on_device,
        mesh=mesh,
        in_specs=(
            P("dp", "seq", None),
            P("dp", "seq", None),
            P("dp", "seq", None),
            P("dp", "seq", None),
            P(),
            P(),
            P("dp"),
        ),
        out_specs=(
            P("dp", "seq", None),
            P("dp", "seq", None),
            P("dp", "seq", None),
            P(None, "seq"),
            P("seq"),
        ),
        check_vma=False,
    )
```

```python
import functools
import math

import jax
import jax.numpy as jnp
from jax import lax
from jax.experimental import pallas as pl
from jax.experimental.pallas import tpu as pltpu
from jax.sharding import PartitionSpec as P

HEADS = 16
KERNEL = 31
PAD = 16
masked_score = -1e30
VMEM = pl.BlockSpec(memory_space=pltpu.VMEM)
SMEM = pl.BlockSpec(memory_space=pltpu.SMEM)
LIMIT = 16 * 1024 * 1024
bf16, f32 = jnp.bfloat16, jnp.float32


def pack_kernel(count, chunks, rank_ref, *refs):
    arrays, outs, turned = refs[:4], refs[4:-1], refs[-1]
    rank = rank_ref[0]
    high = outs[0].shape[1]
    share = high * chunks
    for which, array in enumerate(arrays):
        turned[which] = array[0].T
        for distance in range(count):
            for chunk in range(chunks):
                first = pl.multiple_of((rank ^ distance) * share + chunk * high, 16)
                outs[chunk * count + distance][which] = turned[which, pl.ds(first, high), :]


def pack(rank, arrays, count, chunks):
    _, frames, width = arrays[0].shape
    high = width // count // chunks
    piece = jax.ShapeDtypeStruct((4, high, frames), bf16)
    outs = pl.pallas_call(
        functools.partial(pack_kernel, count, chunks),
        out_shape=(piece,) * (count * chunks),
        in_specs=[SMEM] + [VMEM] * 4,
        out_specs=(VMEM,) * (count * chunks),
        scratch_shapes=[pltpu.VMEM((4, width, frames), bf16)],
        compiler_params=pltpu.CompilerParams(vmem_limit_bytes=LIMIT),
        cost_estimate=pl.CostEstimate(
            flops=0, bytes_accessed=16 * frames * width, transcendentals=0
        ),
    )(rank, *arrays)
    return [outs[chunk * count : (chunk + 1) * count] for chunk in range(chunks)]


def unpack_kernel(count, chunks, rank_ref, *refs):
    pieces, outs, turned = refs[: count * chunks], refs[-4:-1], refs[-1]
    rank = rank_ref[0]
    high = pieces[0].shape[1]
    share = high * chunks
    for which, out in enumerate(outs):
        for distance in range(count):
            for chunk in range(chunks):
                first = pl.multiple_of((rank ^ distance) * share + chunk * high, 16)
                turned[which, pl.ds(first, high), :] = pieces[chunk * count + distance][which]
        out[0] = turned[which].T


def unpack(rank, pieces, count, chunks):
    _, high, frames = pieces[0][0].shape
    width = high * count * chunks
    whole = jax.ShapeDtypeStruct((1, frames, width), bf16)
    return pl.pallas_call(
        functools.partial(unpack_kernel, count, chunks),
        out_shape=(whole,) * 3,
        in_specs=[SMEM] + [VMEM] * (count * chunks),
        out_specs=(VMEM,) * 3,
        scratch_shapes=[pltpu.VMEM((3, width, frames), bf16)],
        compiler_params=pltpu.CompilerParams(vmem_limit_bytes=LIMIT),
        cost_estimate=pl.CostEstimate(
            flops=0, bytes_accessed=12 * frames * width, transcendentals=0
        ),
    )(rank, *[piece for part in pieces for piece in part])


def core_kernel(count, block, scalars, weight_ref, bias_ref, *refs):
    pieces, outs, taps_ref = refs[:count], refs[count : 2 * count], refs[2 * count]
    q_t, k_t, v_t, a_t, q_n, k_n, v_n, g_n, a_n, probs, shifted, pre_grad = refs[2 * count + 1 :]
    heads, rows, depth = q_n.shape
    frames = pieces[0].shape[2]
    blocks = rows // block
    scale = 1.0 / math.sqrt(depth)
    log_scale = scale * math.log2(math.e)
    length, rank = scalars[0], scalars[1]

    def span(head):
        return slice(head * depth, (head + 1) * depth)

    for distance, piece in enumerate(pieces):
        at = pl.ds(pl.multiple_of((rank ^ distance) * frames, 128), frames)
        q_t[:, at] = piece[0]
        k_t[:, at] = piece[1]
        v_t[:, at] = piece[2]
        for head in range(heads):
            q_n[head, at, :] = piece[0, span(head), :].T
            k_n[head, at, :] = piece[1, span(head), :].T
            v_n[head, at, :] = piece[2, span(head), :].T
            g_n[head, at, :] = piece[3, span(head), :].T

    def forward(index, head):
        cols = pl.ds(pl.multiple_of(index * block, block), block)
        scores = jnp.dot(k_n[head], q_t[span(head), cols], preferred_element_type=f32)
        key_at = lax.broadcasted_iota(jnp.int32, scores.shape, 0)
        scores = jnp.where(key_at < length, scores, masked_score)
        exped = jnp.exp2((scores - jnp.max(scores, axis=0, keepdims=True)) * log_scale)
        found = exped * (1.0 / jnp.sum(exped, axis=0, keepdims=True))
        probs[head, :, cols] = found
        out = jnp.dot(v_t[span(head), :], found.astype(bf16), preferred_element_type=f32)
        frame_at = index * block + lax.broadcasted_iota(jnp.int32, out.shape, 1)
        a_t[span(head), cols] = jnp.where(frame_at < length, out, 0.0).astype(bf16)

    def each_block(body):
        if blocks == 1:
            for head in range(heads):
                body(0, head)
        else:

            def step(index, carry):
                for head in range(heads):
                    body(index, head)
                return carry

            lax.fori_loop(0, blocks, step, 0)

    each_block(forward)

    tall = shifted.shape[1]

    def shift_all(source_rows):
        shifted[0, 0:PAD, :] = jnp.zeros((PAD, depth), f32)
        shifted[0, PAD + rows : tall, :] = jnp.zeros((tall - PAD - rows, depth), f32)
        for first in range(0, rows, frames):
            shifted[0, PAD + first : PAD + first + frames, :] = source_rows(first)
        for s in range(1, 8):
            shifted[s, 0 : tall - 8, :] = shifted[0, s : tall - 8 + s, :]

    step_rows = 64

    def filtered(head, row, reverse):
        total = None
        for offset in range(1, KERNEL + 1):
            s, a = offset % 8, offset // 8 * 8
            tap = KERNEL - offset if reverse else offset - 1
            term = weight_ref[head, tap : tap + 1, :] * shifted[s, pl.ds(row + a, step_rows), :]
            total = term if total is None else total + term
        return total

    def eights(array):
        return jnp.sum(array.reshape(step_rows // 8, 8, depth), axis=0)

    for head in range(heads):
        shift_all(lambda first: a_t[span(head), first : first + frames].T.astype(f32))

        def conv_step(index, carry, head=head):
            row = pl.multiple_of(index * step_rows, step_rows)
            conv_pre = filtered(head, row, False) + bias_ref[head]
            sig = 1.0 / (1.0 + jnp.exp(-conv_pre))
            grad = g_n[head, pl.ds(row, step_rows), :].astype(f32)
            pre = grad * (sig * (1.0 + conv_pre * (1.0 - sig)))
            pre = pre.astype(bf16).astype(f32)
            pre_grad[pl.ds(row, step_rows), :] = pre
            new = []
            for offset in range(1, KERNEL + 1):
                s, a = offset % 8, offset // 8 * 8
                term = pre * shifted[s, pl.ds(row + a, step_rows), :]
                new.append(carry[offset - 1] + eights(term))
            new.append(carry[KERNEL] + eights(pre))
            return tuple(new)

        zero = jnp.zeros((8, depth), f32)
        sums = lax.fori_loop(0, rows // step_rows, conv_step, (zero,) * (KERNEL + 1))
        for tap in range(KERNEL + 1):
            taps_ref[head, tap : tap + 1, :] = jnp.sum(sums[tap], axis=0, keepdims=True)

        shift_all(lambda first: pre_grad[first : first + frames, :])

        def back_step(index, carry, head=head):
            row = pl.multiple_of(index * step_rows, step_rows)
            total = g_n[head, pl.ds(row, step_rows), :].astype(f32) + filtered(head, row, True)
            frame_at = row + lax.broadcasted_iota(jnp.int32, total.shape, 0)
            total = jnp.where(frame_at < length, total, 0.0)
            a_n[head, pl.ds(row, step_rows), :] = total.astype(bf16)
            return carry

        lax.fori_loop(0, rows // step_rows, back_step, 0)
        for first in range(0, rows, frames):
            a_t[span(head), first : first + frames] = a_n[head, first : first + frames, :].T

    def backward(index, head):
        cols = pl.ds(pl.multiple_of(index * block, block), block)
        score_grad = jnp.dot(v_n[head], a_t[span(head), cols], preferred_element_type=f32)
        found = probs[head, :, cols]
        delta = jnp.sum(found * score_grad, axis=0, keepdims=True)
        diff = (found * (score_grad - delta)).astype(bf16)
        value = jnp.dot(found.astype(bf16), a_n[head, cols, :], preferred_element_type=f32)
        key = jnp.dot(diff, q_n[head, cols, :], preferred_element_type=f32)
        query = jnp.dot(k_t[span(head), :], diff, preferred_element_type=f32)
        q_t[span(head), cols] = (query * scale).astype(bf16)
        return key, value

    def finish(head, key, value):
        for first in range(0, rows, frames):
            at = slice(first, first + frames)
            k_t[span(head), at] = (key[at, :] * scale).astype(bf16).T
            v_t[span(head), at] = value[at, :].astype(bf16).T

    for head in range(heads):
        if blocks == 1:
            finish(head, *backward(0, head))
        else:
            zeros = jnp.zeros((rows, depth), f32)

            def step(index, carry, head=head):
                key, value = backward(index, head)
                return carry[0] + key, carry[1] + value

            finish(head, *lax.fori_loop(0, blocks, step, (zeros, zeros)))

    for distance, out in enumerate(outs):
        at = pl.ds(pl.multiple_of((rank ^ distance) * frames, 128), frames)
        out[0] = q_t[:, at]
        out[1] = k_t[:, at]
        out[2] = v_t[:, at]


def core(scalars, weight, bias, pieces):
    count = len(pieces)
    _, high, frames = pieces[0].shape
    heads, _, depth = weight.shape
    rows = count * frames
    block = math.gcd(rows, 512)
    tall = rows + 2 * PAD + 8
    piece = jax.ShapeDtypeStruct((3, high, frames), bf16)
    turned = pltpu.VMEM((high, rows), bf16)
    plain = pltpu.VMEM((heads, rows, depth), bf16)
    outs = pl.pallas_call(
        functools.partial(core_kernel, count, block),
        out_shape=(piece,) * count + (jax.ShapeDtypeStruct((heads, KERNEL + 1, depth), f32),),
        in_specs=[SMEM] + [VMEM] * (2 + count),
        out_specs=(VMEM,) * (count + 1),
        scratch_shapes=[turned] * 4
        + [plain] * 5
        + [
            pltpu.VMEM((heads, rows, rows), f32),
            pltpu.VMEM((8, tall, depth), f32),
            pltpu.VMEM((rows, depth), f32),
        ],
        compiler_params=pltpu.CompilerParams(
            vmem_limit_bytes=12 * 2**20 + 8 * heads * rows * rows + 4096 * tall
        ),
        cost_estimate=pl.CostEstimate(
            flops=24 * rows * rows * high,
            bytes_accessed=14 * rows * high,
            transcendentals=heads * rows * rows,
        ),
    )(scalars, weight, bias, *pieces)
    return outs[:count], outs[count]


def swapped(pieces, before):
    count = len(pieces)
    pieces = list(pieces)
    if before is not None and count > 2:
        pieces[1:-1], before = lax.optimization_barrier((pieces[1:-1], before))
    moved = [pieces[0]]
    for distance in range(1, count):
        pairs = [(i, i ^ distance) for i in range(count)]
        moved.append(lax.ppermute(pieces[distance], "seq", pairs))
    return moved, before


def exchanged(parts):
    done = []
    for pieces in parts:
        moved, before = swapped(pieces, done[-1][1:] if done else None)
        if before is not None:
            done[-1] = done[-1][:1] + list(before)
        done.append(moved)
    return done


def summed(array, axis):
    count = lax.axis_size(axis)
    distance = 1
    while distance < count:
        pairs = [(i, i ^ distance) for i in range(count)]
        array = array + lax.ppermute(array, axis, pairs)
        distance *= 2
    return array


def on_device(queries, keys, values, grad_out, conv_weight, conv_bias, lengths):
    count = lax.axis_size("seq")
    rank = lax.axis_index("seq").astype(jnp.int32)
    width = queries.shape[2]
    depth = width // HEADS
    heads = HEADS // count
    chunks = math.gcd(heads, 2)
    step = heads // chunks
    by_head = conv_weight.reshape(KERNEL, HEADS, depth).transpose(1, 0, 2)
    weight = lax.dynamic_slice_in_dim(by_head, rank * heads, heads, axis=0)
    bias = lax.dynamic_slice_in_dim(conv_bias.reshape(HEADS, 1, depth), rank * heads, heads, axis=0)
    scalars = jnp.stack([lengths[0], rank])
    sent = pack(rank[None], (queries, keys, values, grad_out), count, chunks)
    arrived = exchanged(sent)
    kept, taps = [], []
    for chunk, pieces in enumerate(arrived):
        at = slice(chunk * step, (chunk + 1) * step)
        grads, part = core(scalars, weight[at], bias[at], pieces)
        kept.append(grads)
        taps.append(part)
    returned = exchanged(kept)
    taps = summed(jnp.concatenate(taps, axis=0), "dp")
    taps = taps.transpose(1, 0, 2).reshape(KERNEL + 1, heads * depth)
    query_grad, key_grad, value_grad = unpack(rank[None], returned, count, chunks)
    return query_grad, key_grad, value_grad, taps[:KERNEL], taps[KERNEL]


def solution(mesh):
    return jax.shard_map(
        on_device,
        mesh=mesh,
        in_specs=(
            P("dp", "seq", None),
            P("dp", "seq", None),
            P("dp", "seq", None),
            P("dp", "seq", None),
            P(),
            P(),
            P("dp"),
        ),
        out_specs=(
            P("dp", "seq", None),
            P("dp", "seq", None),
            P("dp", "seq", None),
            P(None, "seq"),
            P("seq"),
        ),
        check_vma=False,
    )
```

```python
import functools
import math

import jax
import jax.numpy as jnp
from jax import lax
from jax.experimental import pallas as pl
from jax.experimental.pallas import tpu as pltpu
from jax.sharding import PartitionSpec as P

HEADS = 16
KERNEL = 31
PAD = 16
CUTS = 4
masked_score = -1e30
VMEM = pl.BlockSpec(memory_space=pltpu.VMEM)
SMEM = pl.BlockSpec(memory_space=pltpu.SMEM)
LIMIT = 16 * 1024 * 1024
bf16, f32 = jnp.bfloat16, jnp.float32


def pack_kernel(count, chunks, rank_ref, *refs):
    arrays, outs, (plain, turned, sems) = refs[:4], refs[4:-3], refs[-3:]
    rank = rank_ref[0]
    high = outs[0].shape[1]
    share = high * chunks
    frames = plain.shape[1]
    cut = frames // CUTS

    def copy(which, part):
        at = pl.ds(part * cut, cut)
        return pltpu.make_async_copy(
            arrays[which].at[0, at, :], plain.at[which, at, :], sems.at[which, part]
        )

    for which in range(4):
        for part in range(CUTS):
            copy(which, part).start()
    for which in range(4):
        for part in range(CUTS):
            copy(which, part).wait()
        turned[which] = plain[which].T
        for distance in range(count):
            for chunk in range(chunks):
                first = pl.multiple_of((rank ^ distance) * share + chunk * high, 16)
                outs[chunk * count + distance][which] = turned[which, pl.ds(first, high), :]


def pack(rank, arrays, count, chunks):
    _, frames, width = arrays[0].shape
    high = width // count // chunks
    piece = jax.ShapeDtypeStruct((4, high, frames), bf16)
    outs = pl.pallas_call(
        functools.partial(pack_kernel, count, chunks),
        out_shape=(piece,) * (count * chunks),
        in_specs=[SMEM] + [pl.BlockSpec(memory_space=pltpu.HBM)] * 4,
        out_specs=(VMEM,) * (count * chunks),
        scratch_shapes=[
            pltpu.VMEM((4, frames, width), bf16),
            pltpu.VMEM((4, width, frames), bf16),
            pltpu.SemaphoreType.DMA((4, CUTS)),
        ],
        compiler_params=pltpu.CompilerParams(vmem_limit_bytes=LIMIT),
        cost_estimate=pl.CostEstimate(
            flops=0, bytes_accessed=16 * frames * width, transcendentals=0
        ),
    )(rank, *[pltpu.with_memory_space_constraint(array, pltpu.HBM) for array in arrays])
    return [outs[chunk * count : (chunk + 1) * count] for chunk in range(chunks)]


def unpack_kernel(count, chunks, rank_ref, *refs):
    pieces, outs, turned = refs[: count * chunks], refs[-4:-1], refs[-1]
    rank = rank_ref[0]
    high = pieces[0].shape[1]
    share = high * chunks
    for which, out in enumerate(outs):
        for distance in range(count):
            for chunk in range(chunks):
                first = pl.multiple_of((rank ^ distance) * share + chunk * high, 16)
                turned[which, pl.ds(first, high), :] = pieces[chunk * count + distance][which]
        out[0] = turned[which].T


def unpack(rank, pieces, count, chunks):
    _, high, frames = pieces[0][0].shape
    width = high * count * chunks
    whole = jax.ShapeDtypeStruct((1, frames, width), bf16)
    return pl.pallas_call(
        functools.partial(unpack_kernel, count, chunks),
        out_shape=(whole,) * 3,
        in_specs=[SMEM] + [VMEM] * (count * chunks),
        out_specs=(VMEM,) * 3,
        scratch_shapes=[pltpu.VMEM((3, width, frames), bf16)],
        compiler_params=pltpu.CompilerParams(vmem_limit_bytes=LIMIT),
        cost_estimate=pl.CostEstimate(
            flops=0, bytes_accessed=12 * frames * width, transcendentals=0
        ),
    )(rank, *[piece for part in pieces for piece in part])


def core_kernel(count, block, scalars, weight_ref, bias_ref, *refs):
    pieces, outs, taps_ref = refs[:count], refs[count : 2 * count], refs[2 * count]
    q_t, k_t, v_t, a_t, q_n, k_n, v_n, g_n, a_n, probs, shifted, pre_grad = refs[2 * count + 1 :]
    heads, rows, depth = q_n.shape
    frames = pieces[0].shape[2]
    blocks = rows // block
    scale = 1.0 / math.sqrt(depth)
    log_scale = scale * math.log2(math.e)
    length, rank = scalars[0], scalars[1]

    def span(head):
        return slice(head * depth, (head + 1) * depth)

    for distance, piece in enumerate(pieces):
        at = pl.ds(pl.multiple_of((rank ^ distance) * frames, 128), frames)
        q_t[:, at] = piece[0]
        k_t[:, at] = piece[1]
        v_t[:, at] = piece[2]
        for head in range(heads):
            q_n[head, at, :] = piece[0, span(head), :].T
            k_n[head, at, :] = piece[1, span(head), :].T
            v_n[head, at, :] = piece[2, span(head), :].T
            g_n[head, at, :] = piece[3, span(head), :].T

    def forward(index, head):
        cols = pl.ds(pl.multiple_of(index * block, block), block)
        scores = jnp.dot(k_n[head], q_t[span(head), cols], preferred_element_type=f32)
        key_at = lax.broadcasted_iota(jnp.int32, scores.shape, 0)
        scores = jnp.where(key_at < length, scores, masked_score)
        exped = jnp.exp2((scores - jnp.max(scores, axis=0, keepdims=True)) * log_scale)
        found = exped * (1.0 / jnp.sum(exped, axis=0, keepdims=True))
        probs[head, :, cols] = found
        out = jnp.dot(v_t[span(head), :], found.astype(bf16), preferred_element_type=f32)
        frame_at = index * block + lax.broadcasted_iota(jnp.int32, out.shape, 1)
        a_t[span(head), cols] = jnp.where(frame_at < length, out, 0.0).astype(bf16)

    def each_block(body):
        if blocks == 1:
            for head in range(heads):
                body(0, head)
        else:

            def step(index, carry):
                for head in range(heads):
                    body(index, head)
                return carry

            lax.fori_loop(0, blocks, step, 0)

    each_block(forward)

    tall = shifted.shape[1]

    def shift_all(source_rows):
        shifted[0, 0:PAD, :] = jnp.zeros((PAD, depth), f32)
        shifted[0, PAD + rows : tall, :] = jnp.zeros((tall - PAD - rows, depth), f32)
        for first in range(0, rows, frames):
            shifted[0, PAD + first : PAD + first + frames, :] = source_rows(first)
        for s in range(1, 8):
            shifted[s, 0 : tall - 8, :] = shifted[0, s : tall - 8 + s, :]

    step_rows = 64

    def filtered(head, row, reverse):
        total = None
        for offset in range(1, KERNEL + 1):
            s, a = offset % 8, offset // 8 * 8
            tap = KERNEL - offset if reverse else offset - 1
            term = weight_ref[head, tap : tap + 1, :] * shifted[s, pl.ds(row + a, step_rows), :]
            total = term if total is None else total + term
        return total

    def eights(array):
        return jnp.sum(array.reshape(step_rows // 8, 8, depth), axis=0)

    for head in range(heads):
        shift_all(lambda first: a_t[span(head), first : first + frames].T.astype(f32))

        def conv_step(index, carry, head=head):
            row = pl.multiple_of(index * step_rows, step_rows)
            conv_pre = filtered(head, row, False) + bias_ref[head]
            sig = 1.0 / (1.0 + jnp.exp(-conv_pre))
            grad = g_n[head, pl.ds(row, step_rows), :].astype(f32)
            pre = grad * (sig * (1.0 + conv_pre * (1.0 - sig)))
            pre = pre.astype(bf16).astype(f32)
            pre_grad[pl.ds(row, step_rows), :] = pre
            new = []
            for offset in range(1, KERNEL + 1):
                s, a = offset % 8, offset // 8 * 8
                term = pre * shifted[s, pl.ds(row + a, step_rows), :]
                new.append(carry[offset - 1] + eights(term))
            new.append(carry[KERNEL] + eights(pre))
            return tuple(new)

        zero = jnp.zeros((8, depth), f32)
        sums = lax.fori_loop(0, rows // step_rows, conv_step, (zero,) * (KERNEL + 1))
        for tap in range(KERNEL + 1):
            taps_ref[head, tap : tap + 1, :] = jnp.sum(sums[tap], axis=0, keepdims=True)

        shift_all(lambda first: pre_grad[first : first + frames, :])

        def back_step(index, carry, head=head):
            row = pl.multiple_of(index * step_rows, step_rows)
            total = g_n[head, pl.ds(row, step_rows), :].astype(f32) + filtered(head, row, True)
            frame_at = row + lax.broadcasted_iota(jnp.int32, total.shape, 0)
            total = jnp.where(frame_at < length, total, 0.0)
            a_n[head, pl.ds(row, step_rows), :] = total.astype(bf16)
            return carry

        lax.fori_loop(0, rows // step_rows, back_step, 0)
        for first in range(0, rows, frames):
            a_t[span(head), first : first + frames] = a_n[head, first : first + frames, :].T

    def backward(index, head):
        cols = pl.ds(pl.multiple_of(index * block, block), block)
        score_grad = jnp.dot(v_n[head], a_t[span(head), cols], preferred_element_type=f32)
        found = probs[head, :, cols]
        delta = jnp.sum(found * score_grad, axis=0, keepdims=True)
        diff = (found * (score_grad - delta)).astype(bf16)
        value = jnp.dot(found.astype(bf16), a_n[head, cols, :], preferred_element_type=f32)
        key = jnp.dot(diff, q_n[head, cols, :], preferred_element_type=f32)
        query = jnp.dot(k_t[span(head), :], diff, preferred_element_type=f32)
        q_t[span(head), cols] = (query * scale).astype(bf16)
        return key, value

    def finish(head, key, value):
        for first in range(0, rows, frames):
            at = slice(first, first + frames)
            k_t[span(head), at] = (key[at, :] * scale).astype(bf16).T
            v_t[span(head), at] = value[at, :].astype(bf16).T

    for head in range(heads):
        if blocks == 1:
            finish(head, *backward(0, head))
        else:
            zeros = jnp.zeros((rows, depth), f32)

            def step(index, carry, head=head):
                key, value = backward(index, head)
                return carry[0] + key, carry[1] + value

            finish(head, *lax.fori_loop(0, blocks, step, (zeros, zeros)))

    for distance, out in enumerate(outs):
        at = pl.ds(pl.multiple_of((rank ^ distance) * frames, 128), frames)
        out[0] = q_t[:, at]
        out[1] = k_t[:, at]
        out[2] = v_t[:, at]


def core(scalars, weight, bias, pieces):
    count = len(pieces)
    _, high, frames = pieces[0].shape
    heads, _, depth = weight.shape
    rows = count * frames
    block = math.gcd(rows, 512)
    tall = rows + 2 * PAD + 8
    piece = jax.ShapeDtypeStruct((3, high, frames), bf16)
    turned = pltpu.VMEM((high, rows), bf16)
    plain = pltpu.VMEM((heads, rows, depth), bf16)
    outs = pl.pallas_call(
        functools.partial(core_kernel, count, block),
        out_shape=(piece,) * count + (jax.ShapeDtypeStruct((heads, KERNEL + 1, depth), f32),),
        in_specs=[SMEM] + [VMEM] * (2 + count),
        out_specs=(VMEM,) * (count + 1),
        scratch_shapes=[turned] * 4
        + [plain] * 5
        + [
            pltpu.VMEM((heads, rows, rows), f32),
            pltpu.VMEM((8, tall, depth), f32),
            pltpu.VMEM((rows, depth), f32),
        ],
        compiler_params=pltpu.CompilerParams(
            vmem_limit_bytes=12 * 2**20 + 8 * heads * rows * rows + 4096 * tall
        ),
        cost_estimate=pl.CostEstimate(
            flops=24 * rows * rows * high,
            bytes_accessed=14 * rows * high,
            transcendentals=heads * rows * rows,
        ),
    )(scalars, weight, bias, *pieces)
    return outs[:count], outs[count]


def swapped(pieces, before):
    count = len(pieces)
    pieces = list(pieces)
    if before is not None and count > 2:
        pieces[1:-1], before = lax.optimization_barrier((pieces[1:-1], before))
    moved = [pieces[0]]
    for distance in range(1, count):
        pairs = [(i, i ^ distance) for i in range(count)]
        moved.append(lax.ppermute(pieces[distance], "seq", pairs))
    return moved, before


def exchanged(parts):
    done = []
    for pieces in parts:
        moved, before = swapped(pieces, done[-1][1:] if done else None)
        if before is not None:
            done[-1] = done[-1][:1] + list(before)
        done.append(moved)
    return done


def summed(array, axis):
    count = lax.axis_size(axis)
    distance = 1
    while distance < count:
        pairs = [(i, i ^ distance) for i in range(count)]
        array = array + lax.ppermute(array, axis, pairs)
        distance *= 2
    return array


def on_device(queries, keys, values, grad_out, conv_weight, conv_bias, lengths):
    count = lax.axis_size("seq")
    rank = lax.axis_index("seq").astype(jnp.int32)
    width = queries.shape[2]
    depth = width // HEADS
    heads = HEADS // count
    chunks = math.gcd(heads, 2)
    step = heads // chunks
    by_head = conv_weight.reshape(KERNEL, HEADS, depth).transpose(1, 0, 2)
    weight = lax.dynamic_slice_in_dim(by_head, rank * heads, heads, axis=0)
    bias = lax.dynamic_slice_in_dim(conv_bias.reshape(HEADS, 1, depth), rank * heads, heads, axis=0)
    scalars = jnp.stack([lengths[0], rank])
    sent = pack(rank[None], (queries, keys, values, grad_out), count, chunks)
    arrived = exchanged(sent)
    kept, taps = [], []
    for chunk, pieces in enumerate(arrived):
        at = slice(chunk * step, (chunk + 1) * step)
        grads, part = core(scalars, weight[at], bias[at], pieces)
        kept.append(grads)
        taps.append(part)
    returned = exchanged(kept)
    taps, returned[0] = lax.optimization_barrier((jnp.concatenate(taps, axis=0), returned[0]))
    taps = jnp.sum(lax.all_gather(taps, "dp"), axis=0)
    taps = taps.transpose(1, 0, 2).reshape(KERNEL + 1, heads * depth)
    weight_grad, bias_grad, returned = lax.optimization_barrier(
        (taps[:KERNEL], taps[KERNEL], returned)
    )
    query_grad, key_grad, value_grad = unpack(rank[None], returned, count, chunks)
    return query_grad, key_grad, value_grad, weight_grad, bias_grad


def solution(mesh):
    return jax.shard_map(
        on_device,
        mesh=mesh,
        in_specs=(
            P("dp", "seq", None),
            P("dp", "seq", None),
            P("dp", "seq", None),
            P("dp", "seq", None),
            P(),
            P(),
            P("dp"),
        ),
        out_specs=(
            P("dp", "seq", None),
            P("dp", "seq", None),
            P("dp", "seq", None),
            P(None, "seq"),
            P("seq"),
        ),
        check_vma=False,
    )
```

```python
import functools
import math

import jax
import jax.numpy as jnp
from jax import lax
from jax.experimental import pallas as pl
from jax.experimental.pallas import tpu as pltpu
from jax.sharding import PartitionSpec as P

HEADS = 16
KERNEL = 31
PAD = 16
CUTS = 4
masked_score = -1e30
VMEM = pl.BlockSpec(memory_space=pltpu.VMEM)
SMEM = pl.BlockSpec(memory_space=pltpu.SMEM)
LIMIT = 16 * 1024 * 1024
bf16, f32 = jnp.bfloat16, jnp.float32


def pack_kernel(count, chunks, rank_ref, *refs):
    arrays, outs, (plain, turned, sems) = refs[:4], refs[4:-3], refs[-3:]
    rank = rank_ref[0]
    high = outs[0].shape[1]
    share = high * chunks
    frames = plain.shape[1]
    cut = frames // CUTS

    def copy(which, part):
        at = pl.ds(part * cut, cut)
        return pltpu.make_async_copy(
            arrays[which].at[0, at, :], plain.at[which, at, :], sems.at[which, part]
        )

    for which in range(4):
        for part in range(CUTS):
            copy(which, part).start()
    for which in range(4):
        for part in range(CUTS):
            copy(which, part).wait()
        turned[which] = plain[which].T
        for distance in range(count):
            for chunk in range(chunks):
                first = pl.multiple_of((rank ^ distance) * share + chunk * high, 16)
                outs[chunk * count + distance][which] = turned[which, pl.ds(first, high), :]


def pack(rank, arrays, count, chunks):
    _, frames, width = arrays[0].shape
    high = width // count // chunks
    piece = jax.ShapeDtypeStruct((4, high, frames), bf16)
    outs = pl.pallas_call(
        functools.partial(pack_kernel, count, chunks),
        out_shape=(piece,) * (count * chunks),
        in_specs=[SMEM] + [pl.BlockSpec(memory_space=pltpu.HBM)] * 4,
        out_specs=(VMEM,) * (count * chunks),
        scratch_shapes=[
            pltpu.VMEM((4, frames, width), bf16),
            pltpu.VMEM((4, width, frames), bf16),
            pltpu.SemaphoreType.DMA((4, CUTS)),
        ],
        compiler_params=pltpu.CompilerParams(vmem_limit_bytes=LIMIT),
        cost_estimate=pl.CostEstimate(
            flops=0, bytes_accessed=16 * frames * width, transcendentals=0
        ),
    )(rank, *[pltpu.with_memory_space_constraint(array, pltpu.HBM) for array in arrays])
    return [outs[chunk * count : (chunk + 1) * count] for chunk in range(chunks)]


def unpack_kernel(count, chunks, rank_ref, taps_ref, *refs):
    pieces, outs, turned = refs[: count * chunks], refs[-6:-3], refs[-1]
    weight_ref, bias_ref = refs[-3:-1]
    taps = jnp.sum(taps_ref[...], axis=0)
    heads, _, depth = taps.shape
    for head in range(heads):
        at = slice(head * depth, (head + 1) * depth)
        weight_ref[:, at] = taps[head, :KERNEL]
        bias_ref[:, at] = taps[head, KERNEL:]
    rank = rank_ref[0]
    high = pieces[0].shape[1]
    share = high * chunks
    for which, out in enumerate(outs):
        for distance in range(count):
            for chunk in range(chunks):
                first = pl.multiple_of((rank ^ distance) * share + chunk * high, 16)
                turned[which, pl.ds(first, high), :] = pieces[chunk * count + distance][which]
        out[0] = turned[which].T


def unpack(rank, taps, pieces, count, chunks):
    _, high, frames = pieces[0][0].shape
    width = high * count * chunks
    whole = jax.ShapeDtypeStruct((1, frames, width), bf16)
    return pl.pallas_call(
        functools.partial(unpack_kernel, count, chunks),
        out_shape=(whole,) * 3
        + (
            jax.ShapeDtypeStruct((KERNEL, width // count), f32),
            jax.ShapeDtypeStruct((1, width // count), f32),
        ),
        in_specs=[SMEM] + [VMEM] * (1 + count * chunks),
        out_specs=(VMEM,) * 5,
        scratch_shapes=[pltpu.VMEM((3, width, frames), bf16)],
        compiler_params=pltpu.CompilerParams(vmem_limit_bytes=LIMIT),
        cost_estimate=pl.CostEstimate(
            flops=0, bytes_accessed=12 * frames * width, transcendentals=0
        ),
    )(rank, taps, *[piece for part in pieces for piece in part])


def core_kernel(count, block, scalars, weight_ref, bias_ref, *refs):
    pieces, outs, taps_ref = refs[:count], refs[count : 2 * count], refs[2 * count]
    q_t, k_t, v_t, a_t, q_n, k_n, v_n, g_n, a_n, probs, shifted, pre_grad = refs[2 * count + 1 :]
    heads, rows, depth = q_n.shape
    frames = pieces[0].shape[2]
    blocks = rows // block
    scale = 1.0 / math.sqrt(depth)
    log_scale = scale * math.log2(math.e)
    length, rank = scalars[0], scalars[1]

    def span(head):
        return slice(head * depth, (head + 1) * depth)

    for distance, piece in enumerate(pieces):
        at = pl.ds(pl.multiple_of((rank ^ distance) * frames, 128), frames)
        q_t[:, at] = piece[0]
        k_t[:, at] = piece[1]
        v_t[:, at] = piece[2]
        for head in range(heads):
            q_n[head, at, :] = piece[0, span(head), :].T
            k_n[head, at, :] = piece[1, span(head), :].T
            v_n[head, at, :] = piece[2, span(head), :].T
            g_n[head, at, :] = piece[3, span(head), :].T

    def forward(index, head):
        cols = pl.ds(pl.multiple_of(index * block, block), block)
        scores = jnp.dot(k_n[head], q_t[span(head), cols], preferred_element_type=f32)
        key_at = lax.broadcasted_iota(jnp.int32, scores.shape, 0)
        scores = jnp.where(key_at < length, scores, masked_score)
        exped = jnp.exp2((scores - jnp.max(scores, axis=0, keepdims=True)) * log_scale)
        found = exped * (1.0 / jnp.sum(exped, axis=0, keepdims=True))
        probs[head, :, cols] = found
        out = jnp.dot(v_t[span(head), :], found.astype(bf16), preferred_element_type=f32)
        frame_at = index * block + lax.broadcasted_iota(jnp.int32, out.shape, 1)
        a_t[span(head), cols] = jnp.where(frame_at < length, out, 0.0).astype(bf16)

    def each_block(body):
        if blocks == 1:
            for head in range(heads):
                body(0, head)
        else:

            def step(index, carry):
                for head in range(heads):
                    body(index, head)
                return carry

            lax.fori_loop(0, blocks, step, 0)

    each_block(forward)

    tall = shifted.shape[1]

    def shift_all(source_rows):
        shifted[0, 0:PAD, :] = jnp.zeros((PAD, depth), f32)
        shifted[0, PAD + rows : tall, :] = jnp.zeros((tall - PAD - rows, depth), f32)
        for first in range(0, rows, frames):
            shifted[0, PAD + first : PAD + first + frames, :] = source_rows(first)
        for s in range(1, 8):
            shifted[s, 0 : tall - 8, :] = shifted[0, s : tall - 8 + s, :]

    step_rows = 64

    def filtered(head, row, reverse):
        total = None
        for offset in range(1, KERNEL + 1):
            s, a = offset % 8, offset // 8 * 8
            tap = KERNEL - offset if reverse else offset - 1
            term = weight_ref[head, tap : tap + 1, :] * shifted[s, pl.ds(row + a, step_rows), :]
            total = term if total is None else total + term
        return total

    def eights(array):
        return jnp.sum(array.reshape(step_rows // 8, 8, depth), axis=0)

    for head in range(heads):
        shift_all(lambda first: a_t[span(head), first : first + frames].T.astype(f32))

        def conv_step(index, carry, head=head):
            row = pl.multiple_of(index * step_rows, step_rows)
            conv_pre = filtered(head, row, False) + bias_ref[head]
            sig = 1.0 / (1.0 + jnp.exp(-conv_pre))
            grad = g_n[head, pl.ds(row, step_rows), :].astype(f32)
            pre = grad * (sig * (1.0 + conv_pre * (1.0 - sig)))
            pre = pre.astype(bf16).astype(f32)
            pre_grad[pl.ds(row, step_rows), :] = pre
            new = []
            for offset in range(1, KERNEL + 1):
                s, a = offset % 8, offset // 8 * 8
                term = pre * shifted[s, pl.ds(row + a, step_rows), :]
                new.append(carry[offset - 1] + eights(term))
            new.append(carry[KERNEL] + eights(pre))
            return tuple(new)

        zero = jnp.zeros((8, depth), f32)
        sums = lax.fori_loop(0, rows // step_rows, conv_step, (zero,) * (KERNEL + 1))
        for tap in range(KERNEL + 1):
            taps_ref[head, tap : tap + 1, :] = jnp.sum(sums[tap], axis=0, keepdims=True)

        shift_all(lambda first: pre_grad[first : first + frames, :])

        def back_step(index, carry, head=head):
            row = pl.multiple_of(index * step_rows, step_rows)
            total = g_n[head, pl.ds(row, step_rows), :].astype(f32) + filtered(head, row, True)
            frame_at = row + lax.broadcasted_iota(jnp.int32, total.shape, 0)
            total = jnp.where(frame_at < length, total, 0.0)
            a_n[head, pl.ds(row, step_rows), :] = total.astype(bf16)
            return carry

        lax.fori_loop(0, rows // step_rows, back_step, 0)
        for first in range(0, rows, frames):
            a_t[span(head), first : first + frames] = a_n[head, first : first + frames, :].T

    def backward(index, head):
        cols = pl.ds(pl.multiple_of(index * block, block), block)
        score_grad = jnp.dot(v_n[head], a_t[span(head), cols], preferred_element_type=f32)
        found = probs[head, :, cols]
        delta = jnp.sum(found * score_grad, axis=0, keepdims=True)
        diff = (found * (score_grad - delta)).astype(bf16)
        value = jnp.dot(found.astype(bf16), a_n[head, cols, :], preferred_element_type=f32)
        key = jnp.dot(diff, q_n[head, cols, :], preferred_element_type=f32)
        query = jnp.dot(k_t[span(head), :], diff, preferred_element_type=f32)
        q_t[span(head), cols] = (query * scale).astype(bf16)
        return key, value

    def finish(head, key, value):
        for first in range(0, rows, frames):
            at = slice(first, first + frames)
            k_t[span(head), at] = (key[at, :] * scale).astype(bf16).T
            v_t[span(head), at] = value[at, :].astype(bf16).T

    for head in range(heads):
        if blocks == 1:
            finish(head, *backward(0, head))
        else:
            zeros = jnp.zeros((rows, depth), f32)

            def step(index, carry, head=head):
                key, value = backward(index, head)
                return carry[0] + key, carry[1] + value

            finish(head, *lax.fori_loop(0, blocks, step, (zeros, zeros)))

    for distance, out in enumerate(outs):
        at = pl.ds(pl.multiple_of((rank ^ distance) * frames, 128), frames)
        out[0] = q_t[:, at]
        out[1] = k_t[:, at]
        out[2] = v_t[:, at]


def core(scalars, weight, bias, pieces):
    count = len(pieces)
    _, high, frames = pieces[0].shape
    heads, _, depth = weight.shape
    rows = count * frames
    block = math.gcd(rows, 512)
    tall = rows + 2 * PAD + 8
    piece = jax.ShapeDtypeStruct((3, high, frames), bf16)
    turned = pltpu.VMEM((high, rows), bf16)
    plain = pltpu.VMEM((heads, rows, depth), bf16)
    outs = pl.pallas_call(
        functools.partial(core_kernel, count, block),
        out_shape=(piece,) * count + (jax.ShapeDtypeStruct((heads, KERNEL + 1, depth), f32),),
        in_specs=[SMEM] + [VMEM] * (2 + count),
        out_specs=(VMEM,) * (count + 1),
        scratch_shapes=[turned] * 4
        + [plain] * 5
        + [
            pltpu.VMEM((heads, rows, rows), f32),
            pltpu.VMEM((8, tall, depth), f32),
            pltpu.VMEM((rows, depth), f32),
        ],
        compiler_params=pltpu.CompilerParams(
            vmem_limit_bytes=12 * 2**20 + 8 * heads * rows * rows + 4096 * tall
        ),
        cost_estimate=pl.CostEstimate(
            flops=24 * rows * rows * high,
            bytes_accessed=14 * rows * high,
            transcendentals=heads * rows * rows,
        ),
    )(scalars, weight, bias, *pieces)
    return outs[:count], outs[count]


def exchanged(parts):
    done = []
    for pieces in parts:
        moved = [pieces[0]]
        for distance in range(1, len(pieces)):
            piece = pieces[distance]
            if done:
                piece, done[-1][distance] = lax.optimization_barrier((piece, done[-1][distance]))
            pairs = [(i, i ^ distance) for i in range(len(pieces))]
            moved.append(lax.ppermute(piece, "seq", pairs))
        done.append(moved)
    return done


def on_device(queries, keys, values, grad_out, conv_weight, conv_bias, lengths):
    count = lax.axis_size("seq")
    rank = lax.axis_index("seq").astype(jnp.int32)
    width = queries.shape[2]
    depth = width // HEADS
    heads = HEADS // count
    chunks = math.gcd(heads, 2)
    step = heads // chunks
    by_head = conv_weight.reshape(KERNEL, HEADS, depth).transpose(1, 0, 2)
    weight = lax.dynamic_slice_in_dim(by_head, rank * heads, heads, axis=0)
    bias = lax.dynamic_slice_in_dim(conv_bias.reshape(HEADS, 1, depth), rank * heads, heads, axis=0)
    scalars = jnp.stack([lengths[0], rank])
    sent = pack(rank[None], (queries, keys, values, grad_out), count, chunks)
    arrived = exchanged(sent)
    kept, taps = [], []
    for chunk, pieces in enumerate(arrived):
        at = slice(chunk * step, (chunk + 1) * step)
        grads, part = core(scalars, weight[at], bias[at], pieces)
        kept.append(grads)
        taps.append(part)
    returned = exchanged(kept)
    taps, returned[0] = lax.optimization_barrier((jnp.concatenate(taps, axis=0), returned[0]))
    taps = lax.all_gather(taps, "dp")
    query_grad, key_grad, value_grad, weight_grad, bias_grad = unpack(
        rank[None], taps, returned, count, chunks
    )
    return query_grad, key_grad, value_grad, weight_grad, bias_grad[0]


def solution(mesh):
    return jax.shard_map(
        on_device,
        mesh=mesh,
        in_specs=(
            P("dp", "seq", None),
            P("dp", "seq", None),
            P("dp", "seq", None),
            P("dp", "seq", None),
            P(),
            P(),
            P("dp"),
        ),
        out_specs=(
            P("dp", "seq", None),
            P("dp", "seq", None),
            P("dp", "seq", None),
            P(None, "seq"),
            P("seq"),
        ),
        check_vma=False,
    )
```

```python
import functools
import math

import jax
import jax.numpy as jnp
from jax import lax
from jax.experimental import pallas as pl
from jax.experimental.pallas import tpu as pltpu
from jax.sharding import PartitionSpec as P

HEADS = 16
KERNEL = 31
PAD = 16
CUTS = 4
masked_score = -1e30
VMEM = pl.BlockSpec(memory_space=pltpu.VMEM)
SMEM = pl.BlockSpec(memory_space=pltpu.SMEM)
LIMIT = 16 * 1024 * 1024
bf16, f32 = jnp.bfloat16, jnp.float32


def pack_kernel(count, chunks, rank_ref, *refs):
    arrays, outs, (plain, turned, sems) = refs[:4], refs[4:-3], refs[-3:]
    rank = rank_ref[0]
    high = outs[0].shape[1]
    share = high * chunks
    frames = plain.shape[1]
    cut = frames // CUTS

    def copy(which, part):
        at = pl.ds(part * cut, cut)
        return pltpu.make_async_copy(
            arrays[which].at[0, at, :], plain.at[which, at, :], sems.at[which, part]
        )

    for which in range(4):
        for part in range(CUTS):
            copy(which, part).start()
    for which in range(4):
        for part in range(CUTS):
            copy(which, part).wait()
        turned[which] = plain[which].T
        for distance in range(count):
            for chunk in range(chunks):
                first = pl.multiple_of((rank ^ distance) * share + chunk * high, 16)
                outs[chunk * count + distance][which] = turned[which, pl.ds(first, high), :]


def pack(rank, arrays, count, chunks):
    _, frames, width = arrays[0].shape
    high = width // count // chunks
    piece = jax.ShapeDtypeStruct((4, high, frames), bf16)
    outs = pl.pallas_call(
        functools.partial(pack_kernel, count, chunks),
        out_shape=(piece,) * (count * chunks),
        in_specs=[SMEM] + [pl.BlockSpec(memory_space=pltpu.HBM)] * 4,
        out_specs=(VMEM,) * (count * chunks),
        scratch_shapes=[
            pltpu.VMEM((4, frames, width), bf16),
            pltpu.VMEM((4, width, frames), bf16),
            pltpu.SemaphoreType.DMA((4, CUTS)),
        ],
        compiler_params=pltpu.CompilerParams(vmem_limit_bytes=LIMIT),
        cost_estimate=pl.CostEstimate(
            flops=0, bytes_accessed=16 * frames * width, transcendentals=0
        ),
    )(rank, *[pltpu.with_memory_space_constraint(array, pltpu.HBM) for array in arrays])
    return [outs[chunk * count : (chunk + 1) * count] for chunk in range(chunks)]


def unpack_kernel(count, chunks, rank_ref, taps_ref, *refs):
    pieces, outs = refs[: count * chunks], refs[-7:-4]
    weight_ref, bias_ref, bias_row, turned = refs[-4:]
    taps = jnp.sum(taps_ref[...], axis=0)
    heads, _, depth = taps.shape
    for head in range(heads):
        at = slice(head * depth, (head + 1) * depth)
        weight_ref[:, at] = taps[head, :KERNEL]
        bias_row[:, at] = taps[head, KERNEL:]
    bias_ref[...] = bias_row[0]
    rank = rank_ref[0]
    high = pieces[0].shape[1]
    share = high * chunks
    for which, out in enumerate(outs):
        for distance in range(count):
            for chunk in range(chunks):
                first = pl.multiple_of((rank ^ distance) * share + chunk * high, 16)
                turned[which, pl.ds(first, high), :] = pieces[chunk * count + distance][which]
        out[0] = turned[which].T


def unpack(rank, taps, pieces, count, chunks):
    _, high, frames = pieces[0][0].shape
    width = high * count * chunks
    whole = jax.ShapeDtypeStruct((1, frames, width), bf16)
    return pl.pallas_call(
        functools.partial(unpack_kernel, count, chunks),
        out_shape=(whole,) * 3
        + (
            jax.ShapeDtypeStruct((KERNEL, width // count), f32),
            jax.ShapeDtypeStruct((width // count,), f32),
        ),
        in_specs=[SMEM] + [VMEM] * (1 + count * chunks),
        out_specs=(VMEM,) * 5,
        scratch_shapes=[
            pltpu.VMEM((1, width // count), f32),
            pltpu.VMEM((3, width, frames), bf16),
        ],
        compiler_params=pltpu.CompilerParams(vmem_limit_bytes=LIMIT),
        cost_estimate=pl.CostEstimate(
            flops=0, bytes_accessed=12 * frames * width, transcendentals=0
        ),
    )(rank, taps, *[piece for part in pieces for piece in part])


def core_kernel(count, block, scalars, weight_ref, bias_ref, *refs):
    pieces, outs, taps_ref = refs[:count], refs[count : 2 * count], refs[2 * count]
    q_t, k_t, v_t, a_t, q_n, k_n, v_n, g_n, a_n, probs, shifted, pre_grad = refs[2 * count + 1 :]
    heads, rows, depth = q_n.shape
    frames = pieces[0].shape[2]
    blocks = rows // block
    scale = 1.0 / math.sqrt(depth)
    log_scale = scale * math.log2(math.e)
    length, rank = scalars[0], scalars[1]

    def span(head):
        return slice(head * depth, (head + 1) * depth)

    for distance, piece in enumerate(pieces):
        at = pl.ds(pl.multiple_of((rank ^ distance) * frames, 128), frames)
        q_t[:, at] = piece[0]
        k_t[:, at] = piece[1]
        v_t[:, at] = piece[2]
        for head in range(heads):
            q_n[head, at, :] = piece[0, span(head), :].T
            k_n[head, at, :] = piece[1, span(head), :].T
            v_n[head, at, :] = piece[2, span(head), :].T
            g_n[head, at, :] = piece[3, span(head), :].T

    def forward(index, head):
        cols = pl.ds(pl.multiple_of(index * block, block), block)
        scores = jnp.dot(k_n[head], q_t[span(head), cols], preferred_element_type=f32)
        key_at = lax.broadcasted_iota(jnp.int32, scores.shape, 0)
        scores = jnp.where(key_at < length, scores, masked_score)
        exped = jnp.exp2((scores - jnp.max(scores, axis=0, keepdims=True)) * log_scale)
        found = exped * (1.0 / jnp.sum(exped, axis=0, keepdims=True))
        probs[head, :, cols] = found
        out = jnp.dot(v_t[span(head), :], found.astype(bf16), preferred_element_type=f32)
        frame_at = index * block + lax.broadcasted_iota(jnp.int32, out.shape, 1)
        a_t[span(head), cols] = jnp.where(frame_at < length, out, 0.0).astype(bf16)

    def each_block(body):
        if blocks == 1:
            for head in range(heads):
                body(0, head)
        else:

            def step(index, carry):
                for head in range(heads):
                    body(index, head)
                return carry

            lax.fori_loop(0, blocks, step, 0)

    each_block(forward)

    tall = shifted.shape[1]

    def shift_all(source_rows):
        shifted[0, 0:PAD, :] = jnp.zeros((PAD, depth), f32)
        shifted[0, PAD + rows : tall, :] = jnp.zeros((tall - PAD - rows, depth), f32)
        for first in range(0, rows, frames):
            shifted[0, PAD + first : PAD + first + frames, :] = source_rows(first)
        for s in range(1, 8):
            shifted[s, 0 : tall - 8, :] = shifted[0, s : tall - 8 + s, :]

    step_rows = 64

    def filtered(head, row, reverse):
        total = None
        for offset in range(1, KERNEL + 1):
            s, a = offset % 8, offset // 8 * 8
            tap = KERNEL - offset if reverse else offset - 1
            term = weight_ref[head, tap : tap + 1, :] * shifted[s, pl.ds(row + a, step_rows), :]
            total = term if total is None else total + term
        return total

    def eights(array):
        return jnp.sum(array.reshape(step_rows // 8, 8, depth), axis=0)

    for head in range(heads):
        shift_all(lambda first: a_t[span(head), first : first + frames].T.astype(f32))

        def conv_step(index, carry, head=head):
            row = pl.multiple_of(index * step_rows, step_rows)
            conv_pre = filtered(head, row, False) + bias_ref[head]
            sig = 1.0 / (1.0 + jnp.exp(-conv_pre))
            grad = g_n[head, pl.ds(row, step_rows), :].astype(f32)
            pre = grad * (sig * (1.0 + conv_pre * (1.0 - sig)))
            pre = pre.astype(bf16).astype(f32)
            pre_grad[pl.ds(row, step_rows), :] = pre
            new = []
            for offset in range(1, KERNEL + 1):
                s, a = offset % 8, offset // 8 * 8
                term = pre * shifted[s, pl.ds(row + a, step_rows), :]
                new.append(carry[offset - 1] + eights(term))
            new.append(carry[KERNEL] + eights(pre))
            return tuple(new)

        zero = jnp.zeros((8, depth), f32)
        sums = lax.fori_loop(0, rows // step_rows, conv_step, (zero,) * (KERNEL + 1))
        for tap in range(KERNEL + 1):
            taps_ref[head, tap : tap + 1, :] = jnp.sum(sums[tap], axis=0, keepdims=True)

        shift_all(lambda first: pre_grad[first : first + frames, :])

        def back_step(index, carry, head=head):
            row = pl.multiple_of(index * step_rows, step_rows)
            total = g_n[head, pl.ds(row, step_rows), :].astype(f32) + filtered(head, row, True)
            frame_at = row + lax.broadcasted_iota(jnp.int32, total.shape, 0)
            total = jnp.where(frame_at < length, total, 0.0)
            a_n[head, pl.ds(row, step_rows), :] = total.astype(bf16)
            return carry

        lax.fori_loop(0, rows // step_rows, back_step, 0)
        for first in range(0, rows, frames):
            a_t[span(head), first : first + frames] = a_n[head, first : first + frames, :].T

    def backward(index, head):
        cols = pl.ds(pl.multiple_of(index * block, block), block)
        score_grad = jnp.dot(v_n[head], a_t[span(head), cols], preferred_element_type=f32)
        found = probs[head, :, cols]
        delta = jnp.sum(found * score_grad, axis=0, keepdims=True)
        diff = (found * (score_grad - delta)).astype(bf16)
        value = jnp.dot(found.astype(bf16), a_n[head, cols, :], preferred_element_type=f32)
        key = jnp.dot(diff, q_n[head, cols, :], preferred_element_type=f32)
        query = jnp.dot(k_t[span(head), :], diff, preferred_element_type=f32)
        q_t[span(head), cols] = (query * scale).astype(bf16)
        return key, value

    def finish(head, key, value):
        for first in range(0, rows, frames):
            at = slice(first, first + frames)
            k_t[span(head), at] = (key[at, :] * scale).astype(bf16).T
            v_t[span(head), at] = value[at, :].astype(bf16).T

    for head in range(heads):
        if blocks == 1:
            finish(head, *backward(0, head))
        else:
            zeros = jnp.zeros((rows, depth), f32)

            def step(index, carry, head=head):
                key, value = backward(index, head)
                return carry[0] + key, carry[1] + value

            finish(head, *lax.fori_loop(0, blocks, step, (zeros, zeros)))

    for distance, out in enumerate(outs):
        at = pl.ds(pl.multiple_of((rank ^ distance) * frames, 128), frames)
        out[0] = q_t[:, at]
        out[1] = k_t[:, at]
        out[2] = v_t[:, at]


def core(scalars, weight, bias, pieces):
    count = len(pieces)
    _, high, frames = pieces[0].shape
    heads, _, depth = weight.shape
    rows = count * frames
    block = math.gcd(rows, 512)
    tall = rows + 2 * PAD + 8
    piece = jax.ShapeDtypeStruct((3, high, frames), bf16)
    turned = pltpu.VMEM((high, rows), bf16)
    plain = pltpu.VMEM((heads, rows, depth), bf16)
    outs = pl.pallas_call(
        functools.partial(core_kernel, count, block),
        out_shape=(piece,) * count + (jax.ShapeDtypeStruct((heads, KERNEL + 1, depth), f32),),
        in_specs=[SMEM] + [VMEM] * (2 + count),
        out_specs=(VMEM,) * (count + 1),
        scratch_shapes=[turned] * 4
        + [plain] * 5
        + [
            pltpu.VMEM((heads, rows, rows), f32),
            pltpu.VMEM((8, tall, depth), f32),
            pltpu.VMEM((rows, depth), f32),
        ],
        compiler_params=pltpu.CompilerParams(
            vmem_limit_bytes=12 * 2**20 + 8 * heads * rows * rows + 4096 * tall
        ),
        cost_estimate=pl.CostEstimate(
            flops=24 * rows * rows * high,
            bytes_accessed=14 * rows * high,
            transcendentals=heads * rows * rows,
        ),
    )(scalars, weight, bias, *pieces)
    return outs[:count], outs[count]


def exchanged(parts):
    done = []
    for pieces in parts:
        pieces = list(pieces)
        if done and len(pieces) > 2:
            pieces[2:], before = lax.optimization_barrier((pieces[2:], done[-1][1:]))
            done[-1] = done[-1][:1] + list(before)
        moved = [pieces[0]]
        for distance in range(1, len(pieces)):
            pairs = [(i, i ^ distance) for i in range(len(pieces))]
            moved.append(lax.ppermute(pieces[distance], "seq", pairs))
        done.append(moved)
    return done


def on_device(queries, keys, values, grad_out, conv_weight, conv_bias, lengths):
    count = lax.axis_size("seq")
    rank = lax.axis_index("seq").astype(jnp.int32)
    width = queries.shape[2]
    depth = width // HEADS
    heads = HEADS // count
    chunks = math.gcd(heads, 2)
    step = heads // chunks
    by_head = conv_weight.reshape(KERNEL, HEADS, depth).transpose(1, 0, 2)
    weight = lax.dynamic_slice_in_dim(by_head, rank * heads, heads, axis=0)
    bias = lax.dynamic_slice_in_dim(conv_bias.reshape(HEADS, 1, depth), rank * heads, heads, axis=0)
    scalars = jnp.stack([lengths[0], rank])
    sent = pack(rank[None], (queries, keys, values, grad_out), count, chunks)
    arrived = exchanged(sent)
    kept, taps = [], []
    for chunk, pieces in enumerate(arrived):
        at = slice(chunk * step, (chunk + 1) * step)
        grads, part = core(scalars, weight[at], bias[at], pieces)
        kept.append(grads)
        taps.append(part)
    returned = exchanged(kept)
    taps, returned[0] = lax.optimization_barrier((jnp.concatenate(taps, axis=0), returned[0]))
    taps = lax.all_gather(taps, "dp")
    return unpack(rank[None], taps, returned, count, chunks)


def solution(mesh):
    return jax.shard_map(
        on_device,
        mesh=mesh,
        in_specs=(
            P("dp", "seq", None),
            P("dp", "seq", None),
            P("dp", "seq", None),
            P("dp", "seq", None),
            P(),
            P(),
            P("dp"),
        ),
        out_specs=(
            P("dp", "seq", None),
            P("dp", "seq", None),
            P("dp", "seq", None),
            P(None, "seq"),
            P("seq"),
        ),
        check_vma=False,
    )
```

```python
import functools
import math

import jax
import jax.numpy as jnp
from jax import lax
from jax.experimental import pallas as pl
from jax.experimental.pallas import tpu as pltpu
from jax.sharding import PartitionSpec as P

HEADS = 16
KERNEL = 31
PAD = 16
CUTS = 4
masked_score = -1e30
VMEM = pl.BlockSpec(memory_space=pltpu.VMEM)
SMEM = pl.BlockSpec(memory_space=pltpu.SMEM)
LIMIT = 16 * 1024 * 1024
bf16, f32 = jnp.bfloat16, jnp.float32


def pack_kernel(count, chunks, rank_ref, *refs):
    arrays, outs, (plain, turned, sems) = refs[:4], refs[4:-3], refs[-3:]
    rank = rank_ref[0]
    high = outs[0].shape[1]
    share = high * chunks
    frames = plain.shape[1]
    cut = frames // CUTS

    def copy(which, part):
        at = pl.ds(part * cut, cut)
        return pltpu.make_async_copy(
            arrays[which].at[0, at, :], plain.at[which, at, :], sems.at[which, part]
        )

    for which in range(4):
        for part in range(CUTS):
            copy(which, part).start()
    for which in range(4):
        for part in range(CUTS):
            copy(which, part).wait()
        turned[which] = plain[which].T
        for distance in range(count):
            for chunk in range(chunks):
                first = pl.multiple_of((rank ^ distance) * share + chunk * high, 16)
                outs[chunk * count + distance][which] = turned[which, pl.ds(first, high), :]


def pack(rank, arrays, count, chunks):
    _, frames, width = arrays[0].shape
    high = width // count // chunks
    piece = jax.ShapeDtypeStruct((4, high, frames), bf16)
    outs = pl.pallas_call(
        functools.partial(pack_kernel, count, chunks),
        out_shape=(piece,) * (count * chunks),
        in_specs=[SMEM] + [pl.BlockSpec(memory_space=pltpu.HBM)] * 4,
        out_specs=(VMEM,) * (count * chunks),
        scratch_shapes=[
            pltpu.VMEM((4, frames, width), bf16),
            pltpu.VMEM((4, width, frames), bf16),
            pltpu.SemaphoreType.DMA((4, CUTS)),
        ],
        compiler_params=pltpu.CompilerParams(vmem_limit_bytes=LIMIT),
        cost_estimate=pl.CostEstimate(
            flops=0, bytes_accessed=16 * frames * width, transcendentals=0
        ),
    )(rank, *[pltpu.with_memory_space_constraint(array, pltpu.HBM) for array in arrays])
    return [outs[chunk * count : (chunk + 1) * count] for chunk in range(chunks)]


def unpack_kernel(count, chunks, rank_ref, taps_ref, *refs):
    pieces, outs = refs[: count * chunks], refs[-7:-4]
    weight_ref, bias_ref, bias_row, turned = refs[-4:]
    taps = jnp.sum(taps_ref[...], axis=0)
    heads, _, depth = taps.shape
    for head in range(heads):
        at = slice(head * depth, (head + 1) * depth)
        weight_ref[:, at] = taps[head, :KERNEL]
        bias_row[:, at] = taps[head, KERNEL:]
    bias_ref[...] = bias_row[0]
    rank = rank_ref[0]
    high = pieces[0].shape[1]
    share = high * chunks
    for which, out in enumerate(outs):
        for distance in range(count):
            for chunk in range(chunks):
                first = pl.multiple_of((rank ^ distance) * share + chunk * high, 16)
                turned[which, pl.ds(first, high), :] = pieces[chunk * count + distance][which]
        out[0] = turned[which].T


def unpack(rank, taps, pieces, count, chunks):
    _, high, frames = pieces[0][0].shape
    width = high * count * chunks
    whole = jax.ShapeDtypeStruct((1, frames, width), bf16)
    return pl.pallas_call(
        functools.partial(unpack_kernel, count, chunks),
        out_shape=(whole,) * 3
        + (
            jax.ShapeDtypeStruct((KERNEL, width // count), f32),
            jax.ShapeDtypeStruct((width // count,), f32),
        ),
        in_specs=[SMEM] + [VMEM] * (1 + count * chunks),
        out_specs=(VMEM,) * 5,
        scratch_shapes=[
            pltpu.VMEM((1, width // count), f32),
            pltpu.VMEM((3, width, frames), bf16),
        ],
        compiler_params=pltpu.CompilerParams(vmem_limit_bytes=LIMIT),
        cost_estimate=pl.CostEstimate(
            flops=0, bytes_accessed=12 * frames * width, transcendentals=0
        ),
    )(rank, taps, *[piece for part in pieces for piece in part])


def core_kernel(count, block, scalars, weight_ref, bias_ref, *refs):
    pieces, outs, taps_ref = refs[:count], refs[count : 2 * count], refs[2 * count]
    q_t, k_t, v_t, a_t, q_n, k_n, v_n, g_n, a_n = refs[2 * count + 1 : -7]
    probs, norm, low, diff, score_grads, shifted, pre_grad = refs[-7:]
    heads, rows, depth = q_n.shape
    frames = pieces[0].shape[2]
    blocks = rows // block
    scale = 1.0 / math.sqrt(depth)
    log_scale = scale * math.log2(math.e)
    length, rank = scalars[0], scalars[1]

    def span(head):
        return slice(head * depth, (head + 1) * depth)

    for distance, piece in enumerate(pieces):
        at = pl.ds(pl.multiple_of((rank ^ distance) * frames, 128), frames)
        q_t[:, at] = piece[0]
        k_t[:, at] = piece[1]
        v_t[:, at] = piece[2]
        for head in range(heads):
            q_n[head, at, :] = piece[0, span(head), :].T
            k_n[head, at, :] = piece[1, span(head), :].T
            v_n[head, at, :] = piece[2, span(head), :].T
            g_n[head, at, :] = piece[3, span(head), :].T

    tile, strip = 128, 256
    tiles = [slice(first, first + tile) for first in range(0, rows, tile)]

    def strips(index):
        for first in range(0, block, strip):
            cols = pl.ds(pl.multiple_of(index * block + first, strip), strip)
            yield index * block + first, cols, slice(first, first + strip)

    def folded(array):
        return array.reshape(tile // 8, 8, strip)

    def forward(index, head):
        for start, cols, inner in strips(index):
            queries = q_t[span(head), cols]
            top = jnp.full((8, strip), masked_score, f32)
            for at in tiles:
                scores = jnp.dot(k_n[head, at, :], queries, preferred_element_type=f32)
                key_at = at.start + lax.broadcasted_iota(jnp.int32, scores.shape, 0)
                scores = jnp.where(key_at < length, scores, masked_score)
                probs[head, at, cols] = scores
                top = jnp.maximum(top, jnp.max(folded(scores), axis=0))
            top = jnp.max(top, axis=0, keepdims=True)
            total = jnp.zeros((8, strip), f32)
            for at in tiles:
                exped = jnp.exp2((probs[head, at, cols] - top) * log_scale)
                probs[head, at, cols] = exped
                low[at, inner] = exped.astype(bf16)
                total = total + jnp.sum(folded(exped), axis=0)
            inverse = 1.0 / jnp.sum(total, axis=0, keepdims=True)
            norm[head, :, cols] = inverse
            out = jnp.dot(v_t[span(head), :], low[:, inner], preferred_element_type=f32) * inverse
            frame_at = start + lax.broadcasted_iota(jnp.int32, out.shape, 1)
            a_t[span(head), cols] = jnp.where(frame_at < length, out, 0.0).astype(bf16)

    def each_block(body):
        if blocks == 1:
            for head in range(heads):
                body(0, head)
        else:

            def step(index, carry):
                for head in range(heads):
                    body(index, head)
                return carry

            lax.fori_loop(0, blocks, step, 0)

    each_block(forward)

    tall = shifted.shape[1]

    def shift_all(source_rows):
        shifted[0, 0:PAD, :] = jnp.zeros((PAD, depth), f32)
        shifted[0, PAD + rows : tall, :] = jnp.zeros((tall - PAD - rows, depth), f32)
        for first in range(0, rows, frames):
            shifted[0, PAD + first : PAD + first + frames, :] = source_rows(first)
        for s in range(1, 8):
            shifted[s, 0 : tall - 8, :] = shifted[0, s : tall - 8 + s, :]

    step_rows = 64

    def filtered(head, row, reverse):
        total = None
        for offset in range(1, KERNEL + 1):
            s, a = offset % 8, offset // 8 * 8
            tap = KERNEL - offset if reverse else offset - 1
            term = weight_ref[head, tap : tap + 1, :] * shifted[s, pl.ds(row + a, step_rows), :]
            total = term if total is None else total + term
        return total

    def eights(array):
        return jnp.sum(array.reshape(step_rows // 8, 8, depth), axis=0)

    for head in range(heads):
        shift_all(lambda first: a_t[span(head), first : first + frames].T.astype(f32))

        def conv_step(index, carry, head=head):
            row = pl.multiple_of(index * step_rows, step_rows)
            conv_pre = filtered(head, row, False) + bias_ref[head]
            sig = 1.0 / (1.0 + jnp.exp(-conv_pre))
            grad = g_n[head, pl.ds(row, step_rows), :].astype(f32)
            pre = grad * (sig * (1.0 + conv_pre * (1.0 - sig)))
            pre = pre.astype(bf16).astype(f32)
            pre_grad[pl.ds(row, step_rows), :] = pre
            new = []
            for offset in range(1, KERNEL + 1):
                s, a = offset % 8, offset // 8 * 8
                term = pre * shifted[s, pl.ds(row + a, step_rows), :]
                new.append(carry[offset - 1] + eights(term))
            new.append(carry[KERNEL] + eights(pre))
            return tuple(new)

        zero = jnp.zeros((8, depth), f32)
        sums = lax.fori_loop(0, rows // step_rows, conv_step, (zero,) * (KERNEL + 1))
        for tap in range(KERNEL + 1):
            taps_ref[head, tap : tap + 1, :] = jnp.sum(sums[tap], axis=0, keepdims=True)

        shift_all(lambda first: pre_grad[first : first + frames, :])

        def back_step(index, carry, head=head):
            row = pl.multiple_of(index * step_rows, step_rows)
            total = g_n[head, pl.ds(row, step_rows), :].astype(f32) + filtered(head, row, True)
            frame_at = row + lax.broadcasted_iota(jnp.int32, total.shape, 0)
            total = jnp.where(frame_at < length, total, 0.0)
            a_n[head, pl.ds(row, step_rows), :] = total.astype(bf16)
            return carry

        lax.fori_loop(0, rows // step_rows, back_step, 0)
        for first in range(0, rows, frames):
            a_t[span(head), first : first + frames] = a_n[head, first : first + frames, :].T

    def backward(index, head):
        for start, cols, inner in strips(index):
            inverse = norm[head, :, cols]
            grads = a_t[span(head), cols]
            total = jnp.zeros((8, strip), f32)
            for at in tiles:
                score_grad = jnp.dot(v_n[head, at, :], grads, preferred_element_type=f32)
                score_grads[at, inner] = score_grad
                total = total + jnp.sum(folded(probs[head, at, cols] * score_grad), axis=0)
            delta = jnp.sum(total, axis=0, keepdims=True) * inverse
            for at in tiles:
                found = probs[head, at, cols] * inverse
                low[at, inner] = found.astype(bf16)
                diff[at, inner] = (found * (score_grads[at, inner] - delta)).astype(bf16)
        cols = pl.ds(pl.multiple_of(index * block, block), block)
        value = jnp.dot(low[...], a_n[head, cols, :], preferred_element_type=f32)
        key = jnp.dot(diff[...], q_n[head, cols, :], preferred_element_type=f32)
        query = jnp.dot(k_t[span(head), :], diff[...], preferred_element_type=f32)
        q_t[span(head), cols] = (query * scale).astype(bf16)
        return key, value

    def finish(head, key, value):
        for first in range(0, rows, frames):
            at = slice(first, first + frames)
            k_t[span(head), at] = (key[at, :] * scale).astype(bf16).T
            v_t[span(head), at] = value[at, :].astype(bf16).T

    for head in range(heads):
        if blocks == 1:
            finish(head, *backward(0, head))
        else:
            zeros = jnp.zeros((rows, depth), f32)

            def step(index, carry, head=head):
                key, value = backward(index, head)
                return carry[0] + key, carry[1] + value

            finish(head, *lax.fori_loop(0, blocks, step, (zeros, zeros)))

    for distance, out in enumerate(outs):
        at = pl.ds(pl.multiple_of((rank ^ distance) * frames, 128), frames)
        out[0] = q_t[:, at]
        out[1] = k_t[:, at]
        out[2] = v_t[:, at]


def core(scalars, weight, bias, pieces):
    count = len(pieces)
    _, high, frames = pieces[0].shape
    heads, _, depth = weight.shape
    rows = count * frames
    block = math.gcd(rows, 512)
    tall = rows + 2 * PAD + 8
    piece = jax.ShapeDtypeStruct((3, high, frames), bf16)
    turned = pltpu.VMEM((high, rows), bf16)
    plain = pltpu.VMEM((heads, rows, depth), bf16)
    outs = pl.pallas_call(
        functools.partial(core_kernel, count, block),
        out_shape=(piece,) * count + (jax.ShapeDtypeStruct((heads, KERNEL + 1, depth), f32),),
        in_specs=[SMEM] + [VMEM] * (2 + count),
        out_specs=(VMEM,) * (count + 1),
        scratch_shapes=[turned] * 4
        + [plain] * 5
        + [
            pltpu.VMEM((heads, rows, rows), f32),
            pltpu.VMEM((heads, 1, rows), f32),
            pltpu.VMEM((rows, block), bf16),
            pltpu.VMEM((rows, block), bf16),
            pltpu.VMEM((rows, block), f32),
            pltpu.VMEM((8, tall, depth), f32),
            pltpu.VMEM((rows, depth), f32),
        ],
        compiler_params=pltpu.CompilerParams(
            vmem_limit_bytes=12 * 2**20 + 8 * heads * rows * rows + 4096 * tall
        ),
        cost_estimate=pl.CostEstimate(
            flops=24 * rows * rows * high,
            bytes_accessed=14 * rows * high,
            transcendentals=heads * rows * rows,
        ),
    )(scalars, weight, bias, *pieces)
    return outs[:count], outs[count]


def exchanged(parts):
    done = []
    for pieces in parts:
        pieces = list(pieces)
        if done and len(pieces) > 2:
            pieces[1:-1], before = lax.optimization_barrier((pieces[1:-1], done[-1][1:]))
            done[-1] = done[-1][:1] + list(before)
        moved = [pieces[0]]
        for distance in range(1, len(pieces)):
            pairs = [(i, i ^ distance) for i in range(len(pieces))]
            moved.append(lax.ppermute(pieces[distance], "seq", pairs))
        done.append(moved)
    return done


def on_device(queries, keys, values, grad_out, conv_weight, conv_bias, lengths):
    count = lax.axis_size("seq")
    rank = lax.axis_index("seq").astype(jnp.int32)
    width = queries.shape[2]
    depth = width // HEADS
    heads = HEADS // count
    chunks = math.gcd(heads, 2)
    step = heads // chunks
    by_head = conv_weight.reshape(KERNEL, HEADS, depth).transpose(1, 0, 2)
    weight = lax.dynamic_slice_in_dim(by_head, rank * heads, heads, axis=0)
    bias = lax.dynamic_slice_in_dim(conv_bias.reshape(HEADS, 1, depth), rank * heads, heads, axis=0)
    scalars = jnp.stack([lengths[0], rank])
    sent = pack(rank[None], (queries, keys, values, grad_out), count, chunks)
    arrived = exchanged(sent)
    kept, taps = [], []
    for chunk, pieces in enumerate(arrived):
        at = slice(chunk * step, (chunk + 1) * step)
        grads, part = core(scalars, weight[at], bias[at], pieces)
        kept.append(grads)
        taps.append(part)
    returned = exchanged(kept)
    taps, returned[0] = lax.optimization_barrier((jnp.concatenate(taps, axis=0), returned[0]))
    taps = lax.all_gather(taps, "dp")
    return unpack(rank[None], taps, returned, count, chunks)


def solution(mesh):
    return jax.shard_map(
        on_device,
        mesh=mesh,
        in_specs=(
            P("dp", "seq", None),
            P("dp", "seq", None),
            P("dp", "seq", None),
            P("dp", "seq", None),
            P(),
            P(),
            P("dp"),
        ),
        out_specs=(
            P("dp", "seq", None),
            P("dp", "seq", None),
            P("dp", "seq", None),
            P(None, "seq"),
            P("seq"),
        ),
        check_vma=False,
    )
```

```python
import functools
import math

import jax
import jax.numpy as jnp
from jax import lax
from jax.experimental import pallas as pl
from jax.experimental.pallas import tpu as pltpu
from jax.sharding import PartitionSpec as P

HEADS = 16
KERNEL = 31
PAD = 16
CUTS = 4
masked_score = -1e30
VMEM = pl.BlockSpec(memory_space=pltpu.VMEM)
SMEM = pl.BlockSpec(memory_space=pltpu.SMEM)
LIMIT = 16 * 1024 * 1024
bf16, f32 = jnp.bfloat16, jnp.float32


def pack_kernel(count, chunks, rank_ref, *refs):
    arrays, outs, (plain, turned, sems) = refs[:4], refs[4:-3], refs[-3:]
    rank = rank_ref[0]
    high = outs[0].shape[1]
    share = high * chunks
    frames = plain.shape[1]
    cut = frames // CUTS

    def copy(which, part):
        at = pl.ds(part * cut, cut)
        return pltpu.make_async_copy(
            arrays[which].at[0, at, :], plain.at[which, at, :], sems.at[which, part]
        )

    for which in range(4):
        for part in range(CUTS):
            copy(which, part).start()
    for which in range(4):
        for part in range(CUTS):
            copy(which, part).wait()
        turned[which] = plain[which].T
        for distance in range(count):
            for chunk in range(chunks):
                first = pl.multiple_of((rank ^ distance) * share + chunk * high, 16)
                outs[chunk * count + distance][which] = turned[which, pl.ds(first, high), :]


def pack(rank, arrays, count, chunks):
    _, frames, width = arrays[0].shape
    high = width // count // chunks
    piece = jax.ShapeDtypeStruct((4, high, frames), bf16)
    outs = pl.pallas_call(
        functools.partial(pack_kernel, count, chunks),
        out_shape=(piece,) * (count * chunks),
        in_specs=[SMEM] + [pl.BlockSpec(memory_space=pltpu.HBM)] * 4,
        out_specs=(VMEM,) * (count * chunks),
        scratch_shapes=[
            pltpu.VMEM((4, frames, width), bf16),
            pltpu.VMEM((4, width, frames), bf16),
            pltpu.SemaphoreType.DMA((4, CUTS)),
        ],
        compiler_params=pltpu.CompilerParams(vmem_limit_bytes=LIMIT),
        cost_estimate=pl.CostEstimate(
            flops=0, bytes_accessed=16 * frames * width, transcendentals=0
        ),
    )(rank, *[pltpu.with_memory_space_constraint(array, pltpu.HBM) for array in arrays])
    return [outs[chunk * count : (chunk + 1) * count] for chunk in range(chunks)]


def unpack_kernel(count, chunks, rank_ref, taps_ref, *refs):
    pieces, outs = refs[: count * chunks], refs[-7:-4]
    weight_ref, bias_ref, bias_row, turned = refs[-4:]
    taps = jnp.sum(taps_ref[...], axis=0)
    heads, _, depth = taps.shape
    for head in range(heads):
        at = slice(head * depth, (head + 1) * depth)
        weight_ref[:, at] = taps[head, :KERNEL]
        bias_row[:, at] = taps[head, KERNEL:]
    bias_ref[...] = bias_row[0]
    rank = rank_ref[0]
    high = pieces[0].shape[1]
    share = high * chunks
    for which, out in enumerate(outs):
        for distance in range(count):
            for chunk in range(chunks):
                first = pl.multiple_of((rank ^ distance) * share + chunk * high, 16)
                turned[which, pl.ds(first, high), :] = pieces[chunk * count + distance][which]
        out[0] = turned[which].T


def unpack(rank, taps, pieces, count, chunks):
    _, high, frames = pieces[0][0].shape
    width = high * count * chunks
    whole = jax.ShapeDtypeStruct((1, frames, width), bf16)
    return pl.pallas_call(
        functools.partial(unpack_kernel, count, chunks),
        out_shape=(whole,) * 3
        + (
            jax.ShapeDtypeStruct((KERNEL, width // count), f32),
            jax.ShapeDtypeStruct((width // count,), f32),
        ),
        in_specs=[SMEM] + [VMEM] * (1 + count * chunks),
        out_specs=(VMEM,) * 5,
        scratch_shapes=[
            pltpu.VMEM((1, width // count), f32),
            pltpu.VMEM((3, width, frames), bf16),
        ],
        compiler_params=pltpu.CompilerParams(vmem_limit_bytes=LIMIT),
        cost_estimate=pl.CostEstimate(
            flops=0, bytes_accessed=12 * frames * width, transcendentals=0
        ),
    )(rank, taps, *[piece for part in pieces for piece in part])


def core_kernel(count, block, scalars, weight_ref, bias_ref, *refs):
    pieces, outs, taps_ref = refs[:count], refs[count : 2 * count], refs[2 * count]
    q_t, k_t, v_t, a_t, q_n, k_n, v_n, g_n, a_n, probs, shifted, padded = refs[2 * count + 1 :]
    heads, rows, depth = q_n.shape
    frames = pieces[0].shape[2]
    blocks = rows // block
    scale = 1.0 / math.sqrt(depth)
    log_scale = scale * math.log2(math.e)
    length, rank = scalars[0], scalars[1]

    def span(head):
        return slice(head * depth, (head + 1) * depth)

    for distance, piece in enumerate(pieces):
        at = pl.ds(pl.multiple_of((rank ^ distance) * frames, 128), frames)
        q_t[:, at] = piece[0]
        k_t[:, at] = piece[1]
        v_t[:, at] = piece[2]
        for head in range(heads):
            q_n[head, at, :] = piece[0, span(head), :].T
            k_n[head, at, :] = piece[1, span(head), :].T
            v_n[head, at, :] = piece[2, span(head), :].T
            g_n[head, at, :] = piece[3, span(head), :].T

    def forward(index, head):
        cols = pl.ds(pl.multiple_of(index * block, block), block)
        scores = jnp.dot(k_n[head], q_t[span(head), cols], preferred_element_type=f32)
        key_at = lax.broadcasted_iota(jnp.int32, scores.shape, 0)
        scores = jnp.where(key_at < length, scores, masked_score)
        exped = jnp.exp2((scores - jnp.max(scores, axis=0, keepdims=True)) * log_scale)
        found = exped * (1.0 / jnp.sum(exped, axis=0, keepdims=True))
        probs[head, :, cols] = found
        out = jnp.dot(v_t[span(head), :], found.astype(bf16), preferred_element_type=f32)
        frame_at = index * block + lax.broadcasted_iota(jnp.int32, out.shape, 1)
        a_t[span(head), cols] = jnp.where(frame_at < length, out, 0.0).astype(bf16)

    def each_block(body):
        if blocks == 1:
            for head in range(heads):
                body(0, head)
        else:

            def step(index, carry):
                for head in range(heads):
                    body(index, head)
                return carry

            lax.fori_loop(0, blocks, step, 0)

    each_block(forward)

    tall = padded.shape[0]
    padded[0:PAD, :] = jnp.zeros((PAD, depth), f32)
    padded[PAD + rows : tall, :] = jnp.zeros((tall - PAD - rows, depth), f32)

    def shift_all():
        for s in range(8):
            shifted[s] = padded[s : s + tall - 8, :].reshape(tall // 8 - 1, 8, depth)

    step_tiles = 8
    step_rows = 8 * step_tiles

    def window(index, offset):
        return shifted[offset % 8, pl.ds(index * step_tiles + offset // 8, step_tiles)]

    def filtered(head, index, reverse):
        total = None
        for offset in range(1, KERNEL + 1):
            tap = KERNEL - offset if reverse else offset - 1
            term = weight_ref[head, tap : tap + 1, :] * window(index, offset)
            total = term if total is None else total + term
        return total

    def loaded(ref, index):
        at = pl.ds(pl.multiple_of(index * step_rows, step_rows), step_rows)
        return ref[at, :].astype(f32).reshape(step_tiles, 8, depth)

    for head in range(heads):
        for first in range(0, rows, frames):
            at = slice(PAD + first, PAD + first + frames)
            padded[at, :] = a_t[span(head), first : first + frames].T.astype(f32)
        shift_all()

        def conv_step(index, carry, head=head):
            conv_pre = filtered(head, index, False) + bias_ref[head]
            sig = 1.0 / (1.0 + jnp.exp(-conv_pre))
            pre = loaded(g_n.at[head], index) * (sig * (1.0 + conv_pre * (1.0 - sig)))
            pre = pre.astype(bf16).astype(f32)
            at = pl.ds(pl.multiple_of(PAD + index * step_rows, PAD), step_rows)
            padded[at, :] = pre.reshape(step_rows, depth)
            new = []
            for offset in range(1, KERNEL + 1):
                new.append(carry[offset - 1] + jnp.sum(pre * window(index, offset), axis=0))
            new.append(carry[KERNEL] + jnp.sum(pre, axis=0))
            return tuple(new)

        zero = jnp.zeros((8, depth), f32)
        sums = lax.fori_loop(0, rows // step_rows, conv_step, (zero,) * (KERNEL + 1))
        for tap in range(KERNEL + 1):
            taps_ref[head, tap : tap + 1, :] = jnp.sum(sums[tap], axis=0, keepdims=True)
        shift_all()

        def back_step(index, carry, head=head):
            total = loaded(g_n.at[head], index) + filtered(head, index, True)
            total = total.reshape(step_rows, depth)
            frame_at = index * step_rows + lax.broadcasted_iota(jnp.int32, total.shape, 0)
            total = jnp.where(frame_at < length, total, 0.0)
            at = pl.ds(pl.multiple_of(index * step_rows, step_rows), step_rows)
            a_n[head, at, :] = total.astype(bf16)
            return carry

        lax.fori_loop(0, rows // step_rows, back_step, 0)
        for first in range(0, rows, frames):
            a_t[span(head), first : first + frames] = a_n[head, first : first + frames, :].T

    def backward(index, head):
        cols = pl.ds(pl.multiple_of(index * block, block), block)
        score_grad = jnp.dot(v_n[head], a_t[span(head), cols], preferred_element_type=f32)
        found = probs[head, :, cols]
        delta = jnp.sum(found * score_grad, axis=0, keepdims=True)
        diff = (found * (score_grad - delta)).astype(bf16)
        value = jnp.dot(found.astype(bf16), a_n[head, cols, :], preferred_element_type=f32)
        key = jnp.dot(diff, q_n[head, cols, :], preferred_element_type=f32)
        query = jnp.dot(k_t[span(head), :], diff, preferred_element_type=f32)
        q_t[span(head), cols] = (query * scale).astype(bf16)
        return key, value

    def finish(head, key, value):
        for first in range(0, rows, frames):
            at = slice(first, first + frames)
            k_t[span(head), at] = (key[at, :] * scale).astype(bf16).T
            v_t[span(head), at] = value[at, :].astype(bf16).T

    for head in range(heads):
        if blocks == 1:
            finish(head, *backward(0, head))
        else:
            zeros = jnp.zeros((rows, depth), f32)

            def step(index, carry, head=head):
                key, value = backward(index, head)
                return carry[0] + key, carry[1] + value

            finish(head, *lax.fori_loop(0, blocks, step, (zeros, zeros)))

    for distance, out in enumerate(outs):
        at = pl.ds(pl.multiple_of((rank ^ distance) * frames, 128), frames)
        out[0] = q_t[:, at]
        out[1] = k_t[:, at]
        out[2] = v_t[:, at]


def core(scalars, weight, bias, pieces):
    count = len(pieces)
    _, high, frames = pieces[0].shape
    heads, _, depth = weight.shape
    rows = count * frames
    block = math.gcd(rows, 512)
    tall = rows + 2 * PAD + 8
    piece = jax.ShapeDtypeStruct((3, high, frames), bf16)
    turned = pltpu.VMEM((high, rows), bf16)
    plain = pltpu.VMEM((heads, rows, depth), bf16)
    outs = pl.pallas_call(
        functools.partial(core_kernel, count, block),
        out_shape=(piece,) * count + (jax.ShapeDtypeStruct((heads, KERNEL + 1, depth), f32),),
        in_specs=[SMEM] + [VMEM] * (2 + count),
        out_specs=(VMEM,) * (count + 1),
        scratch_shapes=[turned] * 4
        + [plain] * 5
        + [
            pltpu.VMEM((heads, rows, rows), f32),
            pltpu.VMEM((8, tall // 8 - 1, 8, depth), f32),
            pltpu.VMEM((tall, depth), f32),
        ],
        compiler_params=pltpu.CompilerParams(
            vmem_limit_bytes=12 * 2**20 + 8 * heads * rows * rows + 4096 * tall
        ),
        cost_estimate=pl.CostEstimate(
            flops=24 * rows * rows * high,
            bytes_accessed=14 * rows * high,
            transcendentals=heads * rows * rows,
        ),
    )(scalars, weight, bias, *pieces)
    return outs[:count], outs[count]


def exchanged(pieces, before):
    pieces = list(pieces)
    if before is not None and len(pieces) > 2:
        pieces[2:], after = lax.optimization_barrier((pieces[2:], before[1:]))
        before[1:] = after
    moved = [pieces[0]]
    for distance in range(1, len(pieces)):
        pairs = [(i, i ^ distance) for i in range(len(pieces))]
        moved.append(lax.ppermute(pieces[distance], "seq", pairs))
    return moved


def on_device(queries, keys, values, grad_out, conv_weight, conv_bias, lengths):
    count = lax.axis_size("seq")
    rank = lax.axis_index("seq").astype(jnp.int32)
    width = queries.shape[2]
    depth = width // HEADS
    heads = HEADS // count
    chunks = math.gcd(heads, 2)
    step = heads // chunks
    by_head = conv_weight.reshape(KERNEL, HEADS, depth).transpose(1, 0, 2)
    weight = lax.dynamic_slice_in_dim(by_head, rank * heads, heads, axis=0)
    bias = lax.dynamic_slice_in_dim(conv_bias.reshape(HEADS, 1, depth), rank * heads, heads, axis=0)
    scalars = jnp.stack([lengths[0], rank])
    sent = pack(rank[None], (queries, keys, values, grad_out), count, chunks)
    order = []
    for pieces in sent:
        order.append(exchanged(pieces, order[-1] if order else None))
    taps = []
    for chunk in range(chunks):
        at = slice(chunk * step, (chunk + 1) * step)
        grads, part = core(scalars, weight[at], bias[at], order[chunk])
        order.append(exchanged(grads, order[-1]))
        taps.append(part)
    returned = order[chunks:]
    taps, returned[0] = lax.optimization_barrier((jnp.concatenate(taps, axis=0), returned[0]))
    taps = lax.all_gather(taps, "dp")
    return unpack(rank[None], taps, returned, count, chunks)


def solution(mesh):
    return jax.shard_map(
        on_device,
        mesh=mesh,
        in_specs=(
            P("dp", "seq", None),
            P("dp", "seq", None),
            P("dp", "seq", None),
            P("dp", "seq", None),
            P(),
            P(),
            P("dp"),
        ),
        out_specs=(
            P("dp", "seq", None),
            P("dp", "seq", None),
            P("dp", "seq", None),
            P(None, "seq"),
            P("seq"),
        ),
        check_vma=False,
    )
```

```python
import functools
import math

import jax
import jax.numpy as jnp
from jax import lax
from jax.experimental import pallas as pl
from jax.experimental.pallas import tpu as pltpu
from jax.sharding import PartitionSpec as P

HEADS = 16
KERNEL = 31
PAD = 16
CUTS = 4
masked_score = -1e30
VMEM = pl.BlockSpec(memory_space=pltpu.VMEM)
SMEM = pl.BlockSpec(memory_space=pltpu.SMEM)
LIMIT = 16 * 1024 * 1024
bf16, f32 = jnp.bfloat16, jnp.float32


def pack_kernel(count, chunks, rank_ref, *refs):
    arrays, outs, (plain, turned, sems) = refs[:4], refs[4:-3], refs[-3:]
    rank = rank_ref[0]
    high = outs[0].shape[1]
    share = high * chunks
    frames = plain.shape[1]
    cut = frames // CUTS

    def copy(which, part):
        at = pl.ds(part * cut, cut)
        return pltpu.make_async_copy(
            arrays[which].at[0, at, :], plain.at[which, at, :], sems.at[which, part]
        )

    for which in range(4):
        for part in range(CUTS):
            copy(which, part).start()
    for which in range(4):
        for part in range(CUTS):
            copy(which, part).wait()
        turned[which] = plain[which].T
        for distance in range(count):
            for chunk in range(chunks):
                first = pl.multiple_of((rank ^ distance) * share + chunk * high, 16)
                outs[chunk * count + distance][which] = turned[which, pl.ds(first, high), :]


def pack(rank, arrays, count, chunks):
    _, frames, width = arrays[0].shape
    high = width // count // chunks
    piece = jax.ShapeDtypeStruct((4, high, frames), bf16)
    outs = pl.pallas_call(
        functools.partial(pack_kernel, count, chunks),
        out_shape=(piece,) * (count * chunks),
        in_specs=[SMEM] + [pl.BlockSpec(memory_space=pltpu.HBM)] * 4,
        out_specs=(VMEM,) * (count * chunks),
        scratch_shapes=[
            pltpu.VMEM((4, frames, width), bf16),
            pltpu.VMEM((4, width, frames), bf16),
            pltpu.SemaphoreType.DMA((4, CUTS)),
        ],
        compiler_params=pltpu.CompilerParams(vmem_limit_bytes=LIMIT),
        cost_estimate=pl.CostEstimate(
            flops=0, bytes_accessed=16 * frames * width, transcendentals=0
        ),
    )(rank, *[pltpu.with_memory_space_constraint(array, pltpu.HBM) for array in arrays])
    return [outs[chunk * count : (chunk + 1) * count] for chunk in range(chunks)]


def unpack_kernel(count, chunks, rank_ref, *refs):
    pieces, refs = refs[: count * chunks], refs[count * chunks :]
    taps_refs, outs = refs[:-9], refs[-9:-6]
    weight_ref, bias_ref, bias_row, turned, plain, sems = refs[-6:]
    rank = rank_ref[0]
    high = pieces[0].shape[1]
    share = high * chunks
    frames = plain.shape[1]
    cut = frames // CUTS
    copies = []
    for which, out in enumerate(outs):
        for distance in range(count):
            for chunk in range(chunks):
                first = pl.multiple_of((rank ^ distance) * share + chunk * high, 16)
                turned[which, pl.ds(first, high), :] = pieces[chunk * count + distance][which]
        plain[which] = turned[which].T
        for part in range(CUTS):
            at = pl.ds(part * cut, cut)
            copies.append(
                pltpu.make_async_copy(
                    plain.at[which, at, :], out.at[0, at, :], sems.at[which, part]
                )
            )
            copies[-1].start()
    taps = tree_sum([ref[...] for ref in taps_refs])
    heads, _, depth = taps.shape
    for head in range(heads):
        at = slice(head * depth, (head + 1) * depth)
        weight_ref[:, at] = taps[head, :KERNEL]
        bias_row[:, at] = taps[head, KERNEL:]
    bias_ref[...] = bias_row[0]
    for copy in copies:
        copy.wait()


def unpack(rank, taps, pieces, count, chunks):
    _, high, frames = pieces[0][0].shape
    width = high * count * chunks
    whole = jax.ShapeDtypeStruct((1, frames, width), bf16)
    return pl.pallas_call(
        functools.partial(unpack_kernel, count, chunks),
        out_shape=(whole,) * 3
        + (
            jax.ShapeDtypeStruct((KERNEL, width // count), f32),
            jax.ShapeDtypeStruct((width // count,), f32),
        ),
        in_specs=[SMEM] + [VMEM] * (count * chunks + len(taps)),
        out_specs=(pl.BlockSpec(memory_space=pltpu.HBM),) * 3 + (VMEM,) * 2,
        scratch_shapes=[
            pltpu.VMEM((1, width // count), f32),
            pltpu.VMEM((3, width, frames), bf16),
            pltpu.VMEM((3, frames, width), bf16),
            pltpu.SemaphoreType.DMA((3, CUTS)),
        ],
        compiler_params=pltpu.CompilerParams(vmem_limit_bytes=LIMIT),
        cost_estimate=pl.CostEstimate(
            flops=0, bytes_accessed=12 * frames * width, transcendentals=0
        ),
    )(rank, *[piece for part in pieces for piece in part], *taps)


def core_kernel(count, block, scalars, weight_ref, bias_ref, *refs):
    pieces, outs, taps_ref = refs[:count], refs[count : 2 * count], refs[2 * count]
    q_t, k_t, v_t, a_t, q_n, k_n, v_n, g_n, a_n, probs, shifted, padded = refs[2 * count + 1 :]
    heads, rows, depth = q_n.shape
    frames = pieces[0].shape[2]
    blocks = rows // block
    scale = 1.0 / math.sqrt(depth)
    log_scale = scale * math.log2(math.e)
    length, rank = scalars[0], scalars[1]

    def span(head):
        return slice(head * depth, (head + 1) * depth)

    for distance, piece in enumerate(pieces):
        at = pl.ds(pl.multiple_of((rank ^ distance) * frames, 128), frames)
        q_t[:, at] = piece[0]
        k_t[:, at] = piece[1]
        v_t[:, at] = piece[2]
        for head in range(heads):
            q_n[head, at, :] = piece[0, span(head), :].T
            k_n[head, at, :] = piece[1, span(head), :].T
            v_n[head, at, :] = piece[2, span(head), :].T
            g_n[head, at, :] = piece[3, span(head), :].T

    def forward(index, head):
        cols = pl.ds(pl.multiple_of(index * block, block), block)
        scores = jnp.dot(k_n[head], q_t[span(head), cols], preferred_element_type=f32)
        key_at = lax.broadcasted_iota(jnp.int32, scores.shape, 0)
        scores = jnp.where(key_at < length, scores, masked_score)
        exped = jnp.exp2((scores - jnp.max(scores, axis=0, keepdims=True)) * log_scale)
        found = exped * (1.0 / jnp.sum(exped, axis=0, keepdims=True))
        probs[head, :, cols] = found
        out = jnp.dot(v_t[span(head), :], found.astype(bf16), preferred_element_type=f32)
        frame_at = index * block + lax.broadcasted_iota(jnp.int32, out.shape, 1)
        a_t[span(head), cols] = jnp.where(frame_at < length, out, 0.0).astype(bf16)

    def each_block(body):
        if blocks == 1:
            for head in range(heads):
                body(0, head)
        else:

            def step(index, carry):
                for head in range(heads):
                    body(index, head)
                return carry

            lax.fori_loop(0, blocks, step, 0)

    each_block(forward)

    tall = padded.shape[0]
    padded[0:PAD, :] = jnp.zeros((PAD, depth), f32)
    padded[PAD + rows : tall, :] = jnp.zeros((tall - PAD - rows, depth), f32)

    def shift_all():
        for s in range(8):
            shifted[s] = padded[s : s + tall - 8, :].reshape(tall // 8 - 1, 8, depth)

    step_tiles = 8
    step_rows = 8 * step_tiles

    def window(index, offset):
        return shifted[offset % 8, pl.ds(index * step_tiles + offset // 8, step_tiles)]

    def filtered(head, index, reverse):
        total = None
        for offset in range(1, KERNEL + 1):
            tap = KERNEL - offset if reverse else offset - 1
            term = weight_ref[head, tap : tap + 1, :] * window(index, offset)
            total = term if total is None else total + term
        return total

    def loaded(ref, index):
        at = pl.ds(pl.multiple_of(index * step_rows, step_rows), step_rows)
        return ref[at, :].astype(f32).reshape(step_tiles, 8, depth)

    for head in range(heads):
        for first in range(0, rows, frames):
            at = slice(PAD + first, PAD + first + frames)
            padded[at, :] = a_t[span(head), first : first + frames].T.astype(f32)
        shift_all()

        def conv_step(index, carry, head=head):
            conv_pre = filtered(head, index, False) + bias_ref[head]
            sig = 1.0 / (1.0 + jnp.exp(-conv_pre))
            pre = loaded(g_n.at[head], index) * (sig * (1.0 + conv_pre * (1.0 - sig)))
            pre = pre.astype(bf16).astype(f32)
            at = pl.ds(pl.multiple_of(PAD + index * step_rows, PAD), step_rows)
            padded[at, :] = pre.reshape(step_rows, depth)
            new = []
            for offset in range(1, KERNEL + 1):
                new.append(carry[offset - 1] + jnp.sum(pre * window(index, offset), axis=0))
            new.append(carry[KERNEL] + jnp.sum(pre, axis=0))
            return tuple(new)

        zero = jnp.zeros((8, depth), f32)
        sums = lax.fori_loop(0, rows // step_rows, conv_step, (zero,) * (KERNEL + 1))
        for tap in range(KERNEL + 1):
            taps_ref[head, tap : tap + 1, :] = jnp.sum(sums[tap], axis=0, keepdims=True)
        shift_all()

        def back_step(index, carry, head=head):
            total = loaded(g_n.at[head], index) + filtered(head, index, True)
            total = total.reshape(step_rows, depth)
            frame_at = index * step_rows + lax.broadcasted_iota(jnp.int32, total.shape, 0)
            total = jnp.where(frame_at < length, total, 0.0)
            at = pl.ds(pl.multiple_of(index * step_rows, step_rows), step_rows)
            a_n[head, at, :] = total.astype(bf16)
            return carry

        lax.fori_loop(0, rows // step_rows, back_step, 0)
        for first in range(0, rows, frames):
            a_t[span(head), first : first + frames] = a_n[head, first : first + frames, :].T

    def backward(index, head):
        cols = pl.ds(pl.multiple_of(index * block, block), block)
        score_grad = jnp.dot(v_n[head], a_t[span(head), cols], preferred_element_type=f32)
        found = probs[head, :, cols]
        delta = jnp.sum(found * score_grad, axis=0, keepdims=True)
        diff = (found * (score_grad - delta)).astype(bf16)
        value = jnp.dot(found.astype(bf16), a_n[head, cols, :], preferred_element_type=f32)
        key = jnp.dot(diff, q_n[head, cols, :], preferred_element_type=f32)
        query = jnp.dot(k_t[span(head), :], diff, preferred_element_type=f32)
        q_t[span(head), cols] = (query * scale).astype(bf16)
        return key, value

    def finish(head, key, value):
        for first in range(0, rows, frames):
            at = slice(first, first + frames)
            k_t[span(head), at] = (key[at, :] * scale).astype(bf16).T
            v_t[span(head), at] = value[at, :].astype(bf16).T

    for head in range(heads):
        if blocks == 1:
            finish(head, *backward(0, head))
        else:
            zeros = jnp.zeros((rows, depth), f32)

            def step(index, carry, head=head):
                key, value = backward(index, head)
                return carry[0] + key, carry[1] + value

            finish(head, *lax.fori_loop(0, blocks, step, (zeros, zeros)))

    for distance, out in enumerate(outs):
        at = pl.ds(pl.multiple_of((rank ^ distance) * frames, 128), frames)
        out[0] = q_t[:, at]
        out[1] = k_t[:, at]
        out[2] = v_t[:, at]


def core(scalars, weight, bias, pieces):
    count = len(pieces)
    _, high, frames = pieces[0].shape
    heads, _, depth = weight.shape
    rows = count * frames
    block = math.gcd(rows, 512)
    tall = rows + 2 * PAD + 8
    piece = jax.ShapeDtypeStruct((3, high, frames), bf16)
    turned = pltpu.VMEM((high, rows), bf16)
    plain = pltpu.VMEM((heads, rows, depth), bf16)
    outs = pl.pallas_call(
        functools.partial(core_kernel, count, block),
        out_shape=(piece,) * count + (jax.ShapeDtypeStruct((heads, KERNEL + 1, depth), f32),),
        in_specs=[SMEM] + [VMEM] * (2 + count),
        out_specs=(VMEM,) * (count + 1),
        scratch_shapes=[turned] * 4
        + [plain] * 5
        + [
            pltpu.VMEM((heads, rows, rows), f32),
            pltpu.VMEM((8, tall // 8 - 1, 8, depth), f32),
            pltpu.VMEM((tall, depth), f32),
        ],
        compiler_params=pltpu.CompilerParams(
            vmem_limit_bytes=12 * 2**20 + 8 * heads * rows * rows + 4096 * tall
        ),
        cost_estimate=pl.CostEstimate(
            flops=24 * rows * rows * high,
            bytes_accessed=14 * rows * high,
            transcendentals=heads * rows * rows,
        ),
    )(scalars, weight, bias, *pieces)
    return outs[:count], outs[count]


def exchanged(pieces, before):
    pieces = list(pieces)
    if before is not None and len(pieces) > 2:
        pieces[2:], after = lax.optimization_barrier((pieces[2:], before[1:]))
        before[1:] = after
    moved = pieces[:1] * len(pieces)
    for distance in range(len(pieces) - 1, 0, -1):
        pairs = [(i, i ^ distance) for i in range(len(pieces))]
        moved[distance] = lax.ppermute(pieces[distance], "seq", pairs)
    return moved


def terms(array, axis, stride, reach):
    count = lax.axis_size(axis)
    found = [array]
    for distance in range(stride, reach, stride):
        pairs = [(i, i ^ distance) for i in range(count)]
        found.append(lax.ppermute(array, axis, pairs))
    return found


def tree_sum(found):
    while len(found) > 1:
        found = [a + b for a, b in zip(found[::2], found[1::2])]
    return found[0]


def on_device(queries, keys, values, grad_out, conv_weight, conv_bias, lengths):
    count = lax.axis_size("seq")
    rank = lax.axis_index("seq").astype(jnp.int32)
    width = queries.shape[2]
    depth = width // HEADS
    heads = HEADS // count
    chunks = math.gcd(heads, 2)
    step = heads // chunks
    by_head = conv_weight.reshape(KERNEL, HEADS, depth).transpose(1, 0, 2)
    weight = lax.dynamic_slice_in_dim(by_head, rank * heads, heads, axis=0)
    bias = lax.dynamic_slice_in_dim(conv_bias.reshape(HEADS, 1, depth), rank * heads, heads, axis=0)
    scalars = jnp.stack([lengths[0], rank])
    sent = pack(rank[None], (queries, keys, values, grad_out), count, chunks)
    order = []
    for pieces in sent:
        order.append(exchanged(pieces, order[-1] if order else None))
    taps = []
    for chunk in range(chunks):
        at = slice(chunk * step, (chunk + 1) * step)
        grads, part = core(scalars, weight[at], bias[at], order[chunk])
        order.append(exchanged(grads, order[-1]))
        taps.append(part)
    returned = order[chunks:]
    taps, returned[0] = lax.optimization_barrier((jnp.concatenate(taps, axis=0), returned[0]))
    taps = tree_sum(terms(taps, "dp", 1, 2))
    return unpack(rank[None], terms(taps, "dp", 2, lax.axis_size("dp")), returned, count, chunks)


def solution(mesh):
    return jax.shard_map(
        on_device,
        mesh=mesh,
        in_specs=(
            P("dp", "seq", None),
            P("dp", "seq", None),
            P("dp", "seq", None),
            P("dp", "seq", None),
            P(),
            P(),
            P("dp"),
        ),
        out_specs=(
            P("dp", "seq", None),
            P("dp", "seq", None),
            P("dp", "seq", None),
            P(None, "seq"),
            P("seq"),
        ),
        check_vma=False,
    )
```

```python
import functools
import math

import jax
import jax.numpy as jnp
from jax import lax
from jax.experimental import pallas as pl
from jax.experimental.pallas import tpu as pltpu
from jax.sharding import PartitionSpec as P

HEADS = 16
KERNEL = 31
PAD = 16
masked_score = -1e30
VMEM = pl.BlockSpec(memory_space=pltpu.VMEM)
SMEM = pl.BlockSpec(memory_space=pltpu.SMEM)
LIMIT = 16 * 1024 * 1024
bf16, f32 = jnp.bfloat16, jnp.float32


def pack_kernel(count, chunks, rank_ref, *refs):
    arrays, outs, turned = refs[:4], refs[4:-1], refs[-1]
    rank = rank_ref[0]
    high = outs[0].shape[1]
    share = high * chunks
    for which, array in enumerate(arrays):
        turned[which] = array[0].T
        for distance in range(count):
            for chunk in range(chunks):
                first = pl.multiple_of((rank ^ distance) * share + chunk * high, 16)
                outs[chunk * count + distance][which] = turned[which, pl.ds(first, high), :]


def pack(rank, arrays, count, chunks):
    _, frames, width = arrays[0].shape
    high = width // count // chunks
    piece = jax.ShapeDtypeStruct((4, high, frames), bf16)
    outs = pl.pallas_call(
        functools.partial(pack_kernel, count, chunks),
        out_shape=(piece,) * (count * chunks),
        in_specs=[SMEM] + [VMEM] * 4,
        out_specs=(VMEM,) * (count * chunks),
        scratch_shapes=[pltpu.VMEM((4, width, frames), bf16)],
        compiler_params=pltpu.CompilerParams(vmem_limit_bytes=LIMIT),
        cost_estimate=pl.CostEstimate(
            flops=0, bytes_accessed=16 * frames * width, transcendentals=0
        ),
    )(rank, *[pltpu.with_memory_space_constraint(array, pltpu.HBM) for array in arrays])
    return [outs[chunk * count : (chunk + 1) * count] for chunk in range(chunks)]


def taken(count):
    return [0] + list(range(count - 1, 0, -1))


def unpack_kernel(count, chunks, rank_ref, *refs):
    pieces, refs = refs[: count * chunks], refs[count * chunks :]
    taps_refs, outs = refs[:-7], refs[-7:-4]
    weight_ref, bias_ref, bias_row, turned = refs[-4:]
    rank = rank_ref[0]
    high = pieces[0].shape[1]
    share = high * chunks
    for which, out in enumerate(outs):
        for chunk in range(chunks):
            for place, distance in enumerate(taken(count)):
                first = pl.multiple_of((rank ^ distance) * share + chunk * high, 16)
                turned[which, pl.ds(first, high), :] = pieces[chunk * count + place][which]
        out[0] = turned[which].T
    taps = tree_sum([ref[...] for ref in taps_refs])
    heads, _, depth = taps.shape
    for head in range(heads):
        at = slice(head * depth, (head + 1) * depth)
        weight_ref[:, at] = taps[head, :KERNEL]
        bias_row[:, at] = taps[head, KERNEL:]
    bias_ref[...] = bias_row[0]


def unpack(rank, taps, pieces, count, chunks):
    _, high, frames = pieces[0][0].shape
    width = high * count * chunks
    whole = jax.ShapeDtypeStruct((1, frames, width), bf16)
    return pl.pallas_call(
        functools.partial(unpack_kernel, count, chunks),
        out_shape=(whole,) * 3
        + (
            jax.ShapeDtypeStruct((KERNEL, width // count), f32),
            jax.ShapeDtypeStruct((width // count,), f32),
        ),
        in_specs=[SMEM] + [VMEM] * (count * chunks + len(taps)),
        out_specs=(VMEM,) * 5,
        scratch_shapes=[
            pltpu.VMEM((1, width // count), f32),
            pltpu.VMEM((3, width, frames), bf16),
        ],
        compiler_params=pltpu.CompilerParams(vmem_limit_bytes=LIMIT),
        cost_estimate=pl.CostEstimate(
            flops=0, bytes_accessed=12 * frames * width, transcendentals=0
        ),
    )(rank, *[part[distance] for part in pieces for distance in taken(count)], *taps)


def core_kernel(count, block, scalars, weight_ref, bias_ref, *refs):
    pieces, outs, taps_ref = refs[:count], refs[count : 2 * count], refs[2 * count]
    q_t, k_t, v_t, a_t, q_n, k_n, v_n, g_n, a_n, probs, shifted, padded = refs[2 * count + 1 :]
    heads, rows, depth = q_n.shape
    frames = pieces[0].shape[2]
    blocks = rows // block
    scale = 1.0 / math.sqrt(depth)
    log_scale = scale * math.log2(math.e)
    length, rank = scalars[0], scalars[1]

    def span(head):
        return slice(head * depth, (head + 1) * depth)

    for distance, piece in zip(taken(count), pieces):
        at = pl.ds(pl.multiple_of((rank ^ distance) * frames, 128), frames)
        q_t[:, at] = piece[0]
        k_t[:, at] = piece[1]
        v_t[:, at] = piece[2]
        for head in range(heads):
            q_n[head, at, :] = piece[0, span(head), :].T
            k_n[head, at, :] = piece[1, span(head), :].T
            v_n[head, at, :] = piece[2, span(head), :].T
            g_n[head, at, :] = piece[3, span(head), :].T

    def forward(index, head):
        cols = pl.ds(pl.multiple_of(index * block, block), block)
        scores = jnp.dot(k_n[head], q_t[span(head), cols], preferred_element_type=f32)
        key_at = lax.broadcasted_iota(jnp.int32, scores.shape, 0)
        scores = jnp.where(key_at < length, scores, masked_score)
        exped = jnp.exp2((scores - jnp.max(scores, axis=0, keepdims=True)) * log_scale)
        found = exped * (1.0 / jnp.sum(exped, axis=0, keepdims=True))
        probs[head, :, cols] = found
        out = jnp.dot(v_t[span(head), :], found.astype(bf16), preferred_element_type=f32)
        frame_at = index * block + lax.broadcasted_iota(jnp.int32, out.shape, 1)
        a_t[span(head), cols] = jnp.where(frame_at < length, out, 0.0).astype(bf16)

    def each_block(body):
        if blocks == 1:
            for head in range(heads):
                body(0, head)
        else:

            def step(index, carry):
                for head in range(heads):
                    body(index, head)
                return carry

            lax.fori_loop(0, blocks, step, 0)

    each_block(forward)

    tall = padded.shape[0]
    padded[0:PAD, :] = jnp.zeros((PAD, depth), f32)
    padded[PAD + rows : tall, :] = jnp.zeros((tall - PAD - rows, depth), f32)

    def shift_all():
        for s in range(8):
            shifted[s] = padded[s : s + tall - 8, :].reshape(tall // 8 - 1, 8, depth)

    step_tiles = 8
    step_rows = 8 * step_tiles

    def window(index, offset):
        return shifted[offset % 8, pl.ds(index * step_tiles + offset // 8, step_tiles)]

    def filtered(head, index, reverse):
        total = None
        for offset in range(1, KERNEL + 1):
            tap = KERNEL - offset if reverse else offset - 1
            term = weight_ref[head, tap : tap + 1, :] * window(index, offset)
            total = term if total is None else total + term
        return total

    def loaded(ref, index):
        at = pl.ds(pl.multiple_of(index * step_rows, step_rows), step_rows)
        return ref[at, :].astype(f32).reshape(step_tiles, 8, depth)

    for head in range(heads):
        for first in range(0, rows, frames):
            at = slice(PAD + first, PAD + first + frames)
            padded[at, :] = a_t[span(head), first : first + frames].T.astype(f32)
        shift_all()

        def conv_step(index, carry, head=head):
            conv_pre = filtered(head, index, False) + bias_ref[head]
            sig = 1.0 / (1.0 + jnp.exp(-conv_pre))
            pre = loaded(g_n.at[head], index) * (sig * (1.0 + conv_pre * (1.0 - sig)))
            pre = pre.astype(bf16).astype(f32)
            at = pl.ds(pl.multiple_of(PAD + index * step_rows, PAD), step_rows)
            padded[at, :] = pre.reshape(step_rows, depth)
            new = []
            for offset in range(1, KERNEL + 1):
                new.append(carry[offset - 1] + jnp.sum(pre * window(index, offset), axis=0))
            new.append(carry[KERNEL] + jnp.sum(pre, axis=0))
            return tuple(new)

        zero = jnp.zeros((8, depth), f32)
        sums = lax.fori_loop(0, rows // step_rows, conv_step, (zero,) * (KERNEL + 1))
        for tap in range(KERNEL + 1):
            taps_ref[head, tap : tap + 1, :] = jnp.sum(sums[tap], axis=0, keepdims=True)
        shift_all()

        def back_step(index, carry, head=head):
            total = loaded(g_n.at[head], index) + filtered(head, index, True)
            total = total.reshape(step_rows, depth)
            frame_at = index * step_rows + lax.broadcasted_iota(jnp.int32, total.shape, 0)
            total = jnp.where(frame_at < length, total, 0.0)
            at = pl.ds(pl.multiple_of(index * step_rows, step_rows), step_rows)
            a_n[head, at, :] = total.astype(bf16)
            return carry

        lax.fori_loop(0, rows // step_rows, back_step, 0)
        for first in range(0, rows, frames):
            a_t[span(head), first : first + frames] = a_n[head, first : first + frames, :].T

    def backward(index, head):
        cols = pl.ds(pl.multiple_of(index * block, block), block)
        score_grad = jnp.dot(v_n[head], a_t[span(head), cols], preferred_element_type=f32)
        found = probs[head, :, cols]
        delta = jnp.sum(found * score_grad, axis=0, keepdims=True)
        diff = (found * (score_grad - delta)).astype(bf16)
        value = jnp.dot(found.astype(bf16), a_n[head, cols, :], preferred_element_type=f32)
        key = jnp.dot(diff, q_n[head, cols, :], preferred_element_type=f32)
        query = jnp.dot(k_t[span(head), :], diff, preferred_element_type=f32)
        q_t[span(head), cols] = (query * scale).astype(bf16)
        return key, value

    def finish(head, key, value):
        for first in range(0, rows, frames):
            at = slice(first, first + frames)
            k_t[span(head), at] = (key[at, :] * scale).astype(bf16).T
            v_t[span(head), at] = value[at, :].astype(bf16).T

    for head in range(heads):
        if blocks == 1:
            finish(head, *backward(0, head))
        else:
            zeros = jnp.zeros((rows, depth), f32)

            def step(index, carry, head=head):
                key, value = backward(index, head)
                return carry[0] + key, carry[1] + value

            finish(head, *lax.fori_loop(0, blocks, step, (zeros, zeros)))

    for distance, out in enumerate(outs):
        at = pl.ds(pl.multiple_of((rank ^ distance) * frames, 128), frames)
        out[0] = q_t[:, at]
        out[1] = k_t[:, at]
        out[2] = v_t[:, at]


def core(scalars, weight, bias, pieces):
    count = len(pieces)
    _, high, frames = pieces[0].shape
    heads, _, depth = weight.shape
    rows = count * frames
    block = math.gcd(rows, 512)
    tall = rows + 2 * PAD + 8
    piece = jax.ShapeDtypeStruct((3, high, frames), bf16)
    turned = pltpu.VMEM((high, rows), bf16)
    plain = pltpu.VMEM((heads, rows, depth), bf16)
    outs = pl.pallas_call(
        functools.partial(core_kernel, count, block),
        out_shape=(piece,) * count + (jax.ShapeDtypeStruct((heads, KERNEL + 1, depth), f32),),
        in_specs=[SMEM] + [VMEM] * (2 + count),
        out_specs=(VMEM,) * (count + 1),
        scratch_shapes=[turned] * 4
        + [plain] * 5
        + [
            pltpu.VMEM((heads, rows, rows), f32),
            pltpu.VMEM((8, tall // 8 - 1, 8, depth), f32),
            pltpu.VMEM((tall, depth), f32),
        ],
        compiler_params=pltpu.CompilerParams(
            vmem_limit_bytes=12 * 2**20 + 8 * heads * rows * rows + 4096 * tall
        ),
        cost_estimate=pl.CostEstimate(
            flops=24 * rows * rows * high,
            bytes_accessed=14 * rows * high,
            transcendentals=heads * rows * rows,
        ),
    )(scalars, weight, bias, *[pieces[distance] for distance in taken(count)])
    return outs[:count], outs[count]


def exchanged(pieces, before):
    pieces = list(pieces)
    if before is not None and len(pieces) > 2:
        pieces[:1:-1], before[:0:-1] = lax.optimization_barrier((pieces[:1:-1], before[:0:-1]))
    moved = pieces[:1] * len(pieces)
    for distance in range(len(pieces) - 1, 0, -1):
        pairs = [(i, i ^ distance) for i in range(len(pieces))]
        moved[distance] = lax.ppermute(pieces[distance], "seq", pairs)
    return moved


def terms(array, axis, stride, reach):
    count = lax.axis_size(axis)
    found = [array]
    for distance in range(stride, reach, stride):
        pairs = [(i, i ^ distance) for i in range(count)]
        found.append(lax.ppermute(array, axis, pairs))
    return found


def tree_sum(found):
    while len(found) > 1:
        found = [a + b for a, b in zip(found[::2], found[1::2])]
    return found[0]


def on_device(queries, keys, values, grad_out, conv_weight, conv_bias, lengths):
    count = lax.axis_size("seq")
    rank = lax.axis_index("seq").astype(jnp.int32)
    width = queries.shape[2]
    depth = width // HEADS
    heads = HEADS // count
    chunks = math.gcd(heads, 2)
    step = heads // chunks
    by_head = conv_weight.reshape(KERNEL, HEADS, depth).transpose(1, 0, 2)
    weight = lax.dynamic_slice_in_dim(by_head, rank * heads, heads, axis=0)
    bias = lax.dynamic_slice_in_dim(conv_bias.reshape(HEADS, 1, depth), rank * heads, heads, axis=0)
    scalars = jnp.stack([lengths[0], rank])
    sent = pack(rank[None], (queries, keys, values, grad_out), count, chunks)
    order = []
    for pieces in sent:
        order.append(exchanged(pieces, order[-1] if order else None))
    taps = []
    for chunk in range(chunks):
        at = slice(chunk * step, (chunk + 1) * step)
        grads, part = core(scalars, weight[at], bias[at], order[chunk])
        order.append(exchanged(grads, order[-1]))
        taps.append(part)
    returned = order[chunks:]
    taps, returned[0] = lax.optimization_barrier((jnp.concatenate(taps, axis=0), returned[0]))
    taps = tree_sum(terms(taps, "dp", 1, 2))
    return unpack(rank[None], terms(taps, "dp", 2, lax.axis_size("dp")), returned, count, chunks)


def solution(mesh):
    return jax.shard_map(
        on_device,
        mesh=mesh,
        in_specs=(
            P("dp", "seq", None),
            P("dp", "seq", None),
            P("dp", "seq", None),
            P("dp", "seq", None),
            P(),
            P(),
            P("dp"),
        ),
        out_specs=(
            P("dp", "seq", None),
            P("dp", "seq", None),
            P("dp", "seq", None),
            P(None, "seq"),
            P("seq"),
        ),
        check_vma=False,
    )
```

```python
import functools
import math

import jax
import jax.numpy as jnp
from jax import lax
from jax.experimental import pallas as pl
from jax.experimental.pallas import tpu as pltpu
from jax.sharding import PartitionSpec as P

HEADS = 16
KERNEL = 31
PAD = 16
masked_score = -1e30
VMEM = pl.BlockSpec(memory_space=pltpu.VMEM)
SMEM = pl.BlockSpec(memory_space=pltpu.SMEM)
LIMIT = 16 * 1024 * 1024
bf16, f32 = jnp.bfloat16, jnp.float32


def pack_kernel(count, chunks, rank_ref, *refs):
    arrays, outs, turned = refs[:4], refs[4:-1], refs[-1]
    rank = rank_ref[0]
    high = outs[0].shape[1]
    share = high * chunks
    for which, array in enumerate(arrays):
        turned[which] = array[0].T
        for distance in range(count):
            for chunk in range(chunks):
                first = pl.multiple_of((rank ^ distance) * share + chunk * high, 16)
                outs[chunk * count + distance][which] = turned[which, pl.ds(first, high), :]


def pack(rank, arrays, count, chunks):
    _, frames, width = arrays[0].shape
    high = width // count // chunks
    piece = jax.ShapeDtypeStruct((4, high, frames), bf16)
    outs = pl.pallas_call(
        functools.partial(pack_kernel, count, chunks),
        out_shape=(piece,) * (count * chunks),
        in_specs=[SMEM] + [VMEM] * 4,
        out_specs=(VMEM,) * (count * chunks),
        scratch_shapes=[pltpu.VMEM((4, width, frames), bf16)],
        compiler_params=pltpu.CompilerParams(vmem_limit_bytes=LIMIT),
        cost_estimate=pl.CostEstimate(
            flops=0, bytes_accessed=16 * frames * width, transcendentals=0
        ),
    )(rank, *[pltpu.with_memory_space_constraint(array, pltpu.HBM) for array in arrays])
    return [outs[chunk * count : (chunk + 1) * count] for chunk in range(chunks)]


def taken(count):
    return [0] + list(range(count - 1, 0, -1))


def unpack_kernel(count, chunks, rank_ref, *refs):
    pieces, refs = refs[: count * chunks], refs[count * chunks :]
    taps_refs, outs = refs[:-7], refs[-7:-4]
    weight_ref, bias_ref, bias_row, turned = refs[-4:]
    rank = rank_ref[0]
    high = pieces[0].shape[1]
    share = high * chunks
    for which, out in enumerate(outs):
        for chunk in range(chunks):
            for place, distance in enumerate(taken(count)):
                first = pl.multiple_of((rank ^ distance) * share + chunk * high, 16)
                turned[which, pl.ds(first, high), :] = pieces[chunk * count + place][which]
        out[0] = turned[which].T
    taps = tree_sum([ref[...] for ref in taps_refs])
    heads, _, depth = taps.shape
    for head in range(heads):
        at = slice(head * depth, (head + 1) * depth)
        weight_ref[:, at] = taps[head, :KERNEL]
        bias_row[:, at] = taps[head, KERNEL:]
    bias_ref[...] = bias_row[0]


def unpack(rank, taps, pieces, count, chunks):
    _, high, frames = pieces[0][0].shape
    width = high * count * chunks
    whole = jax.ShapeDtypeStruct((1, frames, width), bf16)
    return pl.pallas_call(
        functools.partial(unpack_kernel, count, chunks),
        out_shape=(whole,) * 3
        + (
            jax.ShapeDtypeStruct((KERNEL, width // count), f32),
            jax.ShapeDtypeStruct((width // count,), f32),
        ),
        in_specs=[SMEM] + [VMEM] * (count * chunks + len(taps)),
        out_specs=(VMEM,) * 5,
        scratch_shapes=[
            pltpu.VMEM((1, width // count), f32),
            pltpu.VMEM((3, width, frames), bf16),
        ],
        compiler_params=pltpu.CompilerParams(vmem_limit_bytes=LIMIT),
        cost_estimate=pl.CostEstimate(
            flops=0, bytes_accessed=12 * frames * width, transcendentals=0
        ),
    )(rank, *[part[distance] for part in pieces for distance in taken(count)], *taps)


def core_kernel(count, block, scalars, weight_ref, bias_ref, *refs):
    pieces, outs, taps_ref = refs[:count], refs[count : 2 * count], refs[2 * count]
    q_t, k_t, v_t, a_t, q_n, k_n, v_n, g_n, a_n, probs, shifted, padded = refs[2 * count + 1 :]
    heads, rows, depth = q_n.shape
    frames = pieces[0].shape[2]
    blocks = rows // block
    scale = 1.0 / math.sqrt(depth)
    log_scale = scale * math.log2(math.e)
    length, rank = scalars[0], scalars[1]

    def span(head):
        return slice(head * depth, (head + 1) * depth)

    for distance, piece in zip(taken(count), pieces):
        at = pl.ds(pl.multiple_of((rank ^ distance) * frames, 128), frames)
        q_t[:, at] = piece[0]
        k_t[:, at] = piece[1]
        v_t[:, at] = piece[2]
        for head in range(heads):
            q_n[head, at, :] = piece[0, span(head), :].T
            k_n[head, at, :] = piece[1, span(head), :].T
            v_n[head, at, :] = piece[2, span(head), :].T
            g_n[head, at, :] = piece[3, span(head), :].T

    def forward(index, head):
        cols = pl.ds(pl.multiple_of(index * block, block), block)
        scores = jnp.dot(k_n[head], q_t[span(head), cols], preferred_element_type=f32)
        key_at = lax.broadcasted_iota(jnp.int32, scores.shape, 0)
        scores = jnp.where(key_at < length, scores, masked_score)
        exped = jnp.exp2((scores - jnp.max(scores, axis=0, keepdims=True)) * log_scale)
        found = exped * (1.0 / jnp.sum(exped, axis=0, keepdims=True))
        probs[head, :, cols] = found
        out = jnp.dot(v_t[span(head), :], found.astype(bf16), preferred_element_type=f32)
        frame_at = index * block + lax.broadcasted_iota(jnp.int32, out.shape, 1)
        a_t[span(head), cols] = jnp.where(frame_at < length, out, 0.0).astype(bf16)

    def each_block(body):
        if blocks == 1:
            for head in range(heads):
                body(0, head)
        else:

            def step(index, carry):
                for head in range(heads):
                    body(index, head)
                return carry

            lax.fori_loop(0, blocks, step, 0)

    each_block(forward)

    tall = padded.shape[0]
    padded[0:PAD, :] = jnp.zeros((PAD, depth), f32)
    padded[PAD + rows : tall, :] = jnp.zeros((tall - PAD - rows, depth), f32)

    def shift_all():
        for s in range(8):
            shifted[s] = padded[s : s + tall - 8, :].reshape(tall // 8 - 1, 8, depth)

    step_tiles = 8
    step_rows = 8 * step_tiles

    def window(index, offset):
        return shifted[offset % 8, pl.ds(index * step_tiles + offset // 8, step_tiles)]

    def filtered(head, index, reverse):
        total = None
        for offset in range(1, KERNEL + 1):
            tap = KERNEL - offset if reverse else offset - 1
            term = weight_ref[head, tap : tap + 1, :] * window(index, offset)
            total = term if total is None else total + term
        return total

    def loaded(ref, index):
        at = pl.ds(pl.multiple_of(index * step_rows, step_rows), step_rows)
        return ref[at, :].astype(f32).reshape(step_tiles, 8, depth)

    for head in range(heads):
        for first in range(0, rows, frames):
            at = slice(PAD + first, PAD + first + frames)
            padded[at, :] = a_t[span(head), first : first + frames].T.astype(f32)
        shift_all()

        def conv_step(index, carry, head=head):
            conv_pre = filtered(head, index, False) + bias_ref[head]
            sig = 1.0 / (1.0 + jnp.exp(-conv_pre))
            pre = loaded(g_n.at[head], index) * (sig * (1.0 + conv_pre * (1.0 - sig)))
            pre = pre.astype(bf16).astype(f32)
            at = pl.ds(pl.multiple_of(PAD + index * step_rows, PAD), step_rows)
            padded[at, :] = pre.reshape(step_rows, depth)
            new = []
            for offset in range(1, KERNEL + 1):
                new.append(carry[offset - 1] + jnp.sum(pre * window(index, offset), axis=0))
            new.append(carry[KERNEL] + jnp.sum(pre, axis=0))
            return tuple(new)

        zero = jnp.zeros((8, depth), f32)
        sums = lax.fori_loop(0, rows // step_rows, conv_step, (zero,) * (KERNEL + 1))
        for tap in range(KERNEL + 1):
            taps_ref[head, tap : tap + 1, :] = jnp.sum(sums[tap], axis=0, keepdims=True)
        shift_all()

        def back_step(index, carry, head=head):
            total = loaded(g_n.at[head], index) + filtered(head, index, True)
            total = total.reshape(step_rows, depth)
            frame_at = index * step_rows + lax.broadcasted_iota(jnp.int32, total.shape, 0)
            total = jnp.where(frame_at < length, total, 0.0)
            at = pl.ds(pl.multiple_of(index * step_rows, step_rows), step_rows)
            a_n[head, at, :] = total.astype(bf16)
            return carry

        lax.fori_loop(0, rows // step_rows, back_step, 0)
        for first in range(0, rows, frames):
            a_t[span(head), first : first + frames] = a_n[head, first : first + frames, :].T

    def backward(index, head):
        cols = pl.ds(pl.multiple_of(index * block, block), block)
        score_grad = jnp.dot(v_n[head], a_t[span(head), cols], preferred_element_type=f32)
        found = probs[head, :, cols]
        delta = jnp.sum(found * score_grad, axis=0, keepdims=True)
        diff = (found * (score_grad - delta)).astype(bf16)
        value = jnp.dot(found.astype(bf16), a_n[head, cols, :], preferred_element_type=f32)
        key = jnp.dot(diff, q_n[head, cols, :], preferred_element_type=f32)
        query = jnp.dot(k_t[span(head), :], diff, preferred_element_type=f32)
        q_t[span(head), cols] = (query * scale).astype(bf16)
        return key, value

    def finish(head, key, value):
        for first in range(0, rows, frames):
            at = slice(first, first + frames)
            k_t[span(head), at] = (key[at, :] * scale).astype(bf16).T
            v_t[span(head), at] = value[at, :].astype(bf16).T

    for head in range(heads):
        if blocks == 1:
            finish(head, *backward(0, head))
        else:
            zeros = jnp.zeros((rows, depth), f32)

            def step(index, carry, head=head):
                key, value = backward(index, head)
                return carry[0] + key, carry[1] + value

            finish(head, *lax.fori_loop(0, blocks, step, (zeros, zeros)))

    for distance, out in enumerate(outs):
        at = pl.ds(pl.multiple_of((rank ^ distance) * frames, 128), frames)
        out[0] = q_t[:, at]
        out[1] = k_t[:, at]
        out[2] = v_t[:, at]


def core(scalars, weight, bias, pieces):
    count = len(pieces)
    _, high, frames = pieces[0].shape
    heads, _, depth = weight.shape
    rows = count * frames
    block = math.gcd(rows, 512)
    tall = rows + 2 * PAD + 8
    piece = jax.ShapeDtypeStruct((3, high, frames), bf16)
    turned = pltpu.VMEM((high, rows), bf16)
    plain = pltpu.VMEM((heads, rows, depth), bf16)
    outs = pl.pallas_call(
        functools.partial(core_kernel, count, block),
        out_shape=(piece,) * count + (jax.ShapeDtypeStruct((heads, KERNEL + 1, depth), f32),),
        in_specs=[SMEM] + [VMEM] * (2 + count),
        out_specs=(VMEM,) * (count + 1),
        scratch_shapes=[turned] * 4
        + [plain] * 5
        + [
            pltpu.VMEM((heads, rows, rows), f32),
            pltpu.VMEM((8, tall // 8 - 1, 8, depth), f32),
            pltpu.VMEM((tall, depth), f32),
        ],
        compiler_params=pltpu.CompilerParams(
            vmem_limit_bytes=12 * 2**20 + 8 * heads * rows * rows + 4096 * tall
        ),
        cost_estimate=pl.CostEstimate(
            flops=24 * rows * rows * high,
            bytes_accessed=14 * rows * high,
            transcendentals=heads * rows * rows,
        ),
    )(scalars, weight, bias, *[pieces[distance] for distance in taken(count)])
    return outs[:count], outs[count]


def exchanged(pieces, before):
    pieces = list(pieces)
    if before is not None:
        pieces[:0:-1], before[:0:-1] = lax.optimization_barrier((pieces[:0:-1], before[:0:-1]))
    moved = pieces[:1] * len(pieces)
    for distance in range(len(pieces) - 1, 0, -1):
        pairs = [(i, i ^ distance) for i in range(len(pieces))]
        moved[distance] = lax.ppermute(pieces[distance], "seq", pairs)
    return moved


def terms(array, axis, stride, reach):
    count = lax.axis_size(axis)
    found = [array]
    for distance in range(stride, reach, stride):
        pairs = [(i, i ^ distance) for i in range(count)]
        found.append(lax.ppermute(array, axis, pairs))
    return found


def tree_sum(found):
    while len(found) > 1:
        found = [a + b for a, b in zip(found[::2], found[1::2])]
    return found[0]


def on_device(queries, keys, values, grad_out, conv_weight, conv_bias, lengths):
    count = lax.axis_size("seq")
    rank = lax.axis_index("seq").astype(jnp.int32)
    width = queries.shape[2]
    depth = width // HEADS
    heads = HEADS // count
    chunks = math.gcd(heads, 2)
    step = heads // chunks
    by_head = conv_weight.reshape(KERNEL, HEADS, depth).transpose(1, 0, 2)
    weight = lax.dynamic_slice_in_dim(by_head, rank * heads, heads, axis=0)
    bias = lax.dynamic_slice_in_dim(conv_bias.reshape(HEADS, 1, depth), rank * heads, heads, axis=0)
    scalars = jnp.stack([lengths[0], rank])
    sent = pack(rank[None], (queries, keys, values, grad_out), count, chunks)
    order = []
    for pieces in sent:
        order.append(exchanged(pieces, order[-1] if order else None))
    taps = []
    for chunk in range(chunks):
        at = slice(chunk * step, (chunk + 1) * step)
        grads, part = core(scalars, weight[at], bias[at], order[chunk])
        order.append(exchanged(grads, order[-1]))
        taps.append(part)
    returned = order[chunks:]
    taps, returned[0] = lax.optimization_barrier((jnp.concatenate(taps, axis=0), returned[0]))
    taps = tree_sum(terms(taps, "dp", 1, 2))
    return unpack(rank[None], terms(taps, "dp", 2, lax.axis_size("dp")), returned, count, chunks)


def solution(mesh):
    return jax.shard_map(
        on_device,
        mesh=mesh,
        in_specs=(
            P("dp", "seq", None),
            P("dp", "seq", None),
            P("dp", "seq", None),
            P("dp", "seq", None),
            P(),
            P(),
            P("dp"),
        ),
        out_specs=(
            P("dp", "seq", None),
            P("dp", "seq", None),
            P("dp", "seq", None),
            P(None, "seq"),
            P("seq"),
        ),
        check_vma=False,
    )
```

```python
import functools
import math

import jax
import jax.numpy as jnp
from jax import lax
from jax.experimental import pallas as pl
from jax.experimental.pallas import tpu as pltpu
from jax.sharding import PartitionSpec as P

HEADS = 16
KERNEL = 31
PAD = 16
masked_score = -1e30
VMEM = pl.BlockSpec(memory_space=pltpu.VMEM)
SMEM = pl.BlockSpec(memory_space=pltpu.SMEM)
LIMIT = 16 * 1024 * 1024
bf16, f32 = jnp.bfloat16, jnp.float32


def pack_kernel(count, chunks, rank_ref, *refs):
    arrays, outs, turned = refs[:4], refs[4:-1], refs[-1]
    rank = rank_ref[0]
    high = outs[0].shape[1]
    share = high * chunks
    for which, array in enumerate(arrays):
        turned[which] = array[0].T
        for distance in range(count):
            for chunk in range(chunks):
                first = pl.multiple_of((rank ^ distance) * share + chunk * high, 16)
                outs[chunk * count + distance][which] = turned[which, pl.ds(first, high), :]


def pack(rank, arrays, count, chunks):
    _, frames, width = arrays[0].shape
    high = width // count // chunks
    piece = jax.ShapeDtypeStruct((4, high, frames), bf16)
    outs = pl.pallas_call(
        functools.partial(pack_kernel, count, chunks),
        out_shape=(piece,) * (count * chunks),
        in_specs=[SMEM] + [VMEM] * 4,
        out_specs=(VMEM,) * (count * chunks),
        scratch_shapes=[pltpu.VMEM((4, width, frames), bf16)],
        compiler_params=pltpu.CompilerParams(vmem_limit_bytes=LIMIT),
        cost_estimate=pl.CostEstimate(
            flops=0, bytes_accessed=16 * frames * width, transcendentals=0
        ),
    )(rank, *[pltpu.with_memory_space_constraint(array, pltpu.HBM) for array in arrays])
    return [outs[chunk * count : (chunk + 1) * count] for chunk in range(chunks)]


def taken(count):
    return [0] + list(range(count - 1, 0, -1))


def unpack_kernel(count, chunks, rank_ref, *refs):
    pieces, refs = refs[: count * chunks], refs[count * chunks :]
    taps_refs, outs = refs[:-7], refs[-7:-4]
    weight_ref, bias_ref, bias_row, turned = refs[-4:]
    rank = rank_ref[0]
    high = pieces[0].shape[1]
    share = high * chunks
    for which, out in enumerate(outs):
        for chunk in range(chunks):
            for place, distance in enumerate(taken(count)):
                first = pl.multiple_of((rank ^ distance) * share + chunk * high, 16)
                turned[which, pl.ds(first, high), :] = pieces[chunk * count + place][which]
        out[0] = turned[which].T
    taps = taps_refs[0][...] + taps_refs[1][...]
    heads, _, depth = taps.shape
    for head in range(heads):
        at = slice(head * depth, (head + 1) * depth)
        weight_ref[:, at] = taps[head, :KERNEL]
        bias_row[:, at] = taps[head, KERNEL:]
    bias_ref[...] = bias_row[0]


def unpack(rank, taps, pieces, count, chunks):
    _, high, frames = pieces[0][0].shape
    width = high * count * chunks
    whole = jax.ShapeDtypeStruct((1, frames, width), bf16)
    return pl.pallas_call(
        functools.partial(unpack_kernel, count, chunks),
        out_shape=(whole,) * 3
        + (
            jax.ShapeDtypeStruct((KERNEL, width // count), f32),
            jax.ShapeDtypeStruct((width // count,), f32),
        ),
        in_specs=[SMEM] + [VMEM] * (count * chunks + len(taps)),
        out_specs=(VMEM,) * 5,
        scratch_shapes=[
            pltpu.VMEM((1, width // count), f32),
            pltpu.VMEM((3, width, frames), bf16),
        ],
        compiler_params=pltpu.CompilerParams(vmem_limit_bytes=LIMIT),
        cost_estimate=pl.CostEstimate(
            flops=0, bytes_accessed=12 * frames * width, transcendentals=0
        ),
    )(rank, *[part[distance] for part in pieces for distance in taken(count)], *taps)


def core_kernel(count, block, scalars, weight_ref, bias_ref, *refs):
    pieces, outs, taps_ref = refs[:count], refs[count : 2 * count], refs[2 * count]
    q_t, k_t, v_t, a_t, q_n, k_n, v_n, g_n, a_n, probs, shifted, padded = refs[2 * count + 1 :]
    heads, rows, depth = q_n.shape
    frames = pieces[0].shape[2]
    blocks = rows // block
    scale = 1.0 / math.sqrt(depth)
    log_scale = scale * math.log2(math.e)
    length, rank = scalars[0], scalars[1]

    def span(head):
        return slice(head * depth, (head + 1) * depth)

    for distance, piece in zip(taken(count), pieces):
        at = pl.ds(pl.multiple_of((rank ^ distance) * frames, 128), frames)
        q_t[:, at] = piece[0]
        k_t[:, at] = piece[1]
        v_t[:, at] = piece[2]
        for head in range(heads):
            q_n[head, at, :] = piece[0, span(head), :].T
            k_n[head, at, :] = piece[1, span(head), :].T
            v_n[head, at, :] = piece[2, span(head), :].T
            g_n[head, at, :] = piece[3, span(head), :].T

    def forward(index, head):
        cols = pl.ds(pl.multiple_of(index * block, block), block)
        scores = jnp.dot(k_n[head], q_t[span(head), cols], preferred_element_type=f32)
        key_at = lax.broadcasted_iota(jnp.int32, scores.shape, 0)
        scores = jnp.where(key_at < length, scores, masked_score)
        exped = jnp.exp2((scores - jnp.max(scores, axis=0, keepdims=True)) * log_scale)
        found = exped * (1.0 / jnp.sum(exped, axis=0, keepdims=True))
        probs[head, :, cols] = found
        out = jnp.dot(v_t[span(head), :], found.astype(bf16), preferred_element_type=f32)
        frame_at = index * block + lax.broadcasted_iota(jnp.int32, out.shape, 1)
        a_t[span(head), cols] = jnp.where(frame_at < length, out, 0.0).astype(bf16)

    def each_block(body):
        if blocks == 1:
            for head in range(heads):
                body(0, head)
        else:

            def step(index, carry):
                for head in range(heads):
                    body(index, head)
                return carry

            lax.fori_loop(0, blocks, step, 0)

    each_block(forward)

    tall = padded.shape[0]
    padded[0:PAD, :] = jnp.zeros((PAD, depth), f32)
    padded[PAD + rows : tall, :] = jnp.zeros((tall - PAD - rows, depth), f32)

    def shift_all():
        for s in range(8):
            shifted[s] = padded[s : s + tall - 8, :].reshape(tall // 8 - 1, 8, depth)

    step_tiles = 8
    step_rows = 8 * step_tiles

    def window(index, offset):
        return shifted[offset % 8, pl.ds(index * step_tiles + offset // 8, step_tiles)]

    def filtered(head, index, reverse):
        total = None
        for offset in range(1, KERNEL + 1):
            tap = KERNEL - offset if reverse else offset - 1
            term = weight_ref[head, tap : tap + 1, :] * window(index, offset)
            total = term if total is None else total + term
        return total

    def loaded(ref, index):
        at = pl.ds(pl.multiple_of(index * step_rows, step_rows), step_rows)
        return ref[at, :].astype(f32).reshape(step_tiles, 8, depth)

    for head in range(heads):
        for first in range(0, rows, frames):
            at = slice(PAD + first, PAD + first + frames)
            padded[at, :] = a_t[span(head), first : first + frames].T.astype(f32)
        shift_all()

        def conv_step(index, carry, head=head):
            conv_pre = filtered(head, index, False) + bias_ref[head]
            sig = 1.0 / (1.0 + jnp.exp(-conv_pre))
            pre = loaded(g_n.at[head], index) * (sig * (1.0 + conv_pre * (1.0 - sig)))
            pre = pre.astype(bf16).astype(f32)
            at = pl.ds(pl.multiple_of(PAD + index * step_rows, PAD), step_rows)
            padded[at, :] = pre.reshape(step_rows, depth)
            new = []
            for offset in range(1, KERNEL + 1):
                new.append(carry[offset - 1] + jnp.sum(pre * window(index, offset), axis=0))
            new.append(carry[KERNEL] + jnp.sum(pre, axis=0))
            return tuple(new)

        zero = jnp.zeros((8, depth), f32)
        sums = lax.fori_loop(0, rows // step_rows, conv_step, (zero,) * (KERNEL + 1))
        for tap in range(KERNEL + 1):
            taps_ref[head, tap : tap + 1, :] = jnp.sum(sums[tap], axis=0, keepdims=True)
        shift_all()

        def back_step(index, carry, head=head):
            total = loaded(g_n.at[head], index) + filtered(head, index, True)
            total = total.reshape(step_rows, depth)
            frame_at = index * step_rows + lax.broadcasted_iota(jnp.int32, total.shape, 0)
            total = jnp.where(frame_at < length, total, 0.0)
            at = pl.ds(pl.multiple_of(index * step_rows, step_rows), step_rows)
            a_n[head, at, :] = total.astype(bf16)
            return carry

        lax.fori_loop(0, rows // step_rows, back_step, 0)
        for first in range(0, rows, frames):
            a_t[span(head), first : first + frames] = a_n[head, first : first + frames, :].T

    def backward(index, head):
        cols = pl.ds(pl.multiple_of(index * block, block), block)
        score_grad = jnp.dot(v_n[head], a_t[span(head), cols], preferred_element_type=f32)
        found = probs[head, :, cols]
        delta = jnp.sum(found * score_grad, axis=0, keepdims=True)
        diff = (found * (score_grad - delta)).astype(bf16)
        value = jnp.dot(found.astype(bf16), a_n[head, cols, :], preferred_element_type=f32)
        key = jnp.dot(diff, q_n[head, cols, :], preferred_element_type=f32)
        query = jnp.dot(k_t[span(head), :], diff, preferred_element_type=f32)
        q_t[span(head), cols] = (query * scale).astype(bf16)
        return key, value

    def finish(head, key, value):
        for first in range(0, rows, frames):
            at = slice(first, first + frames)
            k_t[span(head), at] = (key[at, :] * scale).astype(bf16).T
            v_t[span(head), at] = value[at, :].astype(bf16).T

    for head in range(heads):
        if blocks == 1:
            finish(head, *backward(0, head))
        else:
            zeros = jnp.zeros((rows, depth), f32)

            def step(index, carry, head=head):
                key, value = backward(index, head)
                return carry[0] + key, carry[1] + value

            finish(head, *lax.fori_loop(0, blocks, step, (zeros, zeros)))

    for distance, out in enumerate(outs):
        at = pl.ds(pl.multiple_of((rank ^ distance) * frames, 128), frames)
        out[0] = q_t[:, at]
        out[1] = k_t[:, at]
        out[2] = v_t[:, at]


def core(scalars, weight, bias, pieces):
    count = len(pieces)
    _, high, frames = pieces[0].shape
    heads, _, depth = weight.shape
    rows = count * frames
    block = math.gcd(rows, 512)
    tall = rows + 2 * PAD + 8
    piece = jax.ShapeDtypeStruct((3, high, frames), bf16)
    turned = pltpu.VMEM((high, rows), bf16)
    plain = pltpu.VMEM((heads, rows, depth), bf16)
    outs = pl.pallas_call(
        functools.partial(core_kernel, count, block),
        out_shape=(piece,) * count + (jax.ShapeDtypeStruct((heads, KERNEL + 1, depth), f32),),
        in_specs=[SMEM] + [VMEM] * (2 + count),
        out_specs=(VMEM,) * (count + 1),
        scratch_shapes=[turned] * 4
        + [plain] * 5
        + [
            pltpu.VMEM((heads, rows, rows), f32),
            pltpu.VMEM((8, tall // 8 - 1, 8, depth), f32),
            pltpu.VMEM((tall, depth), f32),
        ],
        compiler_params=pltpu.CompilerParams(
            vmem_limit_bytes=12 * 2**20 + 8 * heads * rows * rows + 4096 * tall
        ),
        cost_estimate=pl.CostEstimate(
            flops=24 * rows * rows * high,
            bytes_accessed=14 * rows * high,
            transcendentals=heads * rows * rows,
        ),
    )(scalars, weight, bias, *[pieces[distance] for distance in taken(count)])
    return outs[:count], outs[count]


def exchanged(pieces, before, late=None):
    pieces = list(pieces)
    if late is not None:
        pieces[1], late = lax.optimization_barrier((pieces[1], late))
    if before is not None and len(pieces) > 2:
        pieces[:1:-1], before[:0:-1] = lax.optimization_barrier((pieces[:1:-1], before[:0:-1]))
    moved = pieces[:1] * len(pieces)
    for distance in range(len(pieces) - 1, 0, -1):
        pairs = [(i, i ^ distance) for i in range(len(pieces))]
        moved[distance] = lax.ppermute(pieces[distance], "seq", pairs)
    return moved


def with_partner(array, axis, distance):
    pairs = [(i, i ^ distance) for i in range(lax.axis_size(axis))]
    return [array, lax.ppermute(array, axis, pairs)]


def on_device(queries, keys, values, grad_out, conv_weight, conv_bias, lengths):
    count = lax.axis_size("seq")
    rank = lax.axis_index("seq").astype(jnp.int32)
    width = queries.shape[2]
    depth = width // HEADS
    heads = HEADS // count
    chunks = math.gcd(heads, 2)
    step = heads // chunks
    by_head = conv_weight.reshape(KERNEL, HEADS, depth).transpose(1, 0, 2)
    weight = lax.dynamic_slice_in_dim(by_head, rank * heads, heads, axis=0)
    bias = lax.dynamic_slice_in_dim(conv_bias.reshape(HEADS, 1, depth), rank * heads, heads, axis=0)
    scalars = jnp.stack([lengths[0], rank])
    sent = pack(rank[None], (queries, keys, values, grad_out), count, chunks)
    order = []
    for pieces in sent:
        order.append(exchanged(pieces, order[-1] if order else None))
    taps = []
    for chunk in range(chunks):
        at = slice(chunk * step, (chunk + 1) * step)
        grads, part = core(scalars, weight[at], bias[at], order[chunk])
        taps.append(part)
        if chunk < chunks - 1:
            order.append(exchanged(grads, order[-1]))
    before = order[-1]
    taps, before[:0:-1] = lax.optimization_barrier((jnp.concatenate(taps, axis=0), before[:0:-1]))
    pair = with_partner(taps, "dp", 1)
    distance = 2
    while distance < lax.axis_size("dp"):
        total = pair[0] + pair[1]
        if distance == 2:
            order.append(exchanged(grads, order[-1], total))
        pair = with_partner(total, "dp", distance)
        distance *= 2
    return unpack(rank[None], pair, order[chunks:], count, chunks)


def solution(mesh):
    return jax.shard_map(
        on_device,
        mesh=mesh,
        in_specs=(
            P("dp", "seq", None),
            P("dp", "seq", None),
            P("dp", "seq", None),
            P("dp", "seq", None),
            P(),
            P(),
            P("dp"),
        ),
        out_specs=(
            P("dp", "seq", None),
            P("dp", "seq", None),
            P("dp", "seq", None),
            P(None, "seq"),
            P("seq"),
        ),
        check_vma=False,
    )
```

```python
import functools
import math

import jax
import jax.numpy as jnp
from jax import lax
from jax.experimental import pallas as pl
from jax.experimental.pallas import tpu as pltpu
from jax.sharding import PartitionSpec as P

HEADS = 16
KERNEL = 31
PAD = 16
masked_score = -1e30
VMEM = pl.BlockSpec(memory_space=pltpu.VMEM)
SMEM = pl.BlockSpec(memory_space=pltpu.SMEM)
LIMIT = 16 * 1024 * 1024
bf16, f32 = jnp.bfloat16, jnp.float32


def pack_kernel(count, chunks, rank_ref, *refs):
    arrays, outs, turned = refs[:4], refs[4:-1], refs[-1]
    rank = rank_ref[0]
    high = outs[0].shape[1]
    share = high * chunks
    for which, array in enumerate(arrays):
        turned[which] = array[0].T
        for distance in range(count):
            for chunk in range(chunks):
                first = pl.multiple_of((rank ^ distance) * share + chunk * high, 16)
                outs[chunk * count + distance][which] = turned[which, pl.ds(first, high), :]


def pack(rank, arrays, count, chunks):
    _, frames, width = arrays[0].shape
    high = width // count // chunks
    piece = jax.ShapeDtypeStruct((4, high, frames), bf16)
    outs = pl.pallas_call(
        functools.partial(pack_kernel, count, chunks),
        out_shape=(piece,) * (count * chunks),
        in_specs=[SMEM] + [VMEM] * 4,
        out_specs=(VMEM,) * (count * chunks),
        scratch_shapes=[pltpu.VMEM((4, width, frames), bf16)],
        compiler_params=pltpu.CompilerParams(vmem_limit_bytes=LIMIT),
        cost_estimate=pl.CostEstimate(
            flops=0, bytes_accessed=16 * frames * width, transcendentals=0
        ),
    )(rank, *[pltpu.with_memory_space_constraint(array, pltpu.HBM) for array in arrays])
    return [outs[chunk * count : (chunk + 1) * count] for chunk in range(chunks)]


def taken(count):
    return [0] + list(range(count - 1, 0, -1))


def unpack_kernel(count, chunks, rank_ref, *refs):
    pieces, refs = refs[: count * chunks], refs[count * chunks :]
    taps_refs, outs = refs[:-7], refs[-7:-4]
    weight_ref, bias_ref, bias_row, turned = refs[-4:]
    rank = rank_ref[0]
    high = pieces[0].shape[1]
    share = high * chunks
    for which, out in enumerate(outs):
        for chunk in range(chunks):
            for place, distance in enumerate(taken(count)):
                first = pl.multiple_of((rank ^ distance) * share + chunk * high, 16)
                turned[which, pl.ds(first, high), :] = pieces[chunk * count + place][which]
        out[0] = turned[which].T
    taps = tree_sum([ref[...] for ref in taps_refs])
    heads, _, depth = taps.shape
    for head in range(heads):
        at = slice(head * depth, (head + 1) * depth)
        weight_ref[:, at] = taps[head, :KERNEL]
        bias_row[:, at] = taps[head, KERNEL:]
    bias_ref[...] = bias_row[0]


def unpack(rank, taps, pieces, count, chunks):
    _, high, frames = pieces[0][0].shape
    width = high * count * chunks
    whole = jax.ShapeDtypeStruct((1, frames, width), bf16)
    return pl.pallas_call(
        functools.partial(unpack_kernel, count, chunks),
        out_shape=(whole,) * 3
        + (
            jax.ShapeDtypeStruct((KERNEL, width // count), f32),
            jax.ShapeDtypeStruct((width // count,), f32),
        ),
        in_specs=[SMEM] + [VMEM] * (count * chunks + len(taps)),
        out_specs=(VMEM,) * 5,
        scratch_shapes=[
            pltpu.VMEM((1, width // count), f32),
            pltpu.VMEM((3, width, frames), bf16),
        ],
        compiler_params=pltpu.CompilerParams(vmem_limit_bytes=LIMIT),
        cost_estimate=pl.CostEstimate(
            flops=0, bytes_accessed=12 * frames * width, transcendentals=0
        ),
    )(rank, *[part[distance] for part in pieces for distance in taken(count)], *taps)


def core_kernel(count, block, scalars, weight_ref, bias_ref, *refs):
    pieces, outs, taps_ref = refs[:count], refs[count : 2 * count], refs[2 * count]
    q_t, k_t, v_t, a_t, q_n, k_n, v_n, g_n, a_n, probs, shifted, padded = refs[2 * count + 1 :]
    heads, rows, depth = q_n.shape
    frames = pieces[0].shape[2]
    blocks = rows // block
    scale = 1.0 / math.sqrt(depth)
    log_scale = scale * math.log2(math.e)
    length, rank = scalars[0], scalars[1]

    def span(head):
        return slice(head * depth, (head + 1) * depth)

    for distance, piece in zip(taken(count), pieces):
        at = pl.ds(pl.multiple_of((rank ^ distance) * frames, 128), frames)
        q_t[:, at] = piece[0]
        k_t[:, at] = piece[1]
        v_t[:, at] = piece[2]
        for head in range(heads):
            q_n[head, at, :] = piece[0, span(head), :].T
            k_n[head, at, :] = piece[1, span(head), :].T
            v_n[head, at, :] = piece[2, span(head), :].T
            g_n[head, at, :] = piece[3, span(head), :].T

    def forward(index, head):
        cols = pl.ds(pl.multiple_of(index * block, block), block)
        scores = jnp.dot(k_n[head], q_t[span(head), cols], preferred_element_type=f32)
        key_at = lax.broadcasted_iota(jnp.int32, scores.shape, 0)
        scores = jnp.where(key_at < length, scores, masked_score)
        exped = jnp.exp2((scores - jnp.max(scores, axis=0, keepdims=True)) * log_scale)
        found = exped * (1.0 / jnp.sum(exped, axis=0, keepdims=True))
        probs[head, :, cols] = found
        out = jnp.dot(v_t[span(head), :], found.astype(bf16), preferred_element_type=f32)
        frame_at = index * block + lax.broadcasted_iota(jnp.int32, out.shape, 1)
        a_t[span(head), cols] = jnp.where(frame_at < length, out, 0.0).astype(bf16)

    def each_block(body):
        if blocks == 1:
            for head in range(heads):
                body(0, head)
        else:

            def step(index, carry):
                for head in range(heads):
                    body(index, head)
                return carry

            lax.fori_loop(0, blocks, step, 0)

    each_block(forward)

    tall = padded.shape[0]
    padded[0:PAD, :] = jnp.zeros((PAD, depth), f32)
    padded[PAD + rows : tall, :] = jnp.zeros((tall - PAD - rows, depth), f32)

    def shift_all():
        for s in range(8):
            shifted[s] = padded[s : s + tall - 8, :].reshape(tall // 8 - 1, 8, depth)

    step_tiles = 8
    step_rows = 8 * step_tiles

    def window(index, offset):
        return shifted[offset % 8, pl.ds(index * step_tiles + offset // 8, step_tiles)]

    def filtered(head, index, reverse):
        total = None
        for offset in range(1, KERNEL + 1):
            tap = KERNEL - offset if reverse else offset - 1
            term = weight_ref[head, tap : tap + 1, :] * window(index, offset)
            total = term if total is None else total + term
        return total

    def loaded(ref, index):
        at = pl.ds(pl.multiple_of(index * step_rows, step_rows), step_rows)
        return ref[at, :].astype(f32).reshape(step_tiles, 8, depth)

    for head in range(heads):
        for first in range(0, rows, frames):
            at = slice(PAD + first, PAD + first + frames)
            padded[at, :] = a_t[span(head), first : first + frames].T.astype(f32)
        shift_all()

        def conv_step(index, carry, head=head):
            conv_pre = filtered(head, index, False) + bias_ref[head]
            sig = 1.0 / (1.0 + jnp.exp(-conv_pre))
            pre = loaded(g_n.at[head], index) * (sig * (1.0 + conv_pre * (1.0 - sig)))
            pre = pre.astype(bf16).astype(f32)
            at = pl.ds(pl.multiple_of(PAD + index * step_rows, PAD), step_rows)
            padded[at, :] = pre.reshape(step_rows, depth)
            new = []
            for offset in range(1, KERNEL + 1):
                new.append(carry[offset - 1] + jnp.sum(pre * window(index, offset), axis=0))
            new.append(carry[KERNEL] + jnp.sum(pre, axis=0))
            return tuple(new)

        zero = jnp.zeros((8, depth), f32)
        sums = lax.fori_loop(0, rows // step_rows, conv_step, (zero,) * (KERNEL + 1))
        for tap in range(KERNEL + 1):
            taps_ref[head, tap : tap + 1, :] = jnp.sum(sums[tap], axis=0, keepdims=True)
        shift_all()

        def back_step(index, carry, head=head):
            total = loaded(g_n.at[head], index) + filtered(head, index, True)
            total = total.reshape(step_rows, depth)
            frame_at = index * step_rows + lax.broadcasted_iota(jnp.int32, total.shape, 0)
            total = jnp.where(frame_at < length, total, 0.0)
            at = pl.ds(pl.multiple_of(index * step_rows, step_rows), step_rows)
            a_n[head, at, :] = total.astype(bf16)
            return carry

        lax.fori_loop(0, rows // step_rows, back_step, 0)
        for first in range(0, rows, frames):
            a_t[span(head), first : first + frames] = a_n[head, first : first + frames, :].T

    def backward(index, head):
        cols = pl.ds(pl.multiple_of(index * block, block), block)
        score_grad = jnp.dot(v_n[head], a_t[span(head), cols], preferred_element_type=f32)
        found = probs[head, :, cols]
        delta = jnp.sum(found * score_grad, axis=0, keepdims=True)
        diff = (found * (score_grad - delta)).astype(bf16)
        value = jnp.dot(found.astype(bf16), a_n[head, cols, :], preferred_element_type=f32)
        key = jnp.dot(diff, q_n[head, cols, :], preferred_element_type=f32)
        query = jnp.dot(k_t[span(head), :], diff, preferred_element_type=f32)
        q_t[span(head), cols] = (query * scale).astype(bf16)
        return key, value

    def finish(head, key, value):
        for first in range(0, rows, frames):
            at = slice(first, first + frames)
            k_t[span(head), at] = (key[at, :] * scale).astype(bf16).T
            v_t[span(head), at] = value[at, :].astype(bf16).T

    for head in range(heads):
        if blocks == 1:
            finish(head, *backward(0, head))
        else:
            zeros = jnp.zeros((rows, depth), f32)

            def step(index, carry, head=head):
                key, value = backward(index, head)
                return carry[0] + key, carry[1] + value

            finish(head, *lax.fori_loop(0, blocks, step, (zeros, zeros)))

    for distance, out in enumerate(outs):
        at = pl.ds(pl.multiple_of((rank ^ distance) * frames, 128), frames)
        out[0] = q_t[:, at]
        out[1] = k_t[:, at]
        out[2] = v_t[:, at]


def core(scalars, weight, bias, pieces):
    count = len(pieces)
    _, high, frames = pieces[0].shape
    heads, _, depth = weight.shape
    rows = count * frames
    block = math.gcd(rows, 512)
    tall = rows + 2 * PAD + 8
    piece = jax.ShapeDtypeStruct((3, high, frames), bf16)
    turned = pltpu.VMEM((high, rows), bf16)
    plain = pltpu.VMEM((heads, rows, depth), bf16)
    outs = pl.pallas_call(
        functools.partial(core_kernel, count, block),
        out_shape=(piece,) * count + (jax.ShapeDtypeStruct((heads, KERNEL + 1, depth), f32),),
        in_specs=[SMEM] + [VMEM] * (2 + count),
        out_specs=(VMEM,) * (count + 1),
        scratch_shapes=[turned] * 4
        + [plain] * 5
        + [
            pltpu.VMEM((heads, rows, rows), f32),
            pltpu.VMEM((8, tall // 8 - 1, 8, depth), f32),
            pltpu.VMEM((tall, depth), f32),
        ],
        compiler_params=pltpu.CompilerParams(
            vmem_limit_bytes=12 * 2**20 + 8 * heads * rows * rows + 4096 * tall
        ),
        cost_estimate=pl.CostEstimate(
            flops=24 * rows * rows * high,
            bytes_accessed=14 * rows * high,
            transcendentals=heads * rows * rows,
        ),
    )(scalars, weight, bias, *[pieces[distance] for distance in taken(count)])
    return outs[:count], outs[count]


def exchanged(pieces, before):
    pieces = list(pieces)
    if before is not None and len(pieces) > 2:
        pieces[:1:-1], before[:0:-1] = lax.optimization_barrier((pieces[:1:-1], before[:0:-1]))
    moved = pieces[:1] * len(pieces)
    for distance in range(len(pieces) - 1, 0, -1):
        pairs = [(i, i ^ distance) for i in range(len(pieces))]
        moved[distance] = lax.ppermute(pieces[distance], "seq", pairs)
    return moved


def terms(array, axis, stride, reach):
    count = lax.axis_size(axis)
    found = [array]
    for distance in range(stride, reach, stride):
        pairs = [(i, i ^ distance) for i in range(count)]
        found.append(lax.ppermute(array, axis, pairs))
    return found


def tree_sum(found):
    while len(found) > 1:
        found = [a + b for a, b in zip(found[::2], found[1::2])]
    return found[0]


def on_device(queries, keys, values, grad_out, conv_weight, conv_bias, lengths):
    count = lax.axis_size("seq")
    rank = lax.axis_index("seq").astype(jnp.int32)
    width = queries.shape[2]
    depth = width // HEADS
    heads = HEADS // count
    chunks = math.gcd(heads, 2)
    step = heads // chunks
    by_head = conv_weight.reshape(KERNEL, HEADS, depth).transpose(1, 0, 2)
    weight = lax.dynamic_slice_in_dim(by_head, rank * heads, heads, axis=0)
    bias = lax.dynamic_slice_in_dim(conv_bias.reshape(HEADS, 1, depth), rank * heads, heads, axis=0)
    scalars = jnp.stack([lengths[0], rank])
    sent = pack(rank[None], (queries, keys, values, grad_out), count, chunks)
    order = []
    for pieces in sent:
        order.append(exchanged(pieces, order[-1] if order else None))
    taps = []
    for chunk in range(chunks):
        at = slice(chunk * step, (chunk + 1) * step)
        grads, part = core(scalars, weight[at], bias[at], order[chunk])
        taps.append(part)
        if chunk < chunks - 1:
            order.append(exchanged(grads, order[-1]))
    before, grads = order[-1], list(grads)
    if chunks > 1:
        for distance in range(count - 1, 0, -1):
            early = count - 1 if distance < count - 1 else 1
            grads[distance], before[early] = lax.optimization_barrier(
                (grads[distance], before[early])
            )
    order.append(exchanged(grads, None))
    taps, before[:0:-1] = lax.optimization_barrier((jnp.concatenate(taps, axis=0), before[:0:-1]))
    taps = tree_sum(terms(taps, "dp", 1, 2))
    return unpack(rank[None], terms(taps, "dp", 2, lax.axis_size("dp")), order[chunks:], count, chunks)


def solution(mesh):
    return jax.shard_map(
        on_device,
        mesh=mesh,
        in_specs=(
            P("dp", "seq", None),
            P("dp", "seq", None),
            P("dp", "seq", None),
            P("dp", "seq", None),
            P(),
            P(),
            P("dp"),
        ),
        out_specs=(
            P("dp", "seq", None),
            P("dp", "seq", None),
            P("dp", "seq", None),
            P(None, "seq"),
            P("seq"),
        ),
        check_vma=False,
    )
```

```python
import functools
import math

import jax
import jax.numpy as jnp
from jax import lax
from jax.experimental import pallas as pl
from jax.experimental.pallas import tpu as pltpu
from jax.sharding import PartitionSpec as P

HEADS = 16
KERNEL = 31
PAD = 16
masked_score = -1e30
VMEM = pl.BlockSpec(memory_space=pltpu.VMEM)
SMEM = pl.BlockSpec(memory_space=pltpu.SMEM)
LIMIT = 16 * 1024 * 1024
bf16, f32 = jnp.bfloat16, jnp.float32


def pack_kernel(count, chunks, rank_ref, *refs):
    arrays, outs, turned = refs[:4], refs[4:-1], refs[-1]
    rank = rank_ref[0]
    high = outs[0].shape[1]
    share = high * chunks
    for which, array in enumerate(arrays):
        turned[which] = array[0].T
        for distance in range(count):
            for chunk in range(chunks):
                first = pl.multiple_of((rank ^ distance) * share + chunk * high, 16)
                outs[chunk * count + distance][which] = turned[which, pl.ds(first, high), :]


def pack(rank, arrays, count, chunks):
    _, frames, width = arrays[0].shape
    high = width // count // chunks
    piece = jax.ShapeDtypeStruct((4, high, frames), bf16)
    outs = pl.pallas_call(
        functools.partial(pack_kernel, count, chunks),
        out_shape=(piece,) * (count * chunks),
        in_specs=[SMEM] + [VMEM] * 4,
        out_specs=(VMEM,) * (count * chunks),
        scratch_shapes=[pltpu.VMEM((4, width, frames), bf16)],
        compiler_params=pltpu.CompilerParams(vmem_limit_bytes=LIMIT),
        cost_estimate=pl.CostEstimate(
            flops=0, bytes_accessed=16 * frames * width, transcendentals=0
        ),
    )(rank, *[pltpu.with_memory_space_constraint(array, pltpu.HBM) for array in arrays])
    return [outs[chunk * count : (chunk + 1) * count] for chunk in range(chunks)]


def taken(count):
    return [0] + list(range(count - 1, 0, -1))


def unpack_kernel(count, chunks, rank_ref, *refs):
    pieces, refs = refs[: count * chunks], refs[count * chunks :]
    taps_refs, outs = refs[:-7], refs[-7:-4]
    weight_ref, bias_ref, bias_row, turned = refs[-4:]
    rank = rank_ref[0]
    high = pieces[0].shape[1]
    share = high * chunks
    for which, out in enumerate(outs):
        for chunk in range(chunks):
            for place, distance in enumerate(taken(count)):
                first = pl.multiple_of((rank ^ distance) * share + chunk * high, 16)
                turned[which, pl.ds(first, high), :] = pieces[chunk * count + place][which]
        out[0] = turned[which].T
    taps = tree_sum([ref[...] for ref in taps_refs])
    heads, _, depth = taps.shape
    for head in range(heads):
        at = slice(head * depth, (head + 1) * depth)
        weight_ref[:, at] = taps[head, :KERNEL]
        bias_row[:, at] = taps[head, KERNEL:]
    bias_ref[...] = bias_row[0]


def unpack(rank, taps, pieces, count, chunks):
    _, high, frames = pieces[0][0].shape
    width = high * count * chunks
    whole = jax.ShapeDtypeStruct((1, frames, width), bf16)
    return pl.pallas_call(
        functools.partial(unpack_kernel, count, chunks),
        out_shape=(whole,) * 3
        + (
            jax.ShapeDtypeStruct((KERNEL, width // count), f32),
            jax.ShapeDtypeStruct((width // count,), f32),
        ),
        in_specs=[SMEM] + [VMEM] * (count * chunks + len(taps)),
        out_specs=(VMEM,) * 5,
        scratch_shapes=[
            pltpu.VMEM((1, width // count), f32),
            pltpu.VMEM((3, width, frames), bf16),
        ],
        compiler_params=pltpu.CompilerParams(vmem_limit_bytes=LIMIT),
        cost_estimate=pl.CostEstimate(
            flops=0, bytes_accessed=12 * frames * width, transcendentals=0
        ),
    )(rank, *[part[distance] for part in pieces for distance in taken(count)], *taps)


def core_kernel(count, block, scalars, weight_ref, bias_ref, *refs):
    pieces, outs, taps_ref = refs[:count], refs[count : 2 * count], refs[2 * count]
    q_t, k_t, v_t, a_t, q_n, k_n, v_n, g_n, a_n, probs, shifted, padded = refs[2 * count + 1 :]
    heads, rows, depth = q_n.shape
    frames = pieces[0].shape[2]
    blocks = rows // block
    scale = 1.0 / math.sqrt(depth)
    log_scale = scale * math.log2(math.e)
    length, rank = scalars[0], scalars[1]

    def span(head):
        return slice(head * depth, (head + 1) * depth)

    for distance, piece in zip(taken(count), pieces):
        at = pl.ds(pl.multiple_of((rank ^ distance) * frames, 128), frames)
        q_t[:, at] = piece[0]
        k_t[:, at] = piece[1]
        v_t[:, at] = piece[2]
        for head in range(heads):
            q_n[head, at, :] = piece[0, span(head), :].T
            k_n[head, at, :] = piece[1, span(head), :].T
            v_n[head, at, :] = piece[2, span(head), :].T
            g_n[head, at, :] = piece[3, span(head), :].T

    def forward(index, head):
        cols = pl.ds(pl.multiple_of(index * block, block), block)
        scores = jnp.dot(k_n[head], q_t[span(head), cols], preferred_element_type=f32)
        key_at = lax.broadcasted_iota(jnp.int32, scores.shape, 0)
        scores = jnp.where(key_at < length, scores, masked_score)
        exped = jnp.exp2((scores - jnp.max(scores, axis=0, keepdims=True)) * log_scale)
        found = exped * (1.0 / jnp.sum(exped, axis=0, keepdims=True))
        probs[head, :, cols] = found
        out = jnp.dot(v_t[span(head), :], found.astype(bf16), preferred_element_type=f32)
        frame_at = index * block + lax.broadcasted_iota(jnp.int32, out.shape, 1)
        a_t[span(head), cols] = jnp.where(frame_at < length, out, 0.0).astype(bf16)

    def each_block(body):
        if blocks == 1:
            for head in range(heads):
                body(0, head)
        else:

            def step(index, carry):
                for head in range(heads):
                    body(index, head)
                return carry

            lax.fori_loop(0, blocks, step, 0)

    each_block(forward)

    tall = padded.shape[0]
    padded[0:PAD, :] = jnp.zeros((PAD, depth), f32)
    padded[PAD + rows : tall, :] = jnp.zeros((tall - PAD - rows, depth), f32)

    def shift_all():
        for s in range(8):
            shifted[s] = padded[s : s + tall - 8, :].reshape(tall // 8 - 1, 8, depth)

    step_tiles = 8
    step_rows = 8 * step_tiles

    def window(index, offset):
        return shifted[offset % 8, pl.ds(index * step_tiles + offset // 8, step_tiles)]

    def filtered(head, index, reverse):
        total = None
        for offset in range(1, KERNEL + 1):
            tap = KERNEL - offset if reverse else offset - 1
            term = weight_ref[head, tap : tap + 1, :] * window(index, offset)
            total = term if total is None else total + term
        return total

    def loaded(ref, index):
        at = pl.ds(pl.multiple_of(index * step_rows, step_rows), step_rows)
        return ref[at, :].astype(f32).reshape(step_tiles, 8, depth)

    for head in range(heads):
        for first in range(0, rows, frames):
            at = slice(PAD + first, PAD + first + frames)
            padded[at, :] = a_t[span(head), first : first + frames].T.astype(f32)
        shift_all()

        def conv_step(index, carry, head=head):
            conv_pre = filtered(head, index, False) + bias_ref[head]
            sig = 1.0 / (1.0 + jnp.exp(-conv_pre))
            pre = loaded(g_n.at[head], index) * (sig * (1.0 + conv_pre * (1.0 - sig)))
            pre = pre.astype(bf16).astype(f32)
            at = pl.ds(pl.multiple_of(PAD + index * step_rows, PAD), step_rows)
            padded[at, :] = pre.reshape(step_rows, depth)
            new = []
            for offset in range(1, KERNEL + 1):
                new.append(carry[offset - 1] + jnp.sum(pre * window(index, offset), axis=0))
            new.append(carry[KERNEL] + jnp.sum(pre, axis=0))
            return tuple(new)

        zero = jnp.zeros((8, depth), f32)
        sums = lax.fori_loop(0, rows // step_rows, conv_step, (zero,) * (KERNEL + 1))
        for tap in range(KERNEL + 1):
            taps_ref[head, tap : tap + 1, :] = jnp.sum(sums[tap], axis=0, keepdims=True)
        shift_all()

        def back_step(index, carry, head=head):
            total = loaded(g_n.at[head], index) + filtered(head, index, True)
            total = total.reshape(step_rows, depth)
            frame_at = index * step_rows + lax.broadcasted_iota(jnp.int32, total.shape, 0)
            total = jnp.where(frame_at < length, total, 0.0)
            at = pl.ds(pl.multiple_of(index * step_rows, step_rows), step_rows)
            a_n[head, at, :] = total.astype(bf16)
            return carry

        lax.fori_loop(0, rows // step_rows, back_step, 0)
        for first in range(0, rows, frames):
            a_t[span(head), first : first + frames] = a_n[head, first : first + frames, :].T

    def backward(index, head):
        cols = pl.ds(pl.multiple_of(index * block, block), block)
        score_grad = jnp.dot(v_n[head], a_t[span(head), cols], preferred_element_type=f32)
        found = probs[head, :, cols]
        delta = jnp.sum(found * score_grad, axis=0, keepdims=True)
        diff = (found * (score_grad - delta)).astype(bf16)
        value = jnp.dot(found.astype(bf16), a_n[head, cols, :], preferred_element_type=f32)
        key = jnp.dot(diff, q_n[head, cols, :], preferred_element_type=f32)
        query = jnp.dot(k_t[span(head), :], diff, preferred_element_type=f32)
        q_t[span(head), cols] = (query * scale).astype(bf16)
        return key, value

    def finish(head, key, value):
        for first in range(0, rows, frames):
            at = slice(first, first + frames)
            k_t[span(head), at] = (key[at, :] * scale).astype(bf16).T
            v_t[span(head), at] = value[at, :].astype(bf16).T

    for head in range(heads):
        if blocks == 1:
            finish(head, *backward(0, head))
        else:
            zeros = jnp.zeros((rows, depth), f32)

            def step(index, carry, head=head):
                key, value = backward(index, head)
                return carry[0] + key, carry[1] + value

            finish(head, *lax.fori_loop(0, blocks, step, (zeros, zeros)))

    for distance, out in enumerate(outs):
        at = pl.ds(pl.multiple_of((rank ^ distance) * frames, 128), frames)
        out[0] = q_t[:, at]
        out[1] = k_t[:, at]
        out[2] = v_t[:, at]


def core(scalars, weight, bias, pieces):
    count = len(pieces)
    _, high, frames = pieces[0].shape
    heads, _, depth = weight.shape
    rows = count * frames
    block = math.gcd(rows, 512)
    tall = rows + 2 * PAD + 8
    piece = jax.ShapeDtypeStruct((3, high, frames), bf16)
    turned = pltpu.VMEM((high, rows), bf16)
    plain = pltpu.VMEM((heads, rows, depth), bf16)
    outs = pl.pallas_call(
        functools.partial(core_kernel, count, block),
        out_shape=(piece,) * count + (jax.ShapeDtypeStruct((heads, KERNEL + 1, depth), f32),),
        in_specs=[SMEM] + [VMEM] * (2 + count),
        out_specs=(VMEM,) * (count + 1),
        scratch_shapes=[turned] * 4
        + [plain] * 5
        + [
            pltpu.VMEM((heads, rows, rows), f32),
            pltpu.VMEM((8, tall // 8 - 1, 8, depth), f32),
            pltpu.VMEM((tall, depth), f32),
        ],
        compiler_params=pltpu.CompilerParams(
            vmem_limit_bytes=12 * 2**20 + 8 * heads * rows * rows + 4096 * tall
        ),
        cost_estimate=pl.CostEstimate(
            flops=24 * rows * rows * high,
            bytes_accessed=14 * rows * high,
            transcendentals=heads * rows * rows,
        ),
    )(scalars, weight, bias, *[pieces[distance] for distance in taken(count)])
    return outs[:count], outs[count]


def exchanged(pieces, before, eager=False):
    pieces = list(pieces)
    last = len(pieces) - 1
    if before is not None and eager:
        pieces[last], before[last] = lax.optimization_barrier((pieces[last], before[last]))
    if before is not None and last > 1:
        wait = slice(last - 1 if eager else last, 1, -1)
        pieces[wait], before[:0:-1] = lax.optimization_barrier((pieces[wait], before[:0:-1]))
    moved = pieces[:1] * len(pieces)
    for distance in range(len(pieces) - 1, 0, -1):
        pairs = [(i, i ^ distance) for i in range(len(pieces))]
        moved[distance] = lax.ppermute(pieces[distance], "seq", pairs)
    return moved


def terms(array, axis, stride, reach, moved=None):
    count = lax.axis_size(axis)
    found = [array]
    for distance in range(stride, reach, stride):
        if moved is not None and distance + stride == reach:
            array, moved[1] = lax.optimization_barrier((array, moved[1]))
        pairs = [(i, i ^ distance) for i in range(count)]
        found.append(lax.ppermute(array, axis, pairs))
    return found


def tree_sum(found):
    while len(found) > 1:
        found = [a + b for a, b in zip(found[::2], found[1::2])]
    return found[0]


def on_device(queries, keys, values, grad_out, conv_weight, conv_bias, lengths):
    count = lax.axis_size("seq")
    rank = lax.axis_index("seq").astype(jnp.int32)
    width = queries.shape[2]
    depth = width // HEADS
    heads = HEADS // count
    chunks = math.gcd(heads, 2)
    step = heads // chunks
    by_head = conv_weight.reshape(KERNEL, HEADS, depth).transpose(1, 0, 2)
    weight = lax.dynamic_slice_in_dim(by_head, rank * heads, heads, axis=0)
    bias = lax.dynamic_slice_in_dim(conv_bias.reshape(HEADS, 1, depth), rank * heads, heads, axis=0)
    scalars = jnp.stack([lengths[0], rank])
    sent = pack(rank[None], (queries, keys, values, grad_out), count, chunks)
    order = []
    for pieces in sent:
        order.append(exchanged(pieces, order[-1] if order else None))
    taps = []
    for chunk in range(chunks):
        at = slice(chunk * step, (chunk + 1) * step)
        grads, part = core(scalars, weight[at], bias[at], order[chunk])
        taps.append(part)
        if chunk < chunks - 1:
            order.append(exchanged(grads, order[-1], True))
    before, grads = order[-1], list(grads)
    if chunks > 1:
        for distance in range(count - 1, 0, -1):
            early = count - 1 if distance < count - 1 else 1
            grads[distance], before[early] = lax.optimization_barrier(
                (grads[distance], before[early])
            )
    order.append(exchanged(grads, None))
    taps, before[:0:-1] = lax.optimization_barrier((jnp.concatenate(taps, axis=0), before[:0:-1]))
    taps = tree_sum(terms(taps, "dp", 1, 2))
    taps = terms(taps, "dp", 2, lax.axis_size("dp"), order[-1])
    return unpack(rank[None], taps, order[chunks:], count, chunks)


def solution(mesh):
    return jax.shard_map(
        on_device,
        mesh=mesh,
        in_specs=(
            P("dp", "seq", None),
            P("dp", "seq", None),
            P("dp", "seq", None),
            P("dp", "seq", None),
            P(),
            P(),
            P("dp"),
        ),
        out_specs=(
            P("dp", "seq", None),
            P("dp", "seq", None),
            P("dp", "seq", None),
            P(None, "seq"),
            P("seq"),
        ),
        check_vma=False,
    )
```

```python
import functools
import math

import jax
import jax.numpy as jnp
from jax import lax
from jax.experimental import pallas as pl
from jax.experimental.pallas import tpu as pltpu
from jax.sharding import PartitionSpec as P

HEADS = 16
KERNEL = 31
PAD = 16
masked_score = -1e30
VMEM = pl.BlockSpec(memory_space=pltpu.VMEM)
SMEM = pl.BlockSpec(memory_space=pltpu.SMEM)
LIMIT = 16 * 1024 * 1024
bf16, f32 = jnp.bfloat16, jnp.float32


def pack_kernel(count, chunks, rank_ref, *refs):
    arrays, outs, turned = refs[:4], refs[4:-1], refs[-1]
    rank = rank_ref[0]
    high = outs[0].shape[1]
    share = high * chunks
    for which, array in enumerate(arrays):
        turned[which] = array[0].T
        for distance in range(count):
            for chunk in range(chunks):
                first = pl.multiple_of((rank ^ distance) * share + chunk * high, 16)
                outs[chunk * count + distance][which] = turned[which, pl.ds(first, high), :]


def pack(rank, arrays, count, chunks):
    _, frames, width = arrays[0].shape
    high = width // count // chunks
    piece = jax.ShapeDtypeStruct((4, high, frames), bf16)
    outs = pl.pallas_call(
        functools.partial(pack_kernel, count, chunks),
        out_shape=(piece,) * (count * chunks),
        in_specs=[SMEM] + [VMEM] * 4,
        out_specs=(VMEM,) * (count * chunks),
        scratch_shapes=[pltpu.VMEM((4, width, frames), bf16)],
        compiler_params=pltpu.CompilerParams(vmem_limit_bytes=LIMIT),
        cost_estimate=pl.CostEstimate(
            flops=0, bytes_accessed=16 * frames * width, transcendentals=0
        ),
    )(rank, *[pltpu.with_memory_space_constraint(array, pltpu.HBM) for array in arrays])
    return [outs[chunk * count : (chunk + 1) * count] for chunk in range(chunks)]


def taken(count):
    return [0] + list(range(count - 1, 0, -1))


def unpack_kernel(count, chunks, rank_ref, *refs):
    pieces, refs = refs[: count * chunks], refs[count * chunks :]
    taps_refs, outs = refs[:-7], refs[-7:-4]
    weight_ref, bias_ref, bias_row, turned = refs[-4:]
    rank = rank_ref[0]
    high = pieces[0].shape[1]
    share = high * chunks
    for which, out in enumerate(outs):
        for chunk in range(chunks):
            for place, distance in enumerate(taken(count)):
                first = pl.multiple_of((rank ^ distance) * share + chunk * high, 16)
                turned[which, pl.ds(first, high), :] = pieces[chunk * count + place][which]
        out[0] = turned[which].T
    taps = taps_refs[0][...] + taps_refs[1][...]
    heads, _, depth = taps.shape
    for head in range(heads):
        at = slice(head * depth, (head + 1) * depth)
        weight_ref[:, at] = taps[head, :KERNEL]
        bias_row[:, at] = taps[head, KERNEL:]
    bias_ref[...] = bias_row[0]


def unpack(rank, taps, pieces, count, chunks):
    _, high, frames = pieces[0][0].shape
    width = high * count * chunks
    whole = jax.ShapeDtypeStruct((1, frames, width), bf16)
    return pl.pallas_call(
        functools.partial(unpack_kernel, count, chunks),
        out_shape=(whole,) * 3
        + (
            jax.ShapeDtypeStruct((KERNEL, width // count), f32),
            jax.ShapeDtypeStruct((width // count,), f32),
        ),
        in_specs=[SMEM] + [VMEM] * (count * chunks + len(taps)),
        out_specs=(VMEM,) * 5,
        scratch_shapes=[
            pltpu.VMEM((1, width // count), f32),
            pltpu.VMEM((3, width, frames), bf16),
        ],
        compiler_params=pltpu.CompilerParams(vmem_limit_bytes=LIMIT),
        cost_estimate=pl.CostEstimate(
            flops=0, bytes_accessed=12 * frames * width, transcendentals=0
        ),
    )(rank, *[part[distance] for part in pieces for distance in taken(count)], *taps)


def core_kernel(count, block, scalars, weight_ref, bias_ref, *refs):
    pieces, outs, taps_ref = refs[:count], refs[count : 2 * count], refs[2 * count]
    q_t, k_t, v_t, a_t, q_n, k_n, v_n, g_n, a_n, probs, shifted, padded = refs[2 * count + 1 :]
    heads, rows, depth = q_n.shape
    frames = pieces[0].shape[2]
    blocks = rows // block
    scale = 1.0 / math.sqrt(depth)
    log_scale = scale * math.log2(math.e)
    length, rank = scalars[0], scalars[1]

    def span(head):
        return slice(head * depth, (head + 1) * depth)

    for distance, piece in zip(taken(count), pieces):
        at = pl.ds(pl.multiple_of((rank ^ distance) * frames, 128), frames)
        q_t[:, at] = piece[0]
        k_t[:, at] = piece[1]
        v_t[:, at] = piece[2]
        for head in range(heads):
            q_n[head, at, :] = piece[0, span(head), :].T
            k_n[head, at, :] = piece[1, span(head), :].T
            v_n[head, at, :] = piece[2, span(head), :].T
            g_n[head, at, :] = piece[3, span(head), :].T

    def forward(index, head):
        cols = pl.ds(pl.multiple_of(index * block, block), block)
        scores = jnp.dot(k_n[head], q_t[span(head), cols], preferred_element_type=f32)
        key_at = lax.broadcasted_iota(jnp.int32, scores.shape, 0)
        scores = jnp.where(key_at < length, scores, masked_score)
        exped = jnp.exp2((scores - jnp.max(scores, axis=0, keepdims=True)) * log_scale)
        found = exped * (1.0 / jnp.sum(exped, axis=0, keepdims=True))
        probs[head, :, cols] = found
        out = jnp.dot(v_t[span(head), :], found.astype(bf16), preferred_element_type=f32)
        frame_at = index * block + lax.broadcasted_iota(jnp.int32, out.shape, 1)
        a_t[span(head), cols] = jnp.where(frame_at < length, out, 0.0).astype(bf16)

    def each_block(body):
        if blocks == 1:
            for head in range(heads):
                body(0, head)
        else:

            def step(index, carry):
                for head in range(heads):
                    body(index, head)
                return carry

            lax.fori_loop(0, blocks, step, 0)

    each_block(forward)

    tall = padded.shape[0]
    padded[0:PAD, :] = jnp.zeros((PAD, depth), f32)
    padded[PAD + rows : tall, :] = jnp.zeros((tall - PAD - rows, depth), f32)

    def shift_all():
        for s in range(8):
            shifted[s] = padded[s : s + tall - 8, :].reshape(tall // 8 - 1, 8, depth)

    step_tiles = 8
    step_rows = 8 * step_tiles

    def window(index, offset):
        return shifted[offset % 8, pl.ds(index * step_tiles + offset // 8, step_tiles)]

    def filtered(head, index, reverse):
        total = None
        for offset in range(1, KERNEL + 1):
            tap = KERNEL - offset if reverse else offset - 1
            term = weight_ref[head, tap : tap + 1, :] * window(index, offset)
            total = term if total is None else total + term
        return total

    def loaded(ref, index):
        at = pl.ds(pl.multiple_of(index * step_rows, step_rows), step_rows)
        return ref[at, :].astype(f32).reshape(step_tiles, 8, depth)

    for head in range(heads):
        for first in range(0, rows, frames):
            at = slice(PAD + first, PAD + first + frames)
            padded[at, :] = a_t[span(head), first : first + frames].T.astype(f32)
        shift_all()

        def conv_step(index, carry, head=head):
            conv_pre = filtered(head, index, False) + bias_ref[head]
            sig = 1.0 / (1.0 + jnp.exp(-conv_pre))
            pre = loaded(g_n.at[head], index) * (sig * (1.0 + conv_pre * (1.0 - sig)))
            pre = pre.astype(bf16).astype(f32)
            at = pl.ds(pl.multiple_of(PAD + index * step_rows, PAD), step_rows)
            padded[at, :] = pre.reshape(step_rows, depth)
            new = []
            for offset in range(1, KERNEL + 1):
                new.append(carry[offset - 1] + jnp.sum(pre * window(index, offset), axis=0))
            new.append(carry[KERNEL] + jnp.sum(pre, axis=0))
            return tuple(new)

        zero = jnp.zeros((8, depth), f32)
        sums = lax.fori_loop(0, rows // step_rows, conv_step, (zero,) * (KERNEL + 1))
        for tap in range(KERNEL + 1):
            taps_ref[head, tap : tap + 1, :] = jnp.sum(sums[tap], axis=0, keepdims=True)
        shift_all()

        def back_step(index, carry, head=head):
            total = loaded(g_n.at[head], index) + filtered(head, index, True)
            total = total.reshape(step_rows, depth)
            frame_at = index * step_rows + lax.broadcasted_iota(jnp.int32, total.shape, 0)
            total = jnp.where(frame_at < length, total, 0.0)
            at = pl.ds(pl.multiple_of(index * step_rows, step_rows), step_rows)
            a_n[head, at, :] = total.astype(bf16)
            return carry

        lax.fori_loop(0, rows // step_rows, back_step, 0)
        for first in range(0, rows, frames):
            a_t[span(head), first : first + frames] = a_n[head, first : first + frames, :].T

    def backward(index, head):
        cols = pl.ds(pl.multiple_of(index * block, block), block)
        score_grad = jnp.dot(v_n[head], a_t[span(head), cols], preferred_element_type=f32)
        found = probs[head, :, cols]
        delta = jnp.sum(found * score_grad, axis=0, keepdims=True)
        diff = (found * (score_grad - delta)).astype(bf16)
        value = jnp.dot(found.astype(bf16), a_n[head, cols, :], preferred_element_type=f32)
        key = jnp.dot(diff, q_n[head, cols, :], preferred_element_type=f32)
        query = jnp.dot(k_t[span(head), :], diff, preferred_element_type=f32)
        q_t[span(head), cols] = (query * scale).astype(bf16)
        return key, value

    def finish(head, key, value):
        for first in range(0, rows, frames):
            at = slice(first, first + frames)
            k_t[span(head), at] = (key[at, :] * scale).astype(bf16).T
            v_t[span(head), at] = value[at, :].astype(bf16).T

    for head in range(heads):
        if blocks == 1:
            finish(head, *backward(0, head))
        else:
            zeros = jnp.zeros((rows, depth), f32)

            def step(index, carry, head=head):
                key, value = backward(index, head)
                return carry[0] + key, carry[1] + value

            finish(head, *lax.fori_loop(0, blocks, step, (zeros, zeros)))

    for distance, out in enumerate(outs):
        at = pl.ds(pl.multiple_of((rank ^ distance) * frames, 128), frames)
        out[0] = q_t[:, at]
        out[1] = k_t[:, at]
        out[2] = v_t[:, at]


def core(scalars, weight, bias, pieces):
    count = len(pieces)
    _, high, frames = pieces[0].shape
    heads, _, depth = weight.shape
    rows = count * frames
    block = math.gcd(rows, 512)
    tall = rows + 2 * PAD + 8
    piece = jax.ShapeDtypeStruct((3, high, frames), bf16)
    turned = pltpu.VMEM((high, rows), bf16)
    plain = pltpu.VMEM((heads, rows, depth), bf16)
    outs = pl.pallas_call(
        functools.partial(core_kernel, count, block),
        out_shape=(piece,) * count + (jax.ShapeDtypeStruct((heads, KERNEL + 1, depth), f32),),
        in_specs=[SMEM] + [VMEM] * (2 + count),
        out_specs=(VMEM,) * (count + 1),
        scratch_shapes=[turned] * 4
        + [plain] * 5
        + [
            pltpu.VMEM((heads, rows, rows), f32),
            pltpu.VMEM((8, tall // 8 - 1, 8, depth), f32),
            pltpu.VMEM((tall, depth), f32),
        ],
        compiler_params=pltpu.CompilerParams(
            vmem_limit_bytes=12 * 2**20 + 8 * heads * rows * rows + 4096 * tall
        ),
        cost_estimate=pl.CostEstimate(
            flops=24 * rows * rows * high,
            bytes_accessed=14 * rows * high,
            transcendentals=heads * rows * rows,
        ),
    )(scalars, weight, bias, *[pieces[distance] for distance in taken(count)])
    return outs[:count], outs[count]


def exchanged(pieces, before, eager=False):
    pieces = list(pieces)
    last = len(pieces) - 1
    if before is not None and eager:
        pieces[last], before[last] = lax.optimization_barrier((pieces[last], before[last]))
    if before is not None and last > 1:
        wait = slice(last - 1 if eager else last, 1, -1)
        pieces[wait], before[:0:-1] = lax.optimization_barrier((pieces[wait], before[:0:-1]))
    moved = pieces[:1] * len(pieces)
    for distance in range(len(pieces) - 1, 0, -1):
        pairs = [(i, i ^ distance) for i in range(len(pieces))]
        moved[distance] = lax.ppermute(pieces[distance], "seq", pairs)
    return moved


def doubled(array, axis):
    count = lax.axis_size(axis)
    pair, distance = (array, jnp.zeros_like(array)), 1
    while distance < count:
        total = array if distance == 1 else pair[0] + pair[1]
        pairs = [(i, i ^ distance) for i in range(count)]
        pair = (total, lax.ppermute(total, axis, pairs))
        distance *= 2
    return pair


def on_device(queries, keys, values, grad_out, conv_weight, conv_bias, lengths):
    count = lax.axis_size("seq")
    rank = lax.axis_index("seq").astype(jnp.int32)
    width = queries.shape[2]
    depth = width // HEADS
    heads = HEADS // count
    chunks = math.gcd(heads, 2)
    step = heads // chunks
    by_head = conv_weight.reshape(KERNEL, HEADS, depth).transpose(1, 0, 2)
    weight = lax.dynamic_slice_in_dim(by_head, rank * heads, heads, axis=0)
    bias = lax.dynamic_slice_in_dim(conv_bias.reshape(HEADS, 1, depth), rank * heads, heads, axis=0)
    scalars = jnp.stack([lengths[0], rank])
    sent = pack(rank[None], (queries, keys, values, grad_out), count, chunks)
    order = []
    for pieces in sent:
        order.append(exchanged(pieces, order[-1] if order else None))
    taps = []
    for chunk in range(chunks):
        at = slice(chunk * step, (chunk + 1) * step)
        grads, part = core(scalars, weight[at], bias[at], order[chunk])
        taps.append(part)
        if chunk < chunks - 1:
            order.append(exchanged(grads, order[-1], True))
    before, grads, taps = order[-1], list(grads), jnp.concatenate(taps, axis=0)
    last = count - 1
    grads[last], before[1] = lax.optimization_barrier((grads[last], before[1]))
    if last > 2:
        (grads[last - 1], taps), before[last] = lax.optimization_barrier(
            ((grads[last - 1], taps), before[last])
        )
        grads[1], before[last - 1] = lax.optimization_barrier((grads[1], before[last - 1]))
    order.append(exchanged(grads, None))
    return unpack(rank[None], doubled(taps, "dp"), order[chunks:], count, chunks)


def solution(mesh):
    return jax.shard_map(
        on_device,
        mesh=mesh,
        in_specs=(
            P("dp", "seq", None),
            P("dp", "seq", None),
            P("dp", "seq", None),
            P("dp", "seq", None),
            P(),
            P(),
            P("dp"),
        ),
        out_specs=(
            P("dp", "seq", None),
            P("dp", "seq", None),
            P("dp", "seq", None),
            P(None, "seq"),
            P("seq"),
        ),
        check_vma=False,
    )
```

```python
import functools
import math

import jax
import jax.numpy as jnp
from jax import lax
from jax.experimental import pallas as pl
from jax.experimental.pallas import tpu as pltpu
from jax.sharding import PartitionSpec as P

HEADS = 16
KERNEL = 31
PAD = 16
masked_score = -1e30
VMEM = pl.BlockSpec(memory_space=pltpu.VMEM)
SMEM = pl.BlockSpec(memory_space=pltpu.SMEM)
LIMIT = 16 * 1024 * 1024
bf16, f32 = jnp.bfloat16, jnp.float32


def pack_kernel(count, chunks, rank_ref, *refs):
    arrays, outs, turned = refs[:4], refs[4:-1], refs[-1]
    rank = rank_ref[0]
    high = outs[0].shape[1]
    share = high * chunks
    for which, array in enumerate(arrays):
        turned[which] = array[0].T
        for distance in range(count):
            for chunk in range(chunks):
                first = pl.multiple_of((rank ^ distance) * share + chunk * high, 16)
                outs[chunk * count + distance][which] = turned[which, pl.ds(first, high), :]


def pack(rank, arrays, count, chunks):
    _, frames, width = arrays[0].shape
    high = width // count // chunks
    piece = jax.ShapeDtypeStruct((4, high, frames), bf16)
    outs = pl.pallas_call(
        functools.partial(pack_kernel, count, chunks),
        out_shape=(piece,) * (count * chunks),
        in_specs=[SMEM] + [VMEM] * 4,
        out_specs=(VMEM,) * (count * chunks),
        scratch_shapes=[pltpu.VMEM((4, width, frames), bf16)],
        compiler_params=pltpu.CompilerParams(vmem_limit_bytes=LIMIT),
        cost_estimate=pl.CostEstimate(
            flops=0, bytes_accessed=16 * frames * width, transcendentals=0
        ),
    )(rank, *[pltpu.with_memory_space_constraint(array, pltpu.HBM) for array in arrays])
    return [outs[chunk * count : (chunk + 1) * count] for chunk in range(chunks)]


def taken(count):
    return [0] + list(range(count - 1, 0, -1))


def unpack_kernel(count, chunks, rank_ref, *refs):
    pieces, refs = refs[: count * chunks], refs[count * chunks :]
    taps_refs, outs = refs[:-7], refs[-7:-4]
    weight_ref, bias_ref, bias_row, turned = refs[-4:]
    rank = rank_ref[0]
    high = pieces[0].shape[1]
    share = high * chunks
    for which, out in enumerate(outs):
        for chunk in range(chunks):
            for place, distance in enumerate(taken(count)):
                first = pl.multiple_of((rank ^ distance) * share + chunk * high, 16)
                turned[which, pl.ds(first, high), :] = pieces[chunk * count + place][which]
        out[0] = turned[which].T
    taps = taps_refs[0][...] + taps_refs[1][...]
    heads, _, depth = taps.shape
    for head in range(heads):
        at = slice(head * depth, (head + 1) * depth)
        weight_ref[:, at] = taps[head, :KERNEL]
        bias_row[:, at] = taps[head, KERNEL:]
    bias_ref[...] = bias_row[0]


def unpack(rank, taps, pieces, count, chunks):
    _, high, frames = pieces[0][0].shape
    width = high * count * chunks
    whole = jax.ShapeDtypeStruct((1, frames, width), bf16)
    return pl.pallas_call(
        functools.partial(unpack_kernel, count, chunks),
        out_shape=(whole,) * 3
        + (
            jax.ShapeDtypeStruct((KERNEL, width // count), f32),
            jax.ShapeDtypeStruct((width // count,), f32),
        ),
        in_specs=[SMEM] + [VMEM] * (count * chunks + len(taps)),
        out_specs=(VMEM,) * 5,
        scratch_shapes=[
            pltpu.VMEM((1, width // count), f32),
            pltpu.VMEM((3, width, frames), bf16),
        ],
        compiler_params=pltpu.CompilerParams(vmem_limit_bytes=LIMIT),
        cost_estimate=pl.CostEstimate(
            flops=0, bytes_accessed=12 * frames * width, transcendentals=0
        ),
    )(rank, *[part[distance] for part in pieces for distance in taken(count)], *taps)


def core_kernel(count, block, scalars, weight_ref, bias_ref, *refs):
    pieces, outs, taps_ref = refs[:count], refs[count : 2 * count], refs[2 * count]
    q_t, k_t, v_t, a_t, q_n, k_n, v_n, g_n, a_n, probs, shifted, padded = refs[2 * count + 1 :]
    heads, rows, depth = q_n.shape
    frames = pieces[0].shape[2]
    blocks = rows // block
    scale = 1.0 / math.sqrt(depth)
    log_scale = scale * math.log2(math.e)
    length, rank = scalars[0], scalars[1]

    def span(head):
        return slice(head * depth, (head + 1) * depth)

    for distance, piece in zip(taken(count), pieces):
        at = pl.ds(pl.multiple_of((rank ^ distance) * frames, 128), frames)
        q_t[:, at] = piece[0]
        k_t[:, at] = piece[1]
        v_t[:, at] = piece[2]
        for head in range(heads):
            q_n[head, at, :] = piece[0, span(head), :].T
            k_n[head, at, :] = piece[1, span(head), :].T
            v_n[head, at, :] = piece[2, span(head), :].T
            g_n[head, at, :] = piece[3, span(head), :].T

    def forward(index, head):
        cols = pl.ds(pl.multiple_of(index * block, block), block)
        scores = jnp.dot(k_n[head], q_t[span(head), cols], preferred_element_type=f32)
        key_at = lax.broadcasted_iota(jnp.int32, scores.shape, 0)
        scores = jnp.where(key_at < length, scores, masked_score)
        exped = jnp.exp2((scores - jnp.max(scores, axis=0, keepdims=True)) * log_scale)
        found = exped * (1.0 / jnp.sum(exped, axis=0, keepdims=True))
        probs[head, :, cols] = found
        out = jnp.dot(v_t[span(head), :], found.astype(bf16), preferred_element_type=f32)
        frame_at = index * block + lax.broadcasted_iota(jnp.int32, out.shape, 1)
        a_t[span(head), cols] = jnp.where(frame_at < length, out, 0.0).astype(bf16)

    def each_block(body):
        if blocks == 1:
            for head in range(heads):
                body(0, head)
        else:

            def step(index, carry):
                for head in range(heads):
                    body(index, head)
                return carry

            lax.fori_loop(0, blocks, step, 0)

    each_block(forward)

    tall = padded.shape[0]
    padded[0:PAD, :] = jnp.zeros((PAD, depth), f32)
    padded[PAD + rows : tall, :] = jnp.zeros((tall - PAD - rows, depth), f32)

    def shift_all():
        for s in range(8):
            shifted[s] = padded[s : s + tall - 8, :].reshape(tall // 8 - 1, 8, depth)

    step_tiles = 8
    step_rows = 8 * step_tiles

    def window(index, offset):
        return shifted[offset % 8, pl.ds(index * step_tiles + offset // 8, step_tiles)]

    def filtered(head, index, reverse):
        total = None
        for offset in range(1, KERNEL + 1):
            tap = KERNEL - offset if reverse else offset - 1
            term = weight_ref[head, tap : tap + 1, :] * window(index, offset)
            total = term if total is None else total + term
        return total

    def loaded(ref, index):
        at = pl.ds(pl.multiple_of(index * step_rows, step_rows), step_rows)
        return ref[at, :].astype(f32).reshape(step_tiles, 8, depth)

    for head in range(heads):
        for first in range(0, rows, frames):
            at = slice(PAD + first, PAD + first + frames)
            padded[at, :] = a_t[span(head), first : first + frames].T.astype(f32)
        shift_all()

        def conv_step(index, carry, head=head):
            conv_pre = filtered(head, index, False) + bias_ref[head]
            sig = 1.0 / (1.0 + jnp.exp(-conv_pre))
            pre = loaded(g_n.at[head], index) * (sig * (1.0 + conv_pre * (1.0 - sig)))
            pre = pre.astype(bf16).astype(f32)
            at = pl.ds(pl.multiple_of(PAD + index * step_rows, PAD), step_rows)
            padded[at, :] = pre.reshape(step_rows, depth)
            new = []
            for offset in range(1, KERNEL + 1):
                new.append(carry[offset - 1] + jnp.sum(pre * window(index, offset), axis=0))
            new.append(carry[KERNEL] + jnp.sum(pre, axis=0))
            return tuple(new)

        zero = jnp.zeros((8, depth), f32)
        sums = lax.fori_loop(0, rows // step_rows, conv_step, (zero,) * (KERNEL + 1))
        for tap in range(KERNEL + 1):
            taps_ref[head, tap : tap + 1, :] = jnp.sum(sums[tap], axis=0, keepdims=True)
        shift_all()

        def back_step(index, carry, head=head):
            total = loaded(g_n.at[head], index) + filtered(head, index, True)
            total = total.reshape(step_rows, depth)
            frame_at = index * step_rows + lax.broadcasted_iota(jnp.int32, total.shape, 0)
            total = jnp.where(frame_at < length, total, 0.0)
            at = pl.ds(pl.multiple_of(index * step_rows, step_rows), step_rows)
            a_n[head, at, :] = total.astype(bf16)
            return carry

        lax.fori_loop(0, rows // step_rows, back_step, 0)
        for first in range(0, rows, frames):
            a_t[span(head), first : first + frames] = a_n[head, first : first + frames, :].T

    def backward(index, head):
        cols = pl.ds(pl.multiple_of(index * block, block), block)
        score_grad = jnp.dot(v_n[head], a_t[span(head), cols], preferred_element_type=f32)
        found = probs[head, :, cols]
        delta = jnp.sum(found * score_grad, axis=0, keepdims=True)
        diff = (found * (score_grad - delta)).astype(bf16)
        value = jnp.dot(found.astype(bf16), a_n[head, cols, :], preferred_element_type=f32)
        key = jnp.dot(diff, q_n[head, cols, :], preferred_element_type=f32)
        query = jnp.dot(k_t[span(head), :], diff, preferred_element_type=f32)
        q_t[span(head), cols] = (query * scale).astype(bf16)
        return key, value

    def finish(head, key, value):
        for first in range(0, rows, frames):
            at = slice(first, first + frames)
            k_t[span(head), at] = (key[at, :] * scale).astype(bf16).T
            v_t[span(head), at] = value[at, :].astype(bf16).T

    for head in range(heads):
        if blocks == 1:
            finish(head, *backward(0, head))
        else:
            zeros = jnp.zeros((rows, depth), f32)

            def step(index, carry, head=head):
                key, value = backward(index, head)
                return carry[0] + key, carry[1] + value

            finish(head, *lax.fori_loop(0, blocks, step, (zeros, zeros)))

    for distance, out in enumerate(outs):
        at = pl.ds(pl.multiple_of((rank ^ distance) * frames, 128), frames)
        out[0] = q_t[:, at]
        out[1] = k_t[:, at]
        out[2] = v_t[:, at]


def core(scalars, weight, bias, pieces):
    count = len(pieces)
    _, high, frames = pieces[0].shape
    heads, _, depth = weight.shape
    rows = count * frames
    block = math.gcd(rows, 512)
    tall = rows + 2 * PAD + 8
    piece = jax.ShapeDtypeStruct((3, high, frames), bf16)
    turned = pltpu.VMEM((high, rows), bf16)
    plain = pltpu.VMEM((heads, rows, depth), bf16)
    outs = pl.pallas_call(
        functools.partial(core_kernel, count, block),
        out_shape=(piece,) * count + (jax.ShapeDtypeStruct((heads, KERNEL + 1, depth), f32),),
        in_specs=[SMEM] + [VMEM] * (2 + count),
        out_specs=(VMEM,) * (count + 1),
        scratch_shapes=[turned] * 4
        + [plain] * 5
        + [
            pltpu.VMEM((heads, rows, rows), f32),
            pltpu.VMEM((8, tall // 8 - 1, 8, depth), f32),
            pltpu.VMEM((tall, depth), f32),
        ],
        compiler_params=pltpu.CompilerParams(
            vmem_limit_bytes=12 * 2**20 + 8 * heads * rows * rows + 4096 * tall
        ),
        cost_estimate=pl.CostEstimate(
            flops=24 * rows * rows * high,
            bytes_accessed=14 * rows * high,
            transcendentals=heads * rows * rows,
        ),
    )(scalars, weight, bias, *[pieces[distance] for distance in taken(count)])
    return outs[:count], outs[count]


def exchanged(pieces, before):
    pieces = list(pieces)
    if before is not None and len(pieces) > 2:
        pieces[:1:-1], before[:0:-1] = lax.optimization_barrier((pieces[:1:-1], before[:0:-1]))
    moved = pieces[:1] * len(pieces)
    for distance in range(len(pieces) - 1, 0, -1):
        pairs = [(i, i ^ distance) for i in range(len(pieces))]
        moved[distance] = lax.ppermute(pieces[distance], "seq", pairs)
    return moved


def doubled(array, axis):
    count = lax.axis_size(axis)
    pair, distance = (array, jnp.zeros_like(array)), 1
    while distance < count:
        total = array if distance == 1 else pair[0] + pair[1]
        pairs = [(i, i ^ distance) for i in range(count)]
        pair = (total, lax.ppermute(total, axis, pairs))
        distance *= 2
    return pair


def on_device(queries, keys, values, grad_out, conv_weight, conv_bias, lengths):
    count = lax.axis_size("seq")
    rank = lax.axis_index("seq").astype(jnp.int32)
    width = queries.shape[2]
    depth = width // HEADS
    heads = HEADS // count
    chunks = math.gcd(heads, 2)
    step = heads // chunks
    by_head = conv_weight.reshape(KERNEL, HEADS, depth).transpose(1, 0, 2)
    weight = lax.dynamic_slice_in_dim(by_head, rank * heads, heads, axis=0)
    bias = lax.dynamic_slice_in_dim(conv_bias.reshape(HEADS, 1, depth), rank * heads, heads, axis=0)
    scalars = jnp.stack([lengths[0], rank])
    sent = pack(rank[None], (queries, keys, values, grad_out), count, chunks)
    order = []
    for pieces in sent:
        order.append(exchanged(pieces, order[-1] if order else None))
    taps = []
    for chunk in range(chunks):
        at = slice(chunk * step, (chunk + 1) * step)
        grads, part = core(scalars, weight[at], bias[at], order[chunk])
        taps.append(part)
        if chunk < chunks - 1:
            order.append(exchanged(grads, order[-1]))
    before, grads, taps = order[-1], list(grads), jnp.concatenate(taps, axis=0)
    last = count - 1
    grads[last], before[1] = lax.optimization_barrier((grads[last], before[1]))
    if last > 2:
        (grads[last - 1], taps), before[last] = lax.optimization_barrier(
            ((grads[last - 1], taps), before[last])
        )
        grads[1], before[last - 1] = lax.optimization_barrier((grads[1], before[last - 1]))
    order.append(exchanged(grads, None))
    return unpack(rank[None], doubled(taps, "dp"), order[chunks:], count, chunks)


def solution(mesh):
    return jax.shard_map(
        on_device,
        mesh=mesh,
        in_specs=(
            P("dp", "seq", None),
            P("dp", "seq", None),
            P("dp", "seq", None),
            P("dp", "seq", None),
            P(),
            P(),
            P("dp"),
        ),
        out_specs=(
            P("dp", "seq", None),
            P("dp", "seq", None),
            P("dp", "seq", None),
            P(None, "seq"),
            P("seq"),
        ),
        check_vma=False,
    )
```

```python
import functools
import math

import jax
import jax.numpy as jnp
from jax import lax
from jax.experimental import pallas as pl
from jax.experimental.pallas import tpu as pltpu
from jax.sharding import PartitionSpec as P

HEADS = 16
KERNEL = 31
PAD = 16
masked_score = -1e30
VMEM = pl.BlockSpec(memory_space=pltpu.VMEM)
SMEM = pl.BlockSpec(memory_space=pltpu.SMEM)
LIMIT = 16 * 1024 * 1024
bf16, f32 = jnp.bfloat16, jnp.float32


def pack_kernel(count, chunks, rank_ref, *refs):
    arrays, outs, turned = refs[:4], refs[4:-1], refs[-1]
    rank = rank_ref[0]
    high = outs[0].shape[1]
    share = high * chunks
    for which, array in enumerate(arrays):
        turned[which] = array[0].T
        for distance in range(count):
            for chunk in range(chunks):
                first = pl.multiple_of((rank ^ distance) * share + chunk * high, 16)
                outs[chunk * count + distance][which] = turned[which, pl.ds(first, high), :]


def pack(rank, arrays, count, chunks):
    _, frames, width = arrays[0].shape
    high = width // count // chunks
    piece = jax.ShapeDtypeStruct((4, high, frames), bf16)
    outs = pl.pallas_call(
        functools.partial(pack_kernel, count, chunks),
        out_shape=(piece,) * (count * chunks),
        in_specs=[SMEM] + [VMEM] * 4,
        out_specs=(VMEM,) * (count * chunks),
        scratch_shapes=[pltpu.VMEM((4, width, frames), bf16)],
        compiler_params=pltpu.CompilerParams(vmem_limit_bytes=LIMIT),
        cost_estimate=pl.CostEstimate(
            flops=0, bytes_accessed=16 * frames * width, transcendentals=0
        ),
    )(rank, *[pltpu.with_memory_space_constraint(array, pltpu.HBM) for array in arrays])
    return [outs[chunk * count : (chunk + 1) * count] for chunk in range(chunks)]


def taken(count):
    return [0] + list(range(count - 1, 0, -1))


def unpack_kernel(count, chunks, rank_ref, *refs):
    pieces, refs = refs[: count * chunks], refs[count * chunks :]
    taps_refs, outs = refs[:-7], refs[-7:-4]
    weight_ref, bias_ref, bias_row, turned = refs[-4:]
    rank = rank_ref[0]
    high = pieces[0].shape[1]
    share = high * chunks
    for which, out in enumerate(outs):
        for chunk in range(chunks):
            for place, distance in enumerate(taken(count)):
                first = pl.multiple_of((rank ^ distance) * share + chunk * high, 16)
                turned[which, pl.ds(first, high), :] = pieces[chunk * count + place][which]
        out[0] = turned[which].T
    taps = taps_refs[0][...] + taps_refs[1][...]
    heads, _, depth = taps.shape
    for head in range(heads):
        at = slice(head * depth, (head + 1) * depth)
        weight_ref[:, at] = taps[head, :KERNEL]
        bias_row[:, at] = taps[head, KERNEL:]
    bias_ref[...] = bias_row[0]


def unpack(rank, taps, pieces, count, chunks):
    _, high, frames = pieces[0][0].shape
    width = high * count * chunks
    whole = jax.ShapeDtypeStruct((1, frames, width), bf16)
    return pl.pallas_call(
        functools.partial(unpack_kernel, count, chunks),
        out_shape=(whole,) * 3
        + (
            jax.ShapeDtypeStruct((KERNEL, width // count), f32),
            jax.ShapeDtypeStruct((width // count,), f32),
        ),
        in_specs=[SMEM] + [VMEM] * (count * chunks + len(taps)),
        out_specs=(VMEM,) * 5,
        scratch_shapes=[
            pltpu.VMEM((1, width // count), f32),
            pltpu.VMEM((3, width, frames), bf16),
        ],
        compiler_params=pltpu.CompilerParams(vmem_limit_bytes=LIMIT),
        cost_estimate=pl.CostEstimate(
            flops=0, bytes_accessed=12 * frames * width, transcendentals=0
        ),
    )(rank, *[part[distance] for part in pieces for distance in taken(count)], *taps)


def core_kernel(count, block, scalars, weight_ref, bias_ref, *refs):
    pieces, outs, taps_ref = refs[:count], refs[count : 2 * count], refs[2 * count]
    q_t, k_t, v_t, a_t, q_n, k_n, v_n, g_n, a_n, probs, shifted, padded = refs[2 * count + 1 :]
    heads, rows, depth = q_n.shape
    frames = pieces[0].shape[2]
    blocks = rows // block
    scale = 1.0 / math.sqrt(depth)
    log_scale = scale * math.log2(math.e)
    length, rank = scalars[0], scalars[1]

    def span(head):
        return slice(head * depth, (head + 1) * depth)

    for distance, piece in zip(taken(count), pieces):
        at = pl.ds(pl.multiple_of((rank ^ distance) * frames, 128), frames)
        q_t[:, at] = piece[0]
        k_t[:, at] = piece[1]
        v_t[:, at] = piece[2]
        for head in range(heads):
            q_n[head, at, :] = piece[0, span(head), :].T
            k_n[head, at, :] = piece[1, span(head), :].T
            v_n[head, at, :] = piece[2, span(head), :].T
            g_n[head, at, :] = piece[3, span(head), :].T

    def forward(index, head):
        cols = pl.ds(pl.multiple_of(index * block, block), block)
        scores = jnp.dot(k_n[head], q_t[span(head), cols], preferred_element_type=f32)
        key_at = lax.broadcasted_iota(jnp.int32, scores.shape, 0)
        scores = jnp.where(key_at < length, scores, masked_score)
        exped = jnp.exp2((scores - jnp.max(scores, axis=0, keepdims=True)) * log_scale)
        found = exped * (1.0 / jnp.sum(exped, axis=0, keepdims=True))
        probs[head, :, cols] = found
        out = jnp.dot(v_t[span(head), :], found.astype(bf16), preferred_element_type=f32)
        frame_at = index * block + lax.broadcasted_iota(jnp.int32, out.shape, 1)
        a_t[span(head), cols] = jnp.where(frame_at < length, out, 0.0).astype(bf16)

    def each_block(body):
        if blocks == 1:
            for head in range(heads):
                body(0, head)
        else:

            def step(index, carry):
                for head in range(heads):
                    body(index, head)
                return carry

            lax.fori_loop(0, blocks, step, 0)

    each_block(forward)

    tall = padded.shape[0]
    padded[0:PAD, :] = jnp.zeros((PAD, depth), f32)
    padded[PAD + rows : tall, :] = jnp.zeros((tall - PAD - rows, depth), f32)

    def shift_all():
        for s in range(8):
            shifted[s] = padded[s : s + tall - 8, :].reshape(tall // 8 - 1, 8, depth)

    step_tiles = 8
    step_rows = 8 * step_tiles

    def window(index, offset):
        return shifted[offset % 8, pl.ds(index * step_tiles + offset // 8, step_tiles)]

    def filtered(head, index, reverse):
        total = None
        for offset in range(1, KERNEL + 1):
            tap = KERNEL - offset if reverse else offset - 1
            term = weight_ref[head, tap : tap + 1, :] * window(index, offset)
            total = term if total is None else total + term
        return total

    def loaded(ref, index):
        at = pl.ds(pl.multiple_of(index * step_rows, step_rows), step_rows)
        return ref[at, :].astype(f32).reshape(step_tiles, 8, depth)

    for head in range(heads):
        for first in range(0, rows, frames):
            at = slice(PAD + first, PAD + first + frames)
            padded[at, :] = a_t[span(head), first : first + frames].T.astype(f32)
        shift_all()

        def conv_step(index, carry, head=head):
            conv_pre = filtered(head, index, False) + bias_ref[head]
            sig = 1.0 / (1.0 + jnp.exp(-conv_pre))
            pre = loaded(g_n.at[head], index) * (sig * (1.0 + conv_pre * (1.0 - sig)))
            pre = pre.astype(bf16).astype(f32)
            at = pl.ds(pl.multiple_of(PAD + index * step_rows, PAD), step_rows)
            padded[at, :] = pre.reshape(step_rows, depth)
            new = []
            for offset in range(1, KERNEL + 1):
                new.append(carry[offset - 1] + jnp.sum(pre * window(index, offset), axis=0))
            new.append(carry[KERNEL] + jnp.sum(pre, axis=0))
            return tuple(new)

        zero = jnp.zeros((8, depth), f32)
        sums = lax.fori_loop(0, rows // step_rows, conv_step, (zero,) * (KERNEL + 1))
        for tap in range(KERNEL + 1):
            taps_ref[head, tap : tap + 1, :] = jnp.sum(sums[tap], axis=0, keepdims=True)
        shift_all()

        def back_step(index, carry, head=head):
            total = loaded(g_n.at[head], index) + filtered(head, index, True)
            total = total.reshape(step_rows, depth)
            frame_at = index * step_rows + lax.broadcasted_iota(jnp.int32, total.shape, 0)
            total = jnp.where(frame_at < length, total, 0.0)
            at = pl.ds(pl.multiple_of(index * step_rows, step_rows), step_rows)
            a_n[head, at, :] = total.astype(bf16)
            return carry

        lax.fori_loop(0, rows // step_rows, back_step, 0)
        for first in range(0, rows, frames):
            a_t[span(head), first : first + frames] = a_n[head, first : first + frames, :].T

    def backward(index, head):
        cols = pl.ds(pl.multiple_of(index * block, block), block)
        score_grad = jnp.dot(v_n[head], a_t[span(head), cols], preferred_element_type=f32)
        found = probs[head, :, cols]
        delta = jnp.sum(found * score_grad, axis=0, keepdims=True)
        diff = (found * (score_grad - delta)).astype(bf16)
        value = jnp.dot(found.astype(bf16), a_n[head, cols, :], preferred_element_type=f32)
        key = jnp.dot(diff, q_n[head, cols, :], preferred_element_type=f32)
        query = jnp.dot(k_t[span(head), :], diff, preferred_element_type=f32)
        q_t[span(head), cols] = (query * scale).astype(bf16)
        return key, value

    def finish(head, key, value):
        for first in range(0, rows, frames):
            at = slice(first, first + frames)
            k_t[span(head), at] = (key[at, :] * scale).astype(bf16).T
            v_t[span(head), at] = value[at, :].astype(bf16).T

    for head in range(heads):
        if blocks == 1:
            finish(head, *backward(0, head))
        else:
            zeros = jnp.zeros((rows, depth), f32)

            def step(index, carry, head=head):
                key, value = backward(index, head)
                return carry[0] + key, carry[1] + value

            finish(head, *lax.fori_loop(0, blocks, step, (zeros, zeros)))

    for distance, out in enumerate(outs):
        at = pl.ds(pl.multiple_of((rank ^ distance) * frames, 128), frames)
        out[0] = q_t[:, at]
        out[1] = k_t[:, at]
        out[2] = v_t[:, at]


def core(scalars, weight, bias, pieces):
    count = len(pieces)
    _, high, frames = pieces[0].shape
    heads, _, depth = weight.shape
    rows = count * frames
    block = math.gcd(rows, 512)
    tall = rows + 2 * PAD + 8
    piece = jax.ShapeDtypeStruct((3, high, frames), bf16)
    turned = pltpu.VMEM((high, rows), bf16)
    plain = pltpu.VMEM((heads, rows, depth), bf16)
    outs = pl.pallas_call(
        functools.partial(core_kernel, count, block),
        out_shape=(piece,) * count + (jax.ShapeDtypeStruct((heads, KERNEL + 1, depth), f32),),
        in_specs=[SMEM] + [VMEM] * (2 + count),
        out_specs=(VMEM,) * (count + 1),
        scratch_shapes=[turned] * 4
        + [plain] * 5
        + [
            pltpu.VMEM((heads, rows, rows), f32),
            pltpu.VMEM((8, tall // 8 - 1, 8, depth), f32),
            pltpu.VMEM((tall, depth), f32),
        ],
        compiler_params=pltpu.CompilerParams(
            vmem_limit_bytes=12 * 2**20 + 8 * heads * rows * rows + 4096 * tall
        ),
        cost_estimate=pl.CostEstimate(
            flops=24 * rows * rows * high,
            bytes_accessed=14 * rows * high,
            transcendentals=heads * rows * rows,
        ),
    )(scalars, weight, bias, *[pieces[distance] for distance in taken(count)])
    return outs[:count], outs[count]


def exchanged(pieces, before, eager=False):
    pieces = list(pieces)
    last = len(pieces) - 1
    if before is not None and eager:
        pieces[last], before[last] = lax.optimization_barrier((pieces[last], before[last]))
    if before is not None and last > 1:
        wait = slice(last - 1 if eager else last, 1, -1)
        pieces[wait], before[:0:-1] = lax.optimization_barrier((pieces[wait], before[:0:-1]))
    moved = pieces[:1] * len(pieces)
    for distance in range(len(pieces) - 1, 0, -1):
        pairs = [(i, i ^ distance) for i in range(len(pieces))]
        moved[distance] = lax.ppermute(pieces[distance], "seq", pairs)
    return moved


def doubled(array, axis):
    count = lax.axis_size(axis)
    pair, distance = (array, jnp.zeros_like(array)), 1
    while distance < count:
        total = array if distance == 1 else pair[0] + pair[1]
        pairs = [(i, i ^ distance) for i in range(count)]
        pair = (total, lax.ppermute(total, axis, pairs))
        distance *= 2
    return pair


def on_device(queries, keys, values, grad_out, conv_weight, conv_bias, lengths):
    count = lax.axis_size("seq")
    rank = lax.axis_index("seq").astype(jnp.int32)
    width = queries.shape[2]
    depth = width // HEADS
    heads = HEADS // count
    chunks = math.gcd(heads, 2)
    step = heads // chunks
    by_head = conv_weight.reshape(KERNEL, HEADS, depth).transpose(1, 0, 2)
    weight = lax.dynamic_slice_in_dim(by_head, rank * heads, heads, axis=0)
    bias = lax.dynamic_slice_in_dim(conv_bias.reshape(HEADS, 1, depth), rank * heads, heads, axis=0)
    scalars = jnp.stack([lengths[0], rank])
    sent = pack(rank[None], (queries, keys, values, grad_out), count, chunks)
    order = []
    for pieces in sent:
        order.append(exchanged(pieces, order[-1] if order else None, True))
    taps = []
    for chunk in range(chunks):
        at = slice(chunk * step, (chunk + 1) * step)
        grads, part = core(scalars, weight[at], bias[at], order[chunk])
        taps.append(part)
        if chunk < chunks - 1:
            order.append(exchanged(grads, order[-1]))
    before, grads, taps = order[-1], list(grads), jnp.concatenate(taps, axis=0)
    last = count - 1
    grads[last - 1], before[1] = lax.optimization_barrier((grads[last - 1], before[1]))
    if last > 2:
        (grads[last], taps), before[last] = lax.optimization_barrier(
            ((grads[last], taps), before[last])
        )
        grads[1], before[last - 1] = lax.optimization_barrier((grads[1], before[last - 1]))
    order.append(exchanged(grads, None))
    return unpack(rank[None], doubled(taps, "dp"), order[chunks:], count, chunks)


def solution(mesh):
    return jax.shard_map(
        on_device,
        mesh=mesh,
        in_specs=(
            P("dp", "seq", None),
            P("dp", "seq", None),
            P("dp", "seq", None),
            P("dp", "seq", None),
            P(),
            P(),
            P("dp"),
        ),
        out_specs=(
            P("dp", "seq", None),
            P("dp", "seq", None),
            P("dp", "seq", None),
            P(None, "seq"),
            P("seq"),
        ),
        check_vma=False,
    )
```

```python
import functools
import math

import jax
import jax.numpy as jnp
from jax import lax
from jax.experimental import pallas as pl
from jax.experimental.pallas import tpu as pltpu
from jax.sharding import PartitionSpec as P

HEADS = 16
KERNEL = 31
PAD = 16
masked_score = -1e30
VMEM = pl.BlockSpec(memory_space=pltpu.VMEM)
SMEM = pl.BlockSpec(memory_space=pltpu.SMEM)
LIMIT = 16 * 1024 * 1024
bf16, f32 = jnp.bfloat16, jnp.float32


def pack_first_kernel(far, share, rank_ref, *refs):
    arrays, outs, (plain, sems) = refs[:4], refs[4:-2], refs[-2:]
    high = outs[0].shape[1]
    wide = plain.shape[3]
    copies = []
    for place, distance in enumerate(far):
        at = pl.ds(pl.multiple_of((rank_ref[0] ^ distance) * share, 128), wide)
        for which, array in enumerate(arrays):
            copies.append(
                pltpu.make_async_copy(
                    array.at[0, :, at], plain.at[place, which], sems.at[place, which]
                )
            )
            copies[-1].start()
    for index, copy in enumerate(copies):
        copy.wait()
        place, which = divmod(index, 4)
        outs[place][which] = plain[place, which].T[:high]


def pack_kernel(wanted, share, rank_ref, *refs):
    arrays, outs, turned = refs[:4], refs[4:-1], refs[-1]
    high = outs[0].shape[1]
    for which, array in enumerate(arrays):
        turned[which] = array[0].T
        for (chunk, distance), out in zip(wanted, outs):
            first = pl.multiple_of((rank_ref[0] ^ distance) * share + chunk * high, 16)
            out[which] = turned[which, pl.ds(first, high), :]


def pack(rank, arrays, count, chunks):
    _, frames, width = arrays[0].shape
    share = width // count
    high = share // chunks
    piece = jax.ShapeDtypeStruct((4, high, frames), bf16)
    wide = -(-high // 128) * 128
    far = tuple(range(count - 1, 1, -1)) if share % 128 == 0 and wide <= share else ()
    params = pltpu.CompilerParams(vmem_limit_bytes=LIMIT)
    arrays = [pltpu.with_memory_space_constraint(array, pltpu.HBM) for array in arrays]
    found = {}
    if far:
        outs = pl.pallas_call(
            functools.partial(pack_first_kernel, far, share),
            out_shape=(piece,) * len(far),
            in_specs=[SMEM] + [pl.BlockSpec(memory_space=pltpu.HBM)] * 4,
            out_specs=(VMEM,) * len(far),
            scratch_shapes=[
                pltpu.VMEM((len(far), 4, frames, wide), bf16),
                pltpu.SemaphoreType.DMA((len(far), 4)),
            ],
            compiler_params=params,
            cost_estimate=pl.CostEstimate(
                flops=0, bytes_accessed=16 * frames * wide * len(far), transcendentals=0
            ),
        )(rank, *arrays)
        found.update(zip([(0, distance) for distance in far], outs))
    every = [(chunk, distance) for chunk in range(chunks) for distance in range(count)]
    wanted = tuple(key for key in every if key not in found)
    outs = pl.pallas_call(
        functools.partial(pack_kernel, wanted, share),
        out_shape=(piece,) * len(wanted),
        in_specs=[SMEM] + [VMEM] * 4,
        out_specs=(VMEM,) * len(wanted),
        scratch_shapes=[pltpu.VMEM((4, width, frames), bf16)],
        compiler_params=params,
        cost_estimate=pl.CostEstimate(
            flops=0, bytes_accessed=16 * frames * width, transcendentals=0
        ),
    )(rank, *arrays)
    found.update(zip(wanted, outs))
    return [[found[chunk, distance] for distance in range(count)] for chunk in range(chunks)]


def taken(count):
    return [0] + list(range(count - 1, 0, -1))


def unpack_kernel(count, chunks, rank_ref, *refs):
    pieces, refs = refs[: count * chunks], refs[count * chunks :]
    taps_refs, outs = refs[:-7], refs[-7:-4]
    weight_ref, bias_ref, bias_row, turned = refs[-4:]
    rank = rank_ref[0]
    high = pieces[0].shape[1]
    share = high * chunks
    for which, out in enumerate(outs):
        for chunk in range(chunks):
            for place, distance in enumerate(taken(count)):
                first = pl.multiple_of((rank ^ distance) * share + chunk * high, 16)
                turned[which, pl.ds(first, high), :] = pieces[chunk * count + place][which]
        out[0] = turned[which].T
    taps = taps_refs[0][...] + taps_refs[1][...]
    heads, _, depth = taps.shape
    for head in range(heads):
        at = slice(head * depth, (head + 1) * depth)
        weight_ref[:, at] = taps[head, :KERNEL]
        bias_row[:, at] = taps[head, KERNEL:]
    bias_ref[...] = bias_row[0]


def unpack(rank, taps, pieces, count, chunks):
    _, high, frames = pieces[0][0].shape
    width = high * count * chunks
    whole = jax.ShapeDtypeStruct((1, frames, width), bf16)
    return pl.pallas_call(
        functools.partial(unpack_kernel, count, chunks),
        out_shape=(whole,) * 3
        + (
            jax.ShapeDtypeStruct((KERNEL, width // count), f32),
            jax.ShapeDtypeStruct((width // count,), f32),
        ),
        in_specs=[SMEM] + [VMEM] * (count * chunks + len(taps)),
        out_specs=(VMEM,) * 5,
        scratch_shapes=[
            pltpu.VMEM((1, width // count), f32),
            pltpu.VMEM((3, width, frames), bf16),
        ],
        compiler_params=pltpu.CompilerParams(vmem_limit_bytes=LIMIT),
        cost_estimate=pl.CostEstimate(
            flops=0, bytes_accessed=12 * frames * width, transcendentals=0
        ),
    )(rank, *[part[distance] for part in pieces for distance in taken(count)], *taps)


def core_kernel(count, block, scalars, weight_ref, bias_ref, *refs):
    pieces, outs, taps_ref = refs[:count], refs[count : 2 * count], refs[2 * count]
    q_t, k_t, v_t, a_t, q_n, k_n, v_n, g_n, a_n, probs, shifted, padded = refs[2 * count + 1 :]
    heads, rows, depth = q_n.shape
    frames = pieces[0].shape[2]
    blocks = rows // block
    scale = 1.0 / math.sqrt(depth)
    log_scale = scale * math.log2(math.e)
    length, rank = scalars[0], scalars[1]

    def span(head):
        return slice(head * depth, (head + 1) * depth)

    for distance, piece in zip(taken(count), pieces):
        at = pl.ds(pl.multiple_of((rank ^ distance) * frames, 128), frames)
        q_t[:, at] = piece[0]
        k_t[:, at] = piece[1]
        v_t[:, at] = piece[2]
        for head in range(heads):
            q_n[head, at, :] = piece[0, span(head), :].T
            k_n[head, at, :] = piece[1, span(head), :].T
            v_n[head, at, :] = piece[2, span(head), :].T
            g_n[head, at, :] = piece[3, span(head), :].T

    def forward(index, head):
        cols = pl.ds(pl.multiple_of(index * block, block), block)
        scores = jnp.dot(k_n[head], q_t[span(head), cols], preferred_element_type=f32)
        key_at = lax.broadcasted_iota(jnp.int32, scores.shape, 0)
        scores = jnp.where(key_at < length, scores, masked_score)
        exped = jnp.exp2((scores - jnp.max(scores, axis=0, keepdims=True)) * log_scale)
        found = exped * (1.0 / jnp.sum(exped, axis=0, keepdims=True))
        probs[head, :, cols] = found
        out = jnp.dot(v_t[span(head), :], found.astype(bf16), preferred_element_type=f32)
        frame_at = index * block + lax.broadcasted_iota(jnp.int32, out.shape, 1)
        a_t[span(head), cols] = jnp.where(frame_at < length, out, 0.0).astype(bf16)

    def each_block(body):
        if blocks == 1:
            for head in range(heads):
                body(0, head)
        else:

            def step(index, carry):
                for head in range(heads):
                    body(index, head)
                return carry

            lax.fori_loop(0, blocks, step, 0)

    each_block(forward)

    tall = padded.shape[0]
    padded[0:PAD, :] = jnp.zeros((PAD, depth), f32)
    padded[PAD + rows : tall, :] = jnp.zeros((tall - PAD - rows, depth), f32)

    def shift_all():
        for s in range(8):
            shifted[s] = padded[s : s + tall - 8, :].reshape(tall // 8 - 1, 8, depth)

    step_tiles = 8
    step_rows = 8 * step_tiles

    def window(index, offset):
        return shifted[offset % 8, pl.ds(index * step_tiles + offset // 8, step_tiles)]

    def filtered(head, index, reverse):
        total = None
        for offset in range(1, KERNEL + 1):
            tap = KERNEL - offset if reverse else offset - 1
            term = weight_ref[head, tap : tap + 1, :] * window(index, offset)
            total = term if total is None else total + term
        return total

    def loaded(ref, index):
        at = pl.ds(pl.multiple_of(index * step_rows, step_rows), step_rows)
        return ref[at, :].astype(f32).reshape(step_tiles, 8, depth)

    for head in range(heads):
        for first in range(0, rows, frames):
            at = slice(PAD + first, PAD + first + frames)
            padded[at, :] = a_t[span(head), first : first + frames].T.astype(f32)
        shift_all()

        def conv_step(index, carry, head=head):
            conv_pre = filtered(head, index, False) + bias_ref[head]
            sig = 1.0 / (1.0 + jnp.exp(-conv_pre))
            pre = loaded(g_n.at[head], index) * (sig * (1.0 + conv_pre * (1.0 - sig)))
            pre = pre.astype(bf16).astype(f32)
            at = pl.ds(pl.multiple_of(PAD + index * step_rows, PAD), step_rows)
            padded[at, :] = pre.reshape(step_rows, depth)
            new = []
            for offset in range(1, KERNEL + 1):
                new.append(carry[offset - 1] + jnp.sum(pre * window(index, offset), axis=0))
            new.append(carry[KERNEL] + jnp.sum(pre, axis=0))
            return tuple(new)

        zero = jnp.zeros((8, depth), f32)
        sums = lax.fori_loop(0, rows // step_rows, conv_step, (zero,) * (KERNEL + 1))
        for tap in range(KERNEL + 1):
            taps_ref[head, tap : tap + 1, :] = jnp.sum(sums[tap], axis=0, keepdims=True)
        shift_all()

        def back_step(index, carry, head=head):
            total = loaded(g_n.at[head], index) + filtered(head, index, True)
            total = total.reshape(step_rows, depth)
            frame_at = index * step_rows + lax.broadcasted_iota(jnp.int32, total.shape, 0)
            total = jnp.where(frame_at < length, total, 0.0)
            at = pl.ds(pl.multiple_of(index * step_rows, step_rows), step_rows)
            a_n[head, at, :] = total.astype(bf16)
            return carry

        lax.fori_loop(0, rows // step_rows, back_step, 0)
        for first in range(0, rows, frames):
            a_t[span(head), first : first + frames] = a_n[head, first : first + frames, :].T

    def backward(index, head):
        cols = pl.ds(pl.multiple_of(index * block, block), block)
        score_grad = jnp.dot(v_n[head], a_t[span(head), cols], preferred_element_type=f32)
        found = probs[head, :, cols]
        delta = jnp.sum(found * score_grad, axis=0, keepdims=True)
        diff = (found * (score_grad - delta)).astype(bf16)
        value = jnp.dot(found.astype(bf16), a_n[head, cols, :], preferred_element_type=f32)
        key = jnp.dot(diff, q_n[head, cols, :], preferred_element_type=f32)
        query = jnp.dot(k_t[span(head), :], diff, preferred_element_type=f32)
        q_t[span(head), cols] = (query * scale).astype(bf16)
        return key, value

    def finish(head, key, value):
        for first in range(0, rows, frames):
            at = slice(first, first + frames)
            k_t[span(head), at] = (key[at, :] * scale).astype(bf16).T
            v_t[span(head), at] = value[at, :].astype(bf16).T

    for head in range(heads):
        if blocks == 1:
            finish(head, *backward(0, head))
        else:
            zeros = jnp.zeros((rows, depth), f32)

            def step(index, carry, head=head):
                key, value = backward(index, head)
                return carry[0] + key, carry[1] + value

            finish(head, *lax.fori_loop(0, blocks, step, (zeros, zeros)))

    for distance, out in enumerate(outs):
        at = pl.ds(pl.multiple_of((rank ^ distance) * frames, 128), frames)
        out[0] = q_t[:, at]
        out[1] = k_t[:, at]
        out[2] = v_t[:, at]


def core(scalars, weight, bias, pieces):
    count = len(pieces)
    _, high, frames = pieces[0].shape
    heads, _, depth = weight.shape
    rows = count * frames
    block = math.gcd(rows, 512)
    tall = rows + 2 * PAD + 8
    piece = jax.ShapeDtypeStruct((3, high, frames), bf16)
    turned = pltpu.VMEM((high, rows), bf16)
    plain = pltpu.VMEM((heads, rows, depth), bf16)
    outs = pl.pallas_call(
        functools.partial(core_kernel, count, block),
        out_shape=(piece,) * count + (jax.ShapeDtypeStruct((heads, KERNEL + 1, depth), f32),),
        in_specs=[SMEM] + [VMEM] * (2 + count),
        out_specs=(VMEM,) * (count + 1),
        scratch_shapes=[turned] * 4
        + [plain] * 5
        + [
            pltpu.VMEM((heads, rows, rows), f32),
            pltpu.VMEM((8, tall // 8 - 1, 8, depth), f32),
            pltpu.VMEM((tall, depth), f32),
        ],
        compiler_params=pltpu.CompilerParams(
            vmem_limit_bytes=12 * 2**20 + 8 * heads * rows * rows + 4096 * tall
        ),
        cost_estimate=pl.CostEstimate(
            flops=24 * rows * rows * high,
            bytes_accessed=14 * rows * high,
            transcendentals=heads * rows * rows,
        ),
    )(scalars, weight, bias, *[pieces[distance] for distance in taken(count)])
    return outs[:count], outs[count]


def exchanged(pieces, before, eager=False):
    pieces = list(pieces)
    last = len(pieces) - 1
    if before is not None and eager:
        pieces[last], before[last] = lax.optimization_barrier((pieces[last], before[last]))
    if before is not None and last > 1:
        wait = slice(last - 1 if eager else last, 1, -1)
        pieces[wait], before[:0:-1] = lax.optimization_barrier((pieces[wait], before[:0:-1]))
    moved = pieces[:1] * len(pieces)
    for distance in range(len(pieces) - 1, 0, -1):
        pairs = [(i, i ^ distance) for i in range(len(pieces))]
        moved[distance] = lax.ppermute(pieces[distance], "seq", pairs)
    return moved


def doubled(array, axis):
    count = lax.axis_size(axis)
    pair, distance = (array, jnp.zeros_like(array)), 1
    while distance < count:
        total = array if distance == 1 else pair[0] + pair[1]
        pairs = [(i, i ^ distance) for i in range(count)]
        pair = (total, lax.ppermute(total, axis, pairs))
        distance *= 2
    return pair


def on_device(queries, keys, values, grad_out, conv_weight, conv_bias, lengths):
    count = lax.axis_size("seq")
    rank = lax.axis_index("seq").astype(jnp.int32)
    width = queries.shape[2]
    depth = width // HEADS
    heads = HEADS // count
    chunks = math.gcd(heads, 2)
    step = heads // chunks
    by_head = conv_weight.reshape(KERNEL, HEADS, depth).transpose(1, 0, 2)
    weight = lax.dynamic_slice_in_dim(by_head, rank * heads, heads, axis=0)
    bias = lax.dynamic_slice_in_dim(conv_bias.reshape(HEADS, 1, depth), rank * heads, heads, axis=0)
    scalars = jnp.stack([lengths[0], rank])
    sent = pack(rank[None], (queries, keys, values, grad_out), count, chunks)
    order = []
    for pieces in sent:
        order.append(exchanged(pieces, order[-1] if order else None, True))
    taps = []
    for chunk in range(chunks):
        at = slice(chunk * step, (chunk + 1) * step)
        grads, part = core(scalars, weight[at], bias[at], order[chunk])
        taps.append(part)
        if chunk < chunks - 1:
            order.append(exchanged(grads, order[-1]))
    before, grads, taps = order[-1], list(grads), jnp.concatenate(taps, axis=0)
    last = count - 1
    grads[last - 1], before[1] = lax.optimization_barrier((grads[last - 1], before[1]))
    if last > 2:
        (grads[1], taps), before[last] = lax.optimization_barrier(((grads[1], taps), before[last]))
        grads[last], before[last - 1] = lax.optimization_barrier((grads[last], before[last - 1]))
    order.append(exchanged(grads, None))
    return unpack(rank[None], doubled(taps, "dp"), order[chunks:], count, chunks)


def solution(mesh):
    return jax.shard_map(
        on_device,
        mesh=mesh,
        in_specs=(
            P("dp", "seq", None),
            P("dp", "seq", None),
            P("dp", "seq", None),
            P("dp", "seq", None),
            P(),
            P(),
            P("dp"),
        ),
        out_specs=(
            P("dp", "seq", None),
            P("dp", "seq", None),
            P("dp", "seq", None),
            P(None, "seq"),
            P("seq"),
        ),
        check_vma=False,
    )
```

```python
import functools
import math

import jax
import jax.numpy as jnp
from jax import lax
from jax.experimental import pallas as pl
from jax.experimental.pallas import tpu as pltpu
from jax.sharding import PartitionSpec as P

HEADS = 16
KERNEL = 31
PAD = 16
masked_score = -1e30
VMEM = pl.BlockSpec(memory_space=pltpu.VMEM)
SMEM = pl.BlockSpec(memory_space=pltpu.SMEM)
LIMIT = 16 * 1024 * 1024
bf16, f32 = jnp.bfloat16, jnp.float32


def pack_first_kernel(far, share, rank_ref, *refs):
    arrays, outs, (plain, sems) = refs[:4], refs[4:-2], refs[-2:]
    high = outs[0].shape[1]
    wide = plain.shape[3]
    copies = []
    for place, distance in enumerate(far):
        at = pl.ds(pl.multiple_of((rank_ref[0] ^ distance) * share, 128), wide)
        for which, array in enumerate(arrays):
            copies.append(
                pltpu.make_async_copy(
                    array.at[0, :, at], plain.at[place, which], sems.at[place, which]
                )
            )
            copies[-1].start()
    for index, copy in enumerate(copies):
        copy.wait()
        place, which = divmod(index, 4)
        outs[place][which] = plain[place, which].T[:high]


def pack_kernel(wanted, share, rank_ref, *refs):
    arrays, outs, turned = refs[:4], refs[4:-1], refs[-1]
    high = outs[0].shape[1]
    for which, array in enumerate(arrays):
        turned[which] = array[0].T
        for (chunk, distance), out in zip(wanted, outs):
            first = pl.multiple_of((rank_ref[0] ^ distance) * share + chunk * high, 16)
            out[which] = turned[which, pl.ds(first, high), :]


def pack(rank, arrays, count, chunks):
    _, frames, width = arrays[0].shape
    share = width // count
    high = share // chunks
    piece = jax.ShapeDtypeStruct((4, high, frames), bf16)
    wide = -(-high // 128) * 128
    far = tuple(range(count - 1, 1, -1)) if share % 128 == 0 and wide <= share else ()
    params = pltpu.CompilerParams(vmem_limit_bytes=LIMIT)
    arrays = [pltpu.with_memory_space_constraint(array, pltpu.HBM) for array in arrays]
    found = {}
    if far:
        outs = pl.pallas_call(
            functools.partial(pack_first_kernel, far, share),
            out_shape=(piece,) * len(far),
            in_specs=[SMEM] + [pl.BlockSpec(memory_space=pltpu.HBM)] * 4,
            out_specs=(VMEM,) * len(far),
            scratch_shapes=[
                pltpu.VMEM((len(far), 4, frames, wide), bf16),
                pltpu.SemaphoreType.DMA((len(far), 4)),
            ],
            compiler_params=params,
            cost_estimate=pl.CostEstimate(
                flops=0, bytes_accessed=16 * frames * wide * len(far), transcendentals=0
            ),
        )(rank, *arrays)
        found.update(zip([(0, distance) for distance in far], outs))
    every = [(chunk, distance) for chunk in range(chunks) for distance in range(count)]
    wanted = tuple(key for key in every if key not in found)
    outs = pl.pallas_call(
        functools.partial(pack_kernel, wanted, share),
        out_shape=(piece,) * len(wanted),
        in_specs=[SMEM] + [VMEM] * 4,
        out_specs=(VMEM,) * len(wanted),
        scratch_shapes=[pltpu.VMEM((4, width, frames), bf16)],
        compiler_params=params,
        cost_estimate=pl.CostEstimate(
            flops=0, bytes_accessed=16 * frames * width, transcendentals=0
        ),
    )(rank, *arrays)
    found.update(zip(wanted, outs))
    return [[found[chunk, distance] for distance in range(count)] for chunk in range(chunks)]


def taken(count):
    return [0] + list(range(count - 1, 0, -1))


def unpack_kernel(count, chunks, rank_ref, *refs):
    pieces, refs = refs[: count * chunks], refs[count * chunks :]
    taps_refs, outs = refs[:-7], refs[-7:-4]
    weight_ref, bias_ref, bias_row, turned = refs[-4:]
    rank = rank_ref[0]
    high = pieces[0].shape[1]
    share = high * chunks
    for which, out in enumerate(outs):
        for chunk in range(chunks):
            for place, distance in enumerate(taken(count)):
                first = pl.multiple_of((rank ^ distance) * share + chunk * high, 16)
                turned[which, pl.ds(first, high), :] = pieces[chunk * count + place][which]
        out[0] = turned[which].T
    taps = taps_refs[0][...] + taps_refs[1][...]
    heads, _, depth = taps.shape
    for head in range(heads):
        at = slice(head * depth, (head + 1) * depth)
        weight_ref[:, at] = taps[head, :KERNEL]
        bias_row[:, at] = taps[head, KERNEL:]
    bias_ref[...] = bias_row[0]


def unpack(rank, taps, pieces, count, chunks):
    _, high, frames = pieces[0][0].shape
    width = high * count * chunks
    whole = jax.ShapeDtypeStruct((1, frames, width), bf16)
    return pl.pallas_call(
        functools.partial(unpack_kernel, count, chunks),
        out_shape=(whole,) * 3
        + (
            jax.ShapeDtypeStruct((KERNEL, width // count), f32),
            jax.ShapeDtypeStruct((width // count,), f32),
        ),
        in_specs=[SMEM] + [VMEM] * (count * chunks + len(taps)),
        out_specs=(VMEM,) * 5,
        scratch_shapes=[
            pltpu.VMEM((1, width // count), f32),
            pltpu.VMEM((3, width, frames), bf16),
        ],
        compiler_params=pltpu.CompilerParams(vmem_limit_bytes=LIMIT),
        cost_estimate=pl.CostEstimate(
            flops=0, bytes_accessed=12 * frames * width, transcendentals=0
        ),
    )(rank, *[part[distance] for part in pieces for distance in taken(count)], *taps)


def core_kernel(count, block, scalars, weight_ref, bias_ref, *refs):
    pieces, outs, taps_ref = refs[:count], refs[count : 2 * count], refs[2 * count]
    q_t, k_t, v_t, a_t, q_n, k_n, v_n, g_n, a_n, probs, shifted, padded = refs[2 * count + 1 :]
    heads, rows, depth = q_n.shape
    frames = pieces[0].shape[2]
    blocks = rows // block
    scale = 1.0 / math.sqrt(depth)
    log_scale = scale * math.log2(math.e)
    length, rank = scalars[0], scalars[1]

    def span(head):
        return slice(head * depth, (head + 1) * depth)

    for distance, piece in zip(taken(count), pieces):
        at = pl.ds(pl.multiple_of((rank ^ distance) * frames, 128), frames)
        q_t[:, at] = piece[0]
        k_t[:, at] = piece[1]
        v_t[:, at] = piece[2]
        for head in range(heads):
            q_n[head, at, :] = piece[0, span(head), :].T
            k_n[head, at, :] = piece[1, span(head), :].T
            v_n[head, at, :] = piece[2, span(head), :].T
            g_n[head, at, :] = piece[3, span(head), :].T

    def forward(index, head):
        cols = pl.ds(pl.multiple_of(index * block, block), block)
        scores = jnp.dot(k_n[head], q_t[span(head), cols], preferred_element_type=f32)
        key_at = lax.broadcasted_iota(jnp.int32, scores.shape, 0)
        scores = jnp.where(key_at < length, scores, masked_score)
        exped = jnp.exp2((scores - jnp.max(scores, axis=0, keepdims=True)) * log_scale)
        found = exped * (1.0 / jnp.sum(exped, axis=0, keepdims=True))
        probs[head, :, cols] = found
        out = jnp.dot(v_t[span(head), :], found.astype(bf16), preferred_element_type=f32)
        frame_at = index * block + lax.broadcasted_iota(jnp.int32, out.shape, 1)
        a_t[span(head), cols] = jnp.where(frame_at < length, out, 0.0).astype(bf16)

    def each_block(body):
        if blocks == 1:
            for head in range(heads):
                body(0, head)
        else:

            def step(index, carry):
                for head in range(heads):
                    body(index, head)
                return carry

            lax.fori_loop(0, blocks, step, 0)

    each_block(forward)

    tall = padded.shape[0]
    padded[0:PAD, :] = jnp.zeros((PAD, depth), f32)
    padded[PAD + rows : tall, :] = jnp.zeros((tall - PAD - rows, depth), f32)

    def shift_all():
        for s in range(8):
            shifted[s] = padded[s : s + tall - 8, :].reshape(tall // 8 - 1, 8, depth)

    step_tiles = 8
    step_rows = 8 * step_tiles

    def window(index, offset):
        return shifted[offset % 8, pl.ds(index * step_tiles + offset // 8, step_tiles)]

    def filtered(head, index, reverse):
        total = None
        for offset in range(1, KERNEL + 1):
            tap = KERNEL - offset if reverse else offset - 1
            term = weight_ref[head, tap : tap + 1, :] * window(index, offset)
            total = term if total is None else total + term
        return total

    def loaded(ref, index):
        at = pl.ds(pl.multiple_of(index * step_rows, step_rows), step_rows)
        return ref[at, :].astype(f32).reshape(step_tiles, 8, depth)

    for head in range(heads):
        for first in range(0, rows, frames):
            at = slice(PAD + first, PAD + first + frames)
            padded[at, :] = a_t[span(head), first : first + frames].T.astype(f32)
        shift_all()

        def conv_step(index, carry, head=head):
            conv_pre = filtered(head, index, False) + bias_ref[head]
            sig = 1.0 / (1.0 + jnp.exp(-conv_pre))
            pre = loaded(g_n.at[head], index) * (sig * (1.0 + conv_pre * (1.0 - sig)))
            pre = pre.astype(bf16).astype(f32)
            at = pl.ds(pl.multiple_of(PAD + index * step_rows, PAD), step_rows)
            padded[at, :] = pre.reshape(step_rows, depth)
            new = []
            for offset in range(1, KERNEL + 1):
                new.append(carry[offset - 1] + jnp.sum(pre * window(index, offset), axis=0))
            new.append(carry[KERNEL] + jnp.sum(pre, axis=0))
            return tuple(new)

        zero = jnp.zeros((8, depth), f32)
        sums = lax.fori_loop(0, rows // step_rows, conv_step, (zero,) * (KERNEL + 1))
        for tap in range(KERNEL + 1):
            taps_ref[head, tap : tap + 1, :] = jnp.sum(sums[tap], axis=0, keepdims=True)
        shift_all()

        def back_step(index, carry, head=head):
            total = loaded(g_n.at[head], index) + filtered(head, index, True)
            total = total.reshape(step_rows, depth)
            frame_at = index * step_rows + lax.broadcasted_iota(jnp.int32, total.shape, 0)
            total = jnp.where(frame_at < length, total, 0.0)
            at = pl.ds(pl.multiple_of(index * step_rows, step_rows), step_rows)
            a_n[head, at, :] = total.astype(bf16)
            return carry

        lax.fori_loop(0, rows // step_rows, back_step, 0)
        for first in range(0, rows, frames):
            a_t[span(head), first : first + frames] = a_n[head, first : first + frames, :].T

    def backward(index, head):
        cols = pl.ds(pl.multiple_of(index * block, block), block)
        score_grad = jnp.dot(v_n[head], a_t[span(head), cols], preferred_element_type=f32)
        found = probs[head, :, cols]
        delta = jnp.sum(found * score_grad, axis=0, keepdims=True)
        diff = (found * (score_grad - delta)).astype(bf16)
        value = jnp.dot(found.astype(bf16), a_n[head, cols, :], preferred_element_type=f32)
        key = jnp.dot(diff, q_n[head, cols, :], preferred_element_type=f32)
        query = jnp.dot(k_t[span(head), :], diff, preferred_element_type=f32)
        q_t[span(head), cols] = (query * scale).astype(bf16)
        return key, value

    def finish(head, key, value):
        for first in range(0, rows, frames):
            at = slice(first, first + frames)
            k_t[span(head), at] = (key[at, :] * scale).astype(bf16).T
            v_t[span(head), at] = value[at, :].astype(bf16).T

    for head in range(heads):
        if blocks == 1:
            finish(head, *backward(0, head))
        else:
            zeros = jnp.zeros((rows, depth), f32)

            def step(index, carry, head=head):
                key, value = backward(index, head)
                return carry[0] + key, carry[1] + value

            finish(head, *lax.fori_loop(0, blocks, step, (zeros, zeros)))

    for distance, out in enumerate(outs):
        at = pl.ds(pl.multiple_of((rank ^ distance) * frames, 128), frames)
        out[0] = q_t[:, at]
        out[1] = k_t[:, at]
        out[2] = v_t[:, at]


def core(scalars, weight, bias, pieces):
    count = len(pieces)
    _, high, frames = pieces[0].shape
    heads, _, depth = weight.shape
    rows = count * frames
    block = math.gcd(rows, 512)
    tall = rows + 2 * PAD + 8
    piece = jax.ShapeDtypeStruct((3, high, frames), bf16)
    turned = pltpu.VMEM((high, rows), bf16)
    plain = pltpu.VMEM((heads, rows, depth), bf16)
    outs = pl.pallas_call(
        functools.partial(core_kernel, count, block),
        out_shape=(piece,) * count + (jax.ShapeDtypeStruct((heads, KERNEL + 1, depth), f32),),
        in_specs=[SMEM] + [VMEM] * (2 + count),
        out_specs=(VMEM,) * (count + 1),
        scratch_shapes=[turned] * 4
        + [plain] * 5
        + [
            pltpu.VMEM((heads, rows, rows), f32),
            pltpu.VMEM((8, tall // 8 - 1, 8, depth), f32),
            pltpu.VMEM((tall, depth), f32),
        ],
        compiler_params=pltpu.CompilerParams(
            vmem_limit_bytes=12 * 2**20 + 8 * heads * rows * rows + 4096 * tall
        ),
        cost_estimate=pl.CostEstimate(
            flops=24 * rows * rows * high,
            bytes_accessed=14 * rows * high,
            transcendentals=heads * rows * rows,
        ),
    )(scalars, weight, bias, *[pieces[distance] for distance in taken(count)])
    return outs[:count], outs[count]


def exchanged(pieces, before):
    pieces = list(pieces)
    if before is not None and len(pieces) > 2:
        pieces[:1:-1], before[:0:-1] = lax.optimization_barrier((pieces[:1:-1], before[:0:-1]))
    moved = pieces[:1] * len(pieces)
    for distance in range(len(pieces) - 1, 0, -1):
        pairs = [(i, i ^ distance) for i in range(len(pieces))]
        moved[distance] = lax.ppermute(pieces[distance], "seq", pairs)
    return moved


def doubled(array, axis):
    count = lax.axis_size(axis)
    pair, distance = (array, jnp.zeros_like(array)), 1
    while distance < count:
        total = array if distance == 1 else pair[0] + pair[1]
        pairs = [(i, i ^ distance) for i in range(count)]
        pair = (total, lax.ppermute(total, axis, pairs))
        distance *= 2
    return pair


def on_device(queries, keys, values, grad_out, conv_weight, conv_bias, lengths):
    count = lax.axis_size("seq")
    rank = lax.axis_index("seq").astype(jnp.int32)
    width = queries.shape[2]
    depth = width // HEADS
    heads = HEADS // count
    chunks = math.gcd(heads, 2)
    step = heads // chunks
    by_head = conv_weight.reshape(KERNEL, HEADS, depth).transpose(1, 0, 2)
    weight = lax.dynamic_slice_in_dim(by_head, rank * heads, heads, axis=0)
    bias = lax.dynamic_slice_in_dim(conv_bias.reshape(HEADS, 1, depth), rank * heads, heads, axis=0)
    scalars = jnp.stack([lengths[0], rank])
    sent = pack(rank[None], (queries, keys, values, grad_out), count, chunks)
    order = []
    for pieces in sent:
        order.append(exchanged(pieces, order[-1] if order else None))
    taps = []
    for chunk in range(chunks):
        at = slice(chunk * step, (chunk + 1) * step)
        grads, part = core(scalars, weight[at], bias[at], order[chunk])
        taps.append(part)
        if chunk < chunks - 1:
            order.append(exchanged(grads, order[-1]))
    before, grads, taps = order[-1], list(grads), jnp.concatenate(taps, axis=0)
    last = count - 1
    grads[last - 1], before[1] = lax.optimization_barrier((grads[last - 1], before[1]))
    if last > 2:
        (grads[1], taps), before[last] = lax.optimization_barrier(((grads[1], taps), before[last]))
        grads[last], before[last - 1] = lax.optimization_barrier((grads[last], before[last - 1]))
    order.append(exchanged(grads, None))
    return unpack(rank[None], doubled(taps, "dp"), order[chunks:], count, chunks)


def solution(mesh):
    return jax.shard_map(
        on_device,
        mesh=mesh,
        in_specs=(
            P("dp", "seq", None),
            P("dp", "seq", None),
            P("dp", "seq", None),
            P("dp", "seq", None),
            P(),
            P(),
            P("dp"),
        ),
        out_specs=(
            P("dp", "seq", None),
            P("dp", "seq", None),
            P("dp", "seq", None),
            P(None, "seq"),
            P("seq"),
        ),
        check_vma=False,
    )
```

```python
import functools
import math

import jax
import jax.numpy as jnp
from jax import lax
from jax.experimental import pallas as pl
from jax.experimental.pallas import tpu as pltpu
from jax.sharding import PartitionSpec as P

HEADS = 16
KERNEL = 31
PAD = 16
masked_score = -1e30
VMEM = pl.BlockSpec(memory_space=pltpu.VMEM)
SMEM = pl.BlockSpec(memory_space=pltpu.SMEM)
LIMIT = 16 * 1024 * 1024
bf16, f32 = jnp.bfloat16, jnp.float32


def pack_first_kernel(far, share, rank_ref, *refs):
    arrays, outs, (plain, sems) = refs[:4], refs[4:-2], refs[-2:]
    high = outs[0].shape[1]
    wide = plain.shape[3]
    copies = []
    for place, distance in enumerate(far):
        at = pl.ds(pl.multiple_of((rank_ref[0] ^ distance) * share, 128), wide)
        for which, array in enumerate(arrays):
            copies.append(
                pltpu.make_async_copy(
                    array.at[0, :, at], plain.at[place, which], sems.at[place, which]
                )
            )
            copies[-1].start()
    for index, copy in enumerate(copies):
        copy.wait()
        place, which = divmod(index, 4)
        outs[place][which] = plain[place, which].T[:high]


def pack_kernel(wanted, share, rank_ref, *refs):
    arrays, outs, turned = refs[:4], refs[4:-1], refs[-1]
    high = outs[0].shape[1]
    for which, array in enumerate(arrays):
        turned[which] = array[0].T
        for (chunk, distance), out in zip(wanted, outs):
            first = pl.multiple_of((rank_ref[0] ^ distance) * share + chunk * high, 16)
            out[which] = turned[which, pl.ds(first, high), :]


def pack(rank, arrays, count, chunks):
    _, frames, width = arrays[0].shape
    share = width // count
    high = share // chunks
    piece = jax.ShapeDtypeStruct((4, high, frames), bf16)
    wide = -(-high // 128) * 128
    far = tuple(range(2, count)) if share % 128 == 0 and wide <= share else ()
    params = pltpu.CompilerParams(vmem_limit_bytes=LIMIT)
    arrays = [pltpu.with_memory_space_constraint(array, pltpu.HBM) for array in arrays]
    found = {}
    if far:
        outs = pl.pallas_call(
            functools.partial(pack_first_kernel, far, share),
            out_shape=(piece,) * len(far),
            in_specs=[SMEM] + [pl.BlockSpec(memory_space=pltpu.HBM)] * 4,
            out_specs=(VMEM,) * len(far),
            scratch_shapes=[
                pltpu.VMEM((len(far), 4, frames, wide), bf16),
                pltpu.SemaphoreType.DMA((len(far), 4)),
            ],
            compiler_params=params,
            cost_estimate=pl.CostEstimate(
                flops=0, bytes_accessed=16 * frames * wide * len(far), transcendentals=0
            ),
        )(rank, *arrays)
        found.update(zip([(0, distance) for distance in far], outs))
    every = [(chunk, distance) for chunk in range(chunks) for distance in range(count)]
    wanted = tuple(key for key in every if key not in found)
    outs = pl.pallas_call(
        functools.partial(pack_kernel, wanted, share),
        out_shape=(piece,) * len(wanted),
        in_specs=[SMEM] + [VMEM] * 4,
        out_specs=(VMEM,) * len(wanted),
        scratch_shapes=[pltpu.VMEM((4, width, frames), bf16)],
        compiler_params=params,
        cost_estimate=pl.CostEstimate(
            flops=0, bytes_accessed=16 * frames * width, transcendentals=0
        ),
    )(rank, *arrays)
    found.update(zip(wanted, outs))
    return [[found[chunk, distance] for distance in range(count)] for chunk in range(chunks)]


def taken(count):
    return [0] + list(range(2, count)) + [1]


def unpack_kernel(count, chunks, rank_ref, *refs):
    pieces, refs = refs[: count * chunks], refs[count * chunks :]
    taps_refs, outs = refs[:-7], refs[-7:-4]
    weight_ref, bias_ref, bias_row, turned = refs[-4:]
    rank = rank_ref[0]
    high = pieces[0].shape[1]
    share = high * chunks
    for which, out in enumerate(outs):
        for chunk in range(chunks):
            for place, distance in enumerate(taken(count)):
                first = pl.multiple_of((rank ^ distance) * share + chunk * high, 16)
                turned[which, pl.ds(first, high), :] = pieces[chunk * count + place][which]
        out[0] = turned[which].T
    taps = taps_refs[0][...] + taps_refs[1][...]
    heads, _, depth = taps.shape
    for head in range(heads):
        at = slice(head * depth, (head + 1) * depth)
        weight_ref[:, at] = taps[head, :KERNEL]
        bias_row[:, at] = taps[head, KERNEL:]
    bias_ref[...] = bias_row[0]


def unpack(rank, taps, pieces, count, chunks):
    _, high, frames = pieces[0][0].shape
    width = high * count * chunks
    whole = jax.ShapeDtypeStruct((1, frames, width), bf16)
    return pl.pallas_call(
        functools.partial(unpack_kernel, count, chunks),
        out_shape=(whole,) * 3
        + (
            jax.ShapeDtypeStruct((KERNEL, width // count), f32),
            jax.ShapeDtypeStruct((width // count,), f32),
        ),
        in_specs=[SMEM] + [VMEM] * (count * chunks + len(taps)),
        out_specs=(VMEM,) * 5,
        scratch_shapes=[
            pltpu.VMEM((1, width // count), f32),
            pltpu.VMEM((3, width, frames), bf16),
        ],
        compiler_params=pltpu.CompilerParams(vmem_limit_bytes=LIMIT),
        cost_estimate=pl.CostEstimate(
            flops=0, bytes_accessed=12 * frames * width, transcendentals=0
        ),
    )(rank, *[part[distance] for part in pieces for distance in taken(count)], *taps)


def core_kernel(count, block, scalars, weight_ref, bias_ref, *refs):
    pieces, outs, taps_ref = refs[:count], refs[count : 2 * count], refs[2 * count]
    q_t, k_t, v_t, a_t, q_n, k_n, v_n, g_n, a_n, probs, shifted, padded = refs[2 * count + 1 :]
    heads, rows, depth = q_n.shape
    frames = pieces[0].shape[2]
    blocks = rows // block
    scale = 1.0 / math.sqrt(depth)
    log_scale = scale * math.log2(math.e)
    length, rank = scalars[0], scalars[1]

    def span(head):
        return slice(head * depth, (head + 1) * depth)

    for distance, piece in zip(taken(count), pieces):
        at = pl.ds(pl.multiple_of((rank ^ distance) * frames, 128), frames)
        q_t[:, at] = piece[0]
        k_t[:, at] = piece[1]
        v_t[:, at] = piece[2]
        for head in range(heads):
            q_n[head, at, :] = piece[0, span(head), :].T
            k_n[head, at, :] = piece[1, span(head), :].T
            v_n[head, at, :] = piece[2, span(head), :].T
            g_n[head, at, :] = piece[3, span(head), :].T

    def forward(index, head):
        cols = pl.ds(pl.multiple_of(index * block, block), block)
        scores = jnp.dot(k_n[head], q_t[span(head), cols], preferred_element_type=f32)
        key_at = lax.broadcasted_iota(jnp.int32, scores.shape, 0)
        scores = jnp.where(key_at < length, scores, masked_score)
        exped = jnp.exp2((scores - jnp.max(scores, axis=0, keepdims=True)) * log_scale)
        found = exped * (1.0 / jnp.sum(exped, axis=0, keepdims=True))
        probs[head, :, cols] = found
        out = jnp.dot(v_t[span(head), :], found.astype(bf16), preferred_element_type=f32)
        frame_at = index * block + lax.broadcasted_iota(jnp.int32, out.shape, 1)
        a_t[span(head), cols] = jnp.where(frame_at < length, out, 0.0).astype(bf16)

    def each_block(body):
        if blocks == 1:
            for head in range(heads):
                body(0, head)
        else:

            def step(index, carry):
                for head in range(heads):
                    body(index, head)
                return carry

            lax.fori_loop(0, blocks, step, 0)

    each_block(forward)

    tall = padded.shape[0]
    padded[0:PAD, :] = jnp.zeros((PAD, depth), f32)
    padded[PAD + rows : tall, :] = jnp.zeros((tall - PAD - rows, depth), f32)

    def shift_all():
        for s in range(8):
            shifted[s] = padded[s : s + tall - 8, :].reshape(tall // 8 - 1, 8, depth)

    step_tiles = 8
    step_rows = 8 * step_tiles

    def window(index, offset):
        return shifted[offset % 8, pl.ds(index * step_tiles + offset // 8, step_tiles)]

    def filtered(head, index, reverse):
        total = None
        for offset in range(1, KERNEL + 1):
            tap = KERNEL - offset if reverse else offset - 1
            term = weight_ref[head, tap : tap + 1, :] * window(index, offset)
            total = term if total is None else total + term
        return total

    def loaded(ref, index):
        at = pl.ds(pl.multiple_of(index * step_rows, step_rows), step_rows)
        return ref[at, :].astype(f32).reshape(step_tiles, 8, depth)

    for head in range(heads):
        for first in range(0, rows, frames):
            at = slice(PAD + first, PAD + first + frames)
            padded[at, :] = a_t[span(head), first : first + frames].T.astype(f32)
        shift_all()

        def conv_step(index, carry, head=head):
            conv_pre = filtered(head, index, False) + bias_ref[head]
            sig = 1.0 / (1.0 + jnp.exp(-conv_pre))
            pre = loaded(g_n.at[head], index) * (sig * (1.0 + conv_pre * (1.0 - sig)))
            pre = pre.astype(bf16).astype(f32)
            at = pl.ds(pl.multiple_of(PAD + index * step_rows, PAD), step_rows)
            padded[at, :] = pre.reshape(step_rows, depth)
            new = []
            for offset in range(1, KERNEL + 1):
                new.append(carry[offset - 1] + jnp.sum(pre * window(index, offset), axis=0))
            new.append(carry[KERNEL] + jnp.sum(pre, axis=0))
            return tuple(new)

        zero = jnp.zeros((8, depth), f32)
        sums = lax.fori_loop(0, rows // step_rows, conv_step, (zero,) * (KERNEL + 1))
        for tap in range(KERNEL + 1):
            taps_ref[head, tap : tap + 1, :] = jnp.sum(sums[tap], axis=0, keepdims=True)
        shift_all()

        def back_step(index, carry, head=head):
            total = loaded(g_n.at[head], index) + filtered(head, index, True)
            total = total.reshape(step_rows, depth)
            frame_at = index * step_rows + lax.broadcasted_iota(jnp.int32, total.shape, 0)
            total = jnp.where(frame_at < length, total, 0.0)
            at = pl.ds(pl.multiple_of(index * step_rows, step_rows), step_rows)
            a_n[head, at, :] = total.astype(bf16)
            return carry

        lax.fori_loop(0, rows // step_rows, back_step, 0)
        for first in range(0, rows, frames):
            a_t[span(head), first : first + frames] = a_n[head, first : first + frames, :].T

    def backward(index, head):
        cols = pl.ds(pl.multiple_of(index * block, block), block)
        score_grad = jnp.dot(v_n[head], a_t[span(head), cols], preferred_element_type=f32)
        found = probs[head, :, cols]
        delta = jnp.sum(found * score_grad, axis=0, keepdims=True)
        diff = (found * (score_grad - delta)).astype(bf16)
        value = jnp.dot(found.astype(bf16), a_n[head, cols, :], preferred_element_type=f32)
        key = jnp.dot(diff, q_n[head, cols, :], preferred_element_type=f32)
        query = jnp.dot(k_t[span(head), :], diff, preferred_element_type=f32)
        q_t[span(head), cols] = (query * scale).astype(bf16)
        return key, value

    def finish(head, key, value):
        for first in range(0, rows, frames):
            at = slice(first, first + frames)
            k_t[span(head), at] = (key[at, :] * scale).astype(bf16).T
            v_t[span(head), at] = value[at, :].astype(bf16).T

    for head in range(heads):
        if blocks == 1:
            finish(head, *backward(0, head))
        else:
            zeros = jnp.zeros((rows, depth), f32)

            def step(index, carry, head=head):
                key, value = backward(index, head)
                return carry[0] + key, carry[1] + value

            finish(head, *lax.fori_loop(0, blocks, step, (zeros, zeros)))

    for distance, out in enumerate(outs):
        at = pl.ds(pl.multiple_of((rank ^ distance) * frames, 128), frames)
        out[0] = q_t[:, at]
        out[1] = k_t[:, at]
        out[2] = v_t[:, at]


def core(scalars, weight, bias, pieces):
    count = len(pieces)
    _, high, frames = pieces[0].shape
    heads, _, depth = weight.shape
    rows = count * frames
    block = math.gcd(rows, 512)
    tall = rows + 2 * PAD + 8
    piece = jax.ShapeDtypeStruct((3, high, frames), bf16)
    turned = pltpu.VMEM((high, rows), bf16)
    plain = pltpu.VMEM((heads, rows, depth), bf16)
    outs = pl.pallas_call(
        functools.partial(core_kernel, count, block),
        out_shape=(piece,) * count + (jax.ShapeDtypeStruct((heads, KERNEL + 1, depth), f32),),
        in_specs=[SMEM] + [VMEM] * (2 + count),
        out_specs=(VMEM,) * (count + 1),
        scratch_shapes=[turned] * 4
        + [plain] * 5
        + [
            pltpu.VMEM((heads, rows, rows), f32),
            pltpu.VMEM((8, tall // 8 - 1, 8, depth), f32),
            pltpu.VMEM((tall, depth), f32),
        ],
        compiler_params=pltpu.CompilerParams(
            vmem_limit_bytes=12 * 2**20 + 8 * heads * rows * rows + 4096 * tall
        ),
        cost_estimate=pl.CostEstimate(
            flops=24 * rows * rows * high,
            bytes_accessed=14 * rows * high,
            transcendentals=heads * rows * rows,
        ),
    )(scalars, weight, bias, *[pieces[distance] for distance in taken(count)])
    return outs[:count], outs[count]


def exchanged(pieces, before):
    pieces, order = list(pieces), taken(len(pieces))[1:]
    if before is not None and len(pieces) > 2:
        sent, here = lax.optimization_barrier(
            ([pieces[distance] for distance in order[:-1]], [before[distance] for distance in order])
        )
        for distance, piece, arrived in zip(order, sent + [pieces[1]], here):
            pieces[distance], before[distance] = piece, arrived
    moved = list(pieces)
    for distance in order:
        pairs = [(i, i ^ distance) for i in range(len(pieces))]
        moved[distance] = lax.ppermute(pieces[distance], "seq", pairs)
    return moved


def doubled(array, axis):
    count = lax.axis_size(axis)
    pair, distance = (array, jnp.zeros_like(array)), 1
    while distance < count:
        total = array if distance == 1 else pair[0] + pair[1]
        pairs = [(i, i ^ distance) for i in range(count)]
        pair = (total, lax.ppermute(total, axis, pairs))
        distance *= 2
    return pair


def on_device(queries, keys, values, grad_out, conv_weight, conv_bias, lengths):
    count = lax.axis_size("seq")
    rank = lax.axis_index("seq").astype(jnp.int32)
    width = queries.shape[2]
    depth = width // HEADS
    heads = HEADS // count
    chunks = math.gcd(heads, 2)
    step = heads // chunks
    by_head = conv_weight.reshape(KERNEL, HEADS, depth).transpose(1, 0, 2)
    weight = lax.dynamic_slice_in_dim(by_head, rank * heads, heads, axis=0)
    bias = lax.dynamic_slice_in_dim(conv_bias.reshape(HEADS, 1, depth), rank * heads, heads, axis=0)
    scalars = jnp.stack([lengths[0], rank])
    sent = pack(rank[None], (queries, keys, values, grad_out), count, chunks)
    order = []
    for pieces in sent:
        order.append(exchanged(pieces, order[-1] if order else None))
    taps = []
    for chunk in range(chunks):
        at = slice(chunk * step, (chunk + 1) * step)
        grads, part = core(scalars, weight[at], bias[at], order[chunk])
        taps.append(part)
        if chunk < chunks - 1:
            order.append(exchanged(grads, order[-1]))
    before, grads, taps = order[-1], list(grads), jnp.concatenate(taps, axis=0)
    last = count - 1
    grads[last - 1], before[1] = lax.optimization_barrier((grads[last - 1], before[1]))
    if last > 2:
        (grads[1], taps), before[2] = lax.optimization_barrier(((grads[1], taps), before[2]))
        grads[last], before[last] = lax.optimization_barrier((grads[last], before[last]))
    order.append(exchanged(grads, None))
    return unpack(rank[None], doubled(taps, "dp"), order[chunks:], count, chunks)


def solution(mesh):
    return jax.shard_map(
        on_device,
        mesh=mesh,
        in_specs=(
            P("dp", "seq", None),
            P("dp", "seq", None),
            P("dp", "seq", None),
            P("dp", "seq", None),
            P(),
            P(),
            P("dp"),
        ),
        out_specs=(
            P("dp", "seq", None),
            P("dp", "seq", None),
            P("dp", "seq", None),
            P(None, "seq"),
            P("seq"),
        ),
        check_vma=False,
    )
```

```python
import functools
import math

import jax
import jax.numpy as jnp
from jax import lax
from jax.experimental import pallas as pl
from jax.experimental.pallas import tpu as pltpu
from jax.sharding import PartitionSpec as P

HEADS = 16
KERNEL = 31
PAD = 16
masked_score = -1e30
VMEM = pl.BlockSpec(memory_space=pltpu.VMEM)
SMEM = pl.BlockSpec(memory_space=pltpu.SMEM)
LIMIT = 16 * 1024 * 1024
bf16, f32 = jnp.bfloat16, jnp.float32


def pack_first_kernel(far, share, rank_ref, *refs):
    arrays, outs, (plain, sems) = refs[:4], refs[4:-2], refs[-2:]
    high = outs[0].shape[1]
    wide = plain.shape[3]
    copies = []
    for place, distance in enumerate(far):
        at = pl.ds(pl.multiple_of((rank_ref[0] ^ distance) * share, 128), wide)
        for which, array in enumerate(arrays):
            copies.append(
                pltpu.make_async_copy(
                    array.at[0, :, at], plain.at[place, which], sems.at[place, which]
                )
            )
            copies[-1].start()
    for index, copy in enumerate(copies):
        copy.wait()
        place, which = divmod(index, 4)
        outs[place][which] = plain[place, which].T[:high]


def pack_kernel(wanted, share, rank_ref, *refs):
    arrays, outs, turned = refs[:4], refs[4:-1], refs[-1]
    high = outs[0].shape[1]
    for which, array in enumerate(arrays):
        turned[which] = array[0].T
        for (chunk, distance), out in zip(wanted, outs):
            first = pl.multiple_of((rank_ref[0] ^ distance) * share + chunk * high, 16)
            out[which] = turned[which, pl.ds(first, high), :]


def pack(rank, arrays, count, chunks):
    _, frames, width = arrays[0].shape
    share = width // count
    high = share // chunks
    piece = jax.ShapeDtypeStruct((4, high, frames), bf16)
    wide = -(-high // 128) * 128
    far = tuple(range(count - 1, 1, -1)) if share % 128 == 0 and wide <= share else ()
    params = pltpu.CompilerParams(vmem_limit_bytes=LIMIT)
    arrays = [pltpu.with_memory_space_constraint(array, pltpu.HBM) for array in arrays]
    found = {}
    if far:
        outs = pl.pallas_call(
            functools.partial(pack_first_kernel, far, share),
            out_shape=(piece,) * len(far),
            in_specs=[SMEM] + [pl.BlockSpec(memory_space=pltpu.HBM)] * 4,
            out_specs=(VMEM,) * len(far),
            scratch_shapes=[
                pltpu.VMEM((len(far), 4, frames, wide), bf16),
                pltpu.SemaphoreType.DMA((len(far), 4)),
            ],
            compiler_params=params,
            cost_estimate=pl.CostEstimate(
                flops=0, bytes_accessed=16 * frames * wide * len(far), transcendentals=0
            ),
        )(rank, *arrays)
        found.update(zip([(0, distance) for distance in far], outs))
    every = [(chunk, distance) for chunk in range(chunks) for distance in range(count)]
    wanted = tuple(key for key in every if key not in found)
    outs = pl.pallas_call(
        functools.partial(pack_kernel, wanted, share),
        out_shape=(piece,) * len(wanted),
        in_specs=[SMEM] + [VMEM] * 4,
        out_specs=(VMEM,) * len(wanted),
        scratch_shapes=[pltpu.VMEM((4, width, frames), bf16)],
        compiler_params=params,
        cost_estimate=pl.CostEstimate(
            flops=0, bytes_accessed=16 * frames * width, transcendentals=0
        ),
    )(rank, *arrays)
    found.update(zip(wanted, outs))
    return [[found[chunk, distance] for distance in range(count)] for chunk in range(chunks)]


def taken(count):
    return [0] + list(range(count - 1, 0, -1))


def returned(count):
    return [0] + list(range(2, count)) + [1]


def unpack_kernel(count, chunks, rank_ref, *refs):
    pieces, refs = refs[: count * chunks], refs[count * chunks :]
    taps_refs, outs = refs[:-7], refs[-7:-4]
    weight_ref, bias_ref, bias_row, turned = refs[-4:]
    rank = rank_ref[0]
    high = pieces[0].shape[1]
    share = high * chunks
    for which, out in enumerate(outs):
        for chunk in range(chunks):
            for place, distance in enumerate(returned(count)):
                first = pl.multiple_of((rank ^ distance) * share + chunk * high, 16)
                turned[which, pl.ds(first, high), :] = pieces[chunk * count + place][which]
        out[0] = turned[which].T
    taps = taps_refs[0][...] + taps_refs[1][...]
    heads, _, depth = taps.shape
    for head in range(heads):
        at = slice(head * depth, (head + 1) * depth)
        weight_ref[:, at] = taps[head, :KERNEL]
        bias_row[:, at] = taps[head, KERNEL:]
    bias_ref[...] = bias_row[0]


def unpack(rank, taps, pieces, count, chunks):
    _, high, frames = pieces[0][0].shape
    width = high * count * chunks
    whole = jax.ShapeDtypeStruct((1, frames, width), bf16)
    return pl.pallas_call(
        functools.partial(unpack_kernel, count, chunks),
        out_shape=(whole,) * 3
        + (
            jax.ShapeDtypeStruct((KERNEL, width // count), f32),
            jax.ShapeDtypeStruct((width // count,), f32),
        ),
        in_specs=[SMEM] + [VMEM] * (count * chunks + len(taps)),
        out_specs=(VMEM,) * 5,
        scratch_shapes=[
            pltpu.VMEM((1, width // count), f32),
            pltpu.VMEM((3, width, frames), bf16),
        ],
        compiler_params=pltpu.CompilerParams(vmem_limit_bytes=LIMIT),
        cost_estimate=pl.CostEstimate(
            flops=0, bytes_accessed=12 * frames * width, transcendentals=0
        ),
    )(rank, *[part[distance] for part in pieces for distance in returned(count)], *taps)


def core_kernel(count, block, scalars, weight_ref, bias_ref, *refs):
    pieces, outs, taps_ref = refs[:count], refs[count : 2 * count], refs[2 * count]
    q_t, k_t, v_t, a_t, q_n, k_n, v_n, g_n, a_n, probs, shifted, padded = refs[2 * count + 1 :]
    heads, rows, depth = q_n.shape
    frames = pieces[0].shape[2]
    blocks = rows // block
    scale = 1.0 / math.sqrt(depth)
    log_scale = scale * math.log2(math.e)
    length, rank = scalars[0], scalars[1]

    def span(head):
        return slice(head * depth, (head + 1) * depth)

    for distance, piece in zip(taken(count), pieces):
        at = pl.ds(pl.multiple_of((rank ^ distance) * frames, 128), frames)
        q_t[:, at] = piece[0]
        k_t[:, at] = piece[1]
        v_t[:, at] = piece[2]
        for head in range(heads):
            q_n[head, at, :] = piece[0, span(head), :].T
            k_n[head, at, :] = piece[1, span(head), :].T
            v_n[head, at, :] = piece[2, span(head), :].T
            g_n[head, at, :] = piece[3, span(head), :].T

    def forward(index, head):
        cols = pl.ds(pl.multiple_of(index * block, block), block)
        scores = jnp.dot(k_n[head], q_t[span(head), cols], preferred_element_type=f32)
        key_at = lax.broadcasted_iota(jnp.int32, scores.shape, 0)
        scores = jnp.where(key_at < length, scores, masked_score)
        exped = jnp.exp2((scores - jnp.max(scores, axis=0, keepdims=True)) * log_scale)
        found = exped * (1.0 / jnp.sum(exped, axis=0, keepdims=True))
        probs[head, :, cols] = found
        out = jnp.dot(v_t[span(head), :], found.astype(bf16), preferred_element_type=f32)
        frame_at = index * block + lax.broadcasted_iota(jnp.int32, out.shape, 1)
        a_t[span(head), cols] = jnp.where(frame_at < length, out, 0.0).astype(bf16)

    def each_block(body):
        if blocks == 1:
            for head in range(heads):
                body(0, head)
        else:

            def step(index, carry):
                for head in range(heads):
                    body(index, head)
                return carry

            lax.fori_loop(0, blocks, step, 0)

    each_block(forward)

    tall = padded.shape[0]
    padded[0:PAD, :] = jnp.zeros((PAD, depth), f32)
    padded[PAD + rows : tall, :] = jnp.zeros((tall - PAD - rows, depth), f32)

    def shift_all():
        for s in range(8):
            shifted[s] = padded[s : s + tall - 8, :].reshape(tall // 8 - 1, 8, depth)

    step_tiles = 8
    step_rows = 8 * step_tiles

    def window(index, offset):
        return shifted[offset % 8, pl.ds(index * step_tiles + offset // 8, step_tiles)]

    def filtered(head, index, reverse):
        total = None
        for offset in range(1, KERNEL + 1):
            tap = KERNEL - offset if reverse else offset - 1
            term = weight_ref[head, tap : tap + 1, :] * window(index, offset)
            total = term if total is None else total + term
        return total

    def loaded(ref, index):
        at = pl.ds(pl.multiple_of(index * step_rows, step_rows), step_rows)
        return ref[at, :].astype(f32).reshape(step_tiles, 8, depth)

    for head in range(heads):
        for first in range(0, rows, frames):
            at = slice(PAD + first, PAD + first + frames)
            padded[at, :] = a_t[span(head), first : first + frames].T.astype(f32)
        shift_all()

        def conv_step(index, carry, head=head):
            conv_pre = filtered(head, index, False) + bias_ref[head]
            sig = 1.0 / (1.0 + jnp.exp(-conv_pre))
            pre = loaded(g_n.at[head], index) * (sig * (1.0 + conv_pre * (1.0 - sig)))
            pre = pre.astype(bf16).astype(f32)
            at = pl.ds(pl.multiple_of(PAD + index * step_rows, PAD), step_rows)
            padded[at, :] = pre.reshape(step_rows, depth)
            new = []
            for offset in range(1, KERNEL + 1):
                new.append(carry[offset - 1] + jnp.sum(pre * window(index, offset), axis=0))
            new.append(carry[KERNEL] + jnp.sum(pre, axis=0))
            return tuple(new)

        zero = jnp.zeros((8, depth), f32)
        sums = lax.fori_loop(0, rows // step_rows, conv_step, (zero,) * (KERNEL + 1))
        for tap in range(KERNEL + 1):
            taps_ref[head, tap : tap + 1, :] = jnp.sum(sums[tap], axis=0, keepdims=True)
        shift_all()

        def back_step(index, carry, head=head):
            total = loaded(g_n.at[head], index) + filtered(head, index, True)
            total = total.reshape(step_rows, depth)
            frame_at = index * step_rows + lax.broadcasted_iota(jnp.int32, total.shape, 0)
            total = jnp.where(frame_at < length, total, 0.0)
            at = pl.ds(pl.multiple_of(index * step_rows, step_rows), step_rows)
            a_n[head, at, :] = total.astype(bf16)
            return carry

        lax.fori_loop(0, rows // step_rows, back_step, 0)
        for first in range(0, rows, frames):
            a_t[span(head), first : first + frames] = a_n[head, first : first + frames, :].T

    def backward(index, head):
        cols = pl.ds(pl.multiple_of(index * block, block), block)
        score_grad = jnp.dot(v_n[head], a_t[span(head), cols], preferred_element_type=f32)
        found = probs[head, :, cols]
        delta = jnp.sum(found * score_grad, axis=0, keepdims=True)
        diff = (found * (score_grad - delta)).astype(bf16)
        value = jnp.dot(found.astype(bf16), a_n[head, cols, :], preferred_element_type=f32)
        key = jnp.dot(diff, q_n[head, cols, :], preferred_element_type=f32)
        query = jnp.dot(k_t[span(head), :], diff, preferred_element_type=f32)
        q_t[span(head), cols] = (query * scale).astype(bf16)
        return key, value

    def finish(head, key, value):
        for first in range(0, rows, frames):
            at = slice(first, first + frames)
            k_t[span(head), at] = (key[at, :] * scale).astype(bf16).T
            v_t[span(head), at] = value[at, :].astype(bf16).T

    for head in range(heads):
        if blocks == 1:
            finish(head, *backward(0, head))
        else:
            zeros = jnp.zeros((rows, depth), f32)

            def step(index, carry, head=head):
                key, value = backward(index, head)
                return carry[0] + key, carry[1] + value

            finish(head, *lax.fori_loop(0, blocks, step, (zeros, zeros)))

    for distance, out in enumerate(outs):
        at = pl.ds(pl.multiple_of((rank ^ distance) * frames, 128), frames)
        out[0] = q_t[:, at]
        out[1] = k_t[:, at]
        out[2] = v_t[:, at]


def core(scalars, weight, bias, pieces):
    count = len(pieces)
    _, high, frames = pieces[0].shape
    heads, _, depth = weight.shape
    rows = count * frames
    block = math.gcd(rows, 512)
    tall = rows + 2 * PAD + 8
    piece = jax.ShapeDtypeStruct((3, high, frames), bf16)
    turned = pltpu.VMEM((high, rows), bf16)
    plain = pltpu.VMEM((heads, rows, depth), bf16)
    outs = pl.pallas_call(
        functools.partial(core_kernel, count, block),
        out_shape=(piece,) * count + (jax.ShapeDtypeStruct((heads, KERNEL + 1, depth), f32),),
        in_specs=[SMEM] + [VMEM] * (2 + count),
        out_specs=(VMEM,) * (count + 1),
        scratch_shapes=[turned] * 4
        + [plain] * 5
        + [
            pltpu.VMEM((heads, rows, rows), f32),
            pltpu.VMEM((8, tall // 8 - 1, 8, depth), f32),
            pltpu.VMEM((tall, depth), f32),
        ],
        compiler_params=pltpu.CompilerParams(
            vmem_limit_bytes=12 * 2**20 + 8 * heads * rows * rows + 4096 * tall
        ),
        cost_estimate=pl.CostEstimate(
            flops=24 * rows * rows * high,
            bytes_accessed=14 * rows * high,
            transcendentals=heads * rows * rows,
        ),
    )(scalars, weight, bias, *[pieces[distance] for distance in taken(count)])
    return outs[:count], outs[count]


def exchanged(pieces, before, farthest_first=True):
    pieces = list(pieces)
    if before is not None and len(pieces) > 2:
        pieces[:1:-1], before[:0:-1] = lax.optimization_barrier((pieces[:1:-1], before[:0:-1]))
    moved = pieces[:1] * len(pieces)
    order = range(1, len(pieces))
    for distance in reversed(order) if farthest_first else [*order[1:], 1]:
        pairs = [(i, i ^ distance) for i in range(len(pieces))]
        moved[distance] = lax.ppermute(pieces[distance], "seq", pairs)
    return moved


def doubled(array, axis):
    count = lax.axis_size(axis)
    pair, distance = (array, jnp.zeros_like(array)), 1
    while distance < count:
        total = array if distance == 1 else pair[0] + pair[1]
        pairs = [(i, i ^ distance) for i in range(count)]
        pair = (total, lax.ppermute(total, axis, pairs))
        distance *= 2
    return pair


def on_device(queries, keys, values, grad_out, conv_weight, conv_bias, lengths):
    count = lax.axis_size("seq")
    rank = lax.axis_index("seq").astype(jnp.int32)
    width = queries.shape[2]
    depth = width // HEADS
    heads = HEADS // count
    chunks = math.gcd(heads, 2)
    step = heads // chunks
    by_head = conv_weight.reshape(KERNEL, HEADS, depth).transpose(1, 0, 2)
    weight = lax.dynamic_slice_in_dim(by_head, rank * heads, heads, axis=0)
    bias = lax.dynamic_slice_in_dim(conv_bias.reshape(HEADS, 1, depth), rank * heads, heads, axis=0)
    scalars = jnp.stack([lengths[0], rank])
    sent = pack(rank[None], (queries, keys, values, grad_out), count, chunks)
    order = []
    for pieces in sent:
        order.append(exchanged(pieces, order[-1] if order else None))
    taps = []
    for chunk in range(chunks):
        at = slice(chunk * step, (chunk + 1) * step)
        grads, part = core(scalars, weight[at], bias[at], order[chunk])
        taps.append(part)
        if chunk < chunks - 1:
            order.append(exchanged(grads, order[-1], False))
    before, grads, taps = order[-1], list(grads), jnp.concatenate(taps, axis=0)
    last = count - 1
    grads[last - 1], before[1] = lax.optimization_barrier((grads[last - 1], before[1]))
    if last > 2:
        (grads[1], taps), before[2] = lax.optimization_barrier(((grads[1], taps), before[2]))
        grads[last], before[last] = lax.optimization_barrier((grads[last], before[last]))
    order.append(exchanged(grads, None, False))
    return unpack(rank[None], doubled(taps, "dp"), order[chunks:], count, chunks)


def solution(mesh):
    return jax.shard_map(
        on_device,
        mesh=mesh,
        in_specs=(
            P("dp", "seq", None),
            P("dp", "seq", None),
            P("dp", "seq", None),
            P("dp", "seq", None),
            P(),
            P(),
            P("dp"),
        ),
        out_specs=(
            P("dp", "seq", None),
            P("dp", "seq", None),
            P("dp", "seq", None),
            P(None, "seq"),
            P("seq"),
        ),
        check_vma=False,
    )
```

```python
import functools
import math

import jax
import jax.numpy as jnp
from jax import lax
from jax.experimental import pallas as pl
from jax.experimental.pallas import tpu as pltpu
from jax.sharding import PartitionSpec as P

HEADS = 16
KERNEL = 31
PAD = 16
masked_score = -1e30
VMEM = pl.BlockSpec(memory_space=pltpu.VMEM)
SMEM = pl.BlockSpec(memory_space=pltpu.SMEM)
LIMIT = 16 * 1024 * 1024
bf16, f32 = jnp.bfloat16, jnp.float32


def pack_first_kernel(far, share, rank_ref, *refs):
    arrays, outs, (plain, sems) = refs[:4], refs[4:-2], refs[-2:]
    high = outs[0].shape[1]
    wide = plain.shape[3]
    copies = []
    for place, distance in enumerate(far):
        at = pl.ds(pl.multiple_of((rank_ref[0] ^ distance) * share, 128), wide)
        for which, array in enumerate(arrays):
            copies.append(
                pltpu.make_async_copy(
                    array.at[0, :, at], plain.at[place, which], sems.at[place, which]
                )
            )
            copies[-1].start()
    for index, copy in enumerate(copies):
        copy.wait()
        place, which = divmod(index, 4)
        outs[place][which] = plain[place, which].T[:high]


def pack_kernel(wanted, share, rank_ref, *refs):
    arrays, outs, turned = refs[:4], refs[4:-1], refs[-1]
    high = outs[0].shape[1]
    for which, array in enumerate(arrays):
        turned[which] = array[0].T
        for (chunk, distance), out in zip(wanted, outs):
            first = pl.multiple_of((rank_ref[0] ^ distance) * share + chunk * high, 16)
            out[which] = turned[which, pl.ds(first, high), :]


def pack(rank, arrays, count, chunks):
    _, frames, width = arrays[0].shape
    share = width // count
    high = share // chunks
    piece = jax.ShapeDtypeStruct((4, high, frames), bf16)
    wide = -(-high // 128) * 128
    far = tuple(range(count - 1, 1, -1)) if share % 128 == 0 and wide <= share else ()
    params = pltpu.CompilerParams(vmem_limit_bytes=LIMIT)
    arrays = [pltpu.with_memory_space_constraint(array, pltpu.HBM) for array in arrays]
    found = {}
    if far:
        outs = pl.pallas_call(
            functools.partial(pack_first_kernel, far, share),
            out_shape=(piece,) * len(far),
            in_specs=[SMEM] + [pl.BlockSpec(memory_space=pltpu.HBM)] * 4,
            out_specs=(VMEM,) * len(far),
            scratch_shapes=[
                pltpu.VMEM((len(far), 4, frames, wide), bf16),
                pltpu.SemaphoreType.DMA((len(far), 4)),
            ],
            compiler_params=params,
            cost_estimate=pl.CostEstimate(
                flops=0, bytes_accessed=16 * frames * wide * len(far), transcendentals=0
            ),
        )(rank, *arrays)
        found.update(zip([(0, distance) for distance in far], outs))
    every = [(chunk, distance) for chunk in range(chunks) for distance in range(count)]
    wanted = tuple(key for key in every if key not in found)
    outs = pl.pallas_call(
        functools.partial(pack_kernel, wanted, share),
        out_shape=(piece,) * len(wanted),
        in_specs=[SMEM] + [VMEM] * 4,
        out_specs=(VMEM,) * len(wanted),
        scratch_shapes=[pltpu.VMEM((4, width, frames), bf16)],
        compiler_params=params,
        cost_estimate=pl.CostEstimate(
            flops=0, bytes_accessed=16 * frames * width, transcendentals=0
        ),
    )(rank, *arrays)
    found.update(zip(wanted, outs))
    return [[found[chunk, distance] for distance in range(count)] for chunk in range(chunks)]


def taken(count):
    return [0] + list(range(count - 1, 0, -1))


def returned(count):
    return [0] + list(range(2, count)) + [1]


def unpack_kernel(count, chunks, rank_ref, *refs):
    pieces, refs = refs[: count * chunks], refs[count * chunks :]
    taps_refs, outs = refs[:-7], refs[-7:-4]
    weight_ref, bias_ref, bias_row, turned = refs[-4:]
    rank = rank_ref[0]
    high = pieces[0].shape[1]
    share = high * chunks
    for which, out in enumerate(outs):
        for chunk in range(chunks):
            for place, distance in enumerate(returned(count)):
                first = pl.multiple_of((rank ^ distance) * share + chunk * high, 16)
                turned[which, pl.ds(first, high), :] = pieces[chunk * count + place][which]
        out[0] = turned[which].T
    taps = taps_refs[0][...] + taps_refs[1][...]
    heads, _, depth = taps.shape
    for head in range(heads):
        at = slice(head * depth, (head + 1) * depth)
        weight_ref[:, at] = taps[head, :KERNEL]
        bias_row[:, at] = taps[head, KERNEL:]
    bias_ref[...] = bias_row[0]


def unpack(rank, taps, pieces, count, chunks):
    _, high, frames = pieces[0][0].shape
    width = high * count * chunks
    whole = jax.ShapeDtypeStruct((1, frames, width), bf16)
    return pl.pallas_call(
        functools.partial(unpack_kernel, count, chunks),
        out_shape=(whole,) * 3
        + (
            jax.ShapeDtypeStruct((KERNEL, width // count), f32),
            jax.ShapeDtypeStruct((width // count,), f32),
        ),
        in_specs=[SMEM] + [VMEM] * (count * chunks + len(taps)),
        out_specs=(VMEM,) * 5,
        scratch_shapes=[
            pltpu.VMEM((1, width // count), f32),
            pltpu.VMEM((3, width, frames), bf16),
        ],
        compiler_params=pltpu.CompilerParams(vmem_limit_bytes=LIMIT),
        cost_estimate=pl.CostEstimate(
            flops=0, bytes_accessed=12 * frames * width, transcendentals=0
        ),
    )(rank, *[part[distance] for part in pieces for distance in returned(count)], *taps)


def core_kernel(count, block, scalars, weight_ref, bias_ref, *refs):
    pieces, outs, taps_ref = refs[:count], refs[count : 2 * count], refs[2 * count]
    q_t, k_t, v_t, a_t, q_n, k_n, v_n, g_n, a_n, probs, shifted, padded = refs[2 * count + 1 :]
    heads, rows, depth = q_n.shape
    frames = pieces[0].shape[2]
    blocks = rows // block
    scale = 1.0 / math.sqrt(depth)
    log_scale = scale * math.log2(math.e)
    length, rank = scalars[0], scalars[1]

    def span(head):
        return slice(head * depth, (head + 1) * depth)

    for distance, piece in zip(taken(count), pieces):
        at = pl.ds(pl.multiple_of((rank ^ distance) * frames, 128), frames)
        q_t[:, at] = piece[0]
        k_t[:, at] = piece[1]
        v_t[:, at] = piece[2]
        for head in range(heads):
            q_n[head, at, :] = piece[0, span(head), :].T
            k_n[head, at, :] = piece[1, span(head), :].T
            v_n[head, at, :] = piece[2, span(head), :].T
            g_n[head, at, :] = piece[3, span(head), :].T

    def forward(index, head):
        cols = pl.ds(pl.multiple_of(index * block, block), block)
        scores = jnp.dot(k_n[head], q_t[span(head), cols], preferred_element_type=f32)
        key_at = lax.broadcasted_iota(jnp.int32, scores.shape, 0)
        scores = jnp.where(key_at < length, scores, masked_score)
        exped = jnp.exp2((scores - jnp.max(scores, axis=0, keepdims=True)) * log_scale)
        found = exped * (1.0 / jnp.sum(exped, axis=0, keepdims=True))
        probs[head, :, cols] = found
        out = jnp.dot(v_t[span(head), :], found.astype(bf16), preferred_element_type=f32)
        frame_at = index * block + lax.broadcasted_iota(jnp.int32, out.shape, 1)
        a_t[span(head), cols] = jnp.where(frame_at < length, out, 0.0).astype(bf16)

    def each_block(body):
        if blocks == 1:
            for head in range(heads):
                body(0, head)
        else:

            def step(index, carry):
                for head in range(heads):
                    body(index, head)
                return carry

            lax.fori_loop(0, blocks, step, 0)

    each_block(forward)

    tall = padded.shape[0]
    padded[0:PAD, :] = jnp.zeros((PAD, depth), f32)
    padded[PAD + rows : tall, :] = jnp.zeros((tall - PAD - rows, depth), f32)

    def shift_all():
        for s in range(8):
            shifted[s] = padded[s : s + tall - 8, :].reshape(tall // 8 - 1, 8, depth)

    step_tiles = 8
    step_rows = 8 * step_tiles

    def window(index, offset):
        return shifted[offset % 8, pl.ds(index * step_tiles + offset // 8, step_tiles)]

    def filtered(head, index, reverse):
        total = None
        for offset in range(1, KERNEL + 1):
            tap = KERNEL - offset if reverse else offset - 1
            term = weight_ref[head, tap : tap + 1, :] * window(index, offset)
            total = term if total is None else total + term
        return total

    def loaded(ref, index):
        at = pl.ds(pl.multiple_of(index * step_rows, step_rows), step_rows)
        return ref[at, :].astype(f32).reshape(step_tiles, 8, depth)

    for head in range(heads):
        for first in range(0, rows, frames):
            at = slice(PAD + first, PAD + first + frames)
            padded[at, :] = a_t[span(head), first : first + frames].T.astype(f32)
        shift_all()

        def conv_step(index, carry, head=head):
            conv_pre = filtered(head, index, False) + bias_ref[head]
            sig = 1.0 / (1.0 + jnp.exp(-conv_pre))
            pre = loaded(g_n.at[head], index) * (sig * (1.0 + conv_pre * (1.0 - sig)))
            pre = pre.astype(bf16).astype(f32)
            at = pl.ds(pl.multiple_of(PAD + index * step_rows, PAD), step_rows)
            padded[at, :] = pre.reshape(step_rows, depth)
            new = []
            for offset in range(1, KERNEL + 1):
                new.append(carry[offset - 1] + jnp.sum(pre * window(index, offset), axis=0))
            new.append(carry[KERNEL] + jnp.sum(pre, axis=0))
            return tuple(new)

        zero = jnp.zeros((8, depth), f32)
        sums = lax.fori_loop(0, rows // step_rows, conv_step, (zero,) * (KERNEL + 1))
        for tap in range(KERNEL + 1):
            taps_ref[head, tap : tap + 1, :] = jnp.sum(sums[tap], axis=0, keepdims=True)
        shift_all()

        def back_step(index, carry, head=head):
            total = loaded(g_n.at[head], index) + filtered(head, index, True)
            total = total.reshape(step_rows, depth)
            frame_at = index * step_rows + lax.broadcasted_iota(jnp.int32, total.shape, 0)
            total = jnp.where(frame_at < length, total, 0.0)
            at = pl.ds(pl.multiple_of(index * step_rows, step_rows), step_rows)
            a_n[head, at, :] = total.astype(bf16)
            return carry

        lax.fori_loop(0, rows // step_rows, back_step, 0)
        for first in range(0, rows, frames):
            a_t[span(head), first : first + frames] = a_n[head, first : first + frames, :].T

    def backward(index, head):
        cols = pl.ds(pl.multiple_of(index * block, block), block)
        score_grad = jnp.dot(v_n[head], a_t[span(head), cols], preferred_element_type=f32)
        found = probs[head, :, cols]
        delta = jnp.sum(found * score_grad, axis=0, keepdims=True)
        diff = (found * (score_grad - delta)).astype(bf16)
        value = jnp.dot(found.astype(bf16), a_n[head, cols, :], preferred_element_type=f32)
        key = jnp.dot(diff, q_n[head, cols, :], preferred_element_type=f32)
        query = jnp.dot(k_t[span(head), :], diff, preferred_element_type=f32)
        q_t[span(head), cols] = (query * scale).astype(bf16)
        return key, value

    def finish(head, key, value):
        for first in range(0, rows, frames):
            at = slice(first, first + frames)
            k_t[span(head), at] = (key[at, :] * scale).astype(bf16).T
            v_t[span(head), at] = value[at, :].astype(bf16).T

    for head in range(heads):
        if blocks == 1:
            finish(head, *backward(0, head))
        else:
            zeros = jnp.zeros((rows, depth), f32)

            def step(index, carry, head=head):
                key, value = backward(index, head)
                return carry[0] + key, carry[1] + value

            finish(head, *lax.fori_loop(0, blocks, step, (zeros, zeros)))

    for distance, out in enumerate(outs):
        at = pl.ds(pl.multiple_of((rank ^ distance) * frames, 128), frames)
        out[0] = q_t[:, at]
        out[1] = k_t[:, at]
        out[2] = v_t[:, at]


def core(scalars, weight, bias, pieces):
    count = len(pieces)
    _, high, frames = pieces[0].shape
    heads, _, depth = weight.shape
    rows = count * frames
    block = math.gcd(rows, 512)
    tall = rows + 2 * PAD + 8
    piece = jax.ShapeDtypeStruct((3, high, frames), bf16)
    turned = pltpu.VMEM((high, rows), bf16)
    plain = pltpu.VMEM((heads, rows, depth), bf16)
    outs = pl.pallas_call(
        functools.partial(core_kernel, count, block),
        out_shape=(piece,) * count + (jax.ShapeDtypeStruct((heads, KERNEL + 1, depth), f32),),
        in_specs=[SMEM] + [VMEM] * (2 + count),
        out_specs=(VMEM,) * (count + 1),
        scratch_shapes=[turned] * 4
        + [plain] * 5
        + [
            pltpu.VMEM((heads, rows, rows), f32),
            pltpu.VMEM((8, tall // 8 - 1, 8, depth), f32),
            pltpu.VMEM((tall, depth), f32),
        ],
        compiler_params=pltpu.CompilerParams(
            vmem_limit_bytes=12 * 2**20 + 8 * heads * rows * rows + 4096 * tall
        ),
        cost_estimate=pl.CostEstimate(
            flops=24 * rows * rows * high,
            bytes_accessed=14 * rows * high,
            transcendentals=heads * rows * rows,
        ),
    )(scalars, weight, bias, *[pieces[distance] for distance in taken(count)])
    return outs[:count], outs[count]


def exchanged(pieces, before, farthest_first=True):
    pieces = list(pieces)
    if before is not None and len(pieces) > 2:
        pieces[:1:-1], before[:0:-1] = lax.optimization_barrier((pieces[:1:-1], before[:0:-1]))
    moved = pieces[:1] * len(pieces)
    order = range(1, len(pieces))
    for distance in reversed(order) if farthest_first else [*order[1:], 1]:
        pairs = [(i, i ^ distance) for i in range(len(pieces))]
        moved[distance] = lax.ppermute(pieces[distance], "seq", pairs)
    return moved


def doubled(array, axis):
    count = lax.axis_size(axis)
    pair, distance = (array, jnp.zeros_like(array)), 1
    while distance < count:
        total = array if distance == 1 else pair[0] + pair[1]
        pairs = [(i, i ^ distance) for i in range(count)]
        pair = (total, lax.ppermute(total, axis, pairs))
        distance *= 2
    return pair


def on_device(queries, keys, values, grad_out, conv_weight, conv_bias, lengths):
    count = lax.axis_size("seq")
    rank = lax.axis_index("seq").astype(jnp.int32)
    width = queries.shape[2]
    depth = width // HEADS
    heads = HEADS // count
    chunks = math.gcd(heads, 2)
    step = heads // chunks
    by_head = conv_weight.reshape(KERNEL, HEADS, depth).transpose(1, 0, 2)
    weight = lax.dynamic_slice_in_dim(by_head, rank * heads, heads, axis=0)
    bias = lax.dynamic_slice_in_dim(conv_bias.reshape(HEADS, 1, depth), rank * heads, heads, axis=0)
    scalars = jnp.stack([lengths[0], rank])
    sent = pack(rank[None], (queries, keys, values, grad_out), count, chunks)
    order = []
    for pieces in sent:
        order.append(exchanged(pieces, order[-1] if order else None))
    taps = []
    for chunk in range(chunks):
        at = slice(chunk * step, (chunk + 1) * step)
        grads, part = core(scalars, weight[at], bias[at], order[chunk])
        taps.append(part)
        if chunk < chunks - 1:
            order.append(exchanged(grads, order[-1], False))
    before, grads, taps = order[-1], list(grads), jnp.concatenate(taps, axis=0)
    last = count - 1
    grads[1], before[1] = lax.optimization_barrier((grads[1], before[1]))
    if last > 2:
        (grads[2], taps), before[2] = lax.optimization_barrier(((grads[2], taps), before[2]))
        grads[last], before[last] = lax.optimization_barrier((grads[last], before[last]))
    order.append(exchanged(grads, None, False))
    return unpack(rank[None], doubled(taps, "dp"), order[chunks:], count, chunks)


def solution(mesh):
    return jax.shard_map(
        on_device,
        mesh=mesh,
        in_specs=(
            P("dp", "seq", None),
            P("dp", "seq", None),
            P("dp", "seq", None),
            P("dp", "seq", None),
            P(),
            P(),
            P("dp"),
        ),
        out_specs=(
            P("dp", "seq", None),
            P("dp", "seq", None),
            P("dp", "seq", None),
            P(None, "seq"),
            P("seq"),
        ),
        check_vma=False,
    )
```

```python
import functools
import math

import jax
import jax.numpy as jnp
from jax import lax
from jax.experimental import pallas as pl
from jax.experimental.pallas import tpu as pltpu
from jax.sharding import PartitionSpec as P

HEADS = 16
KERNEL = 31
PAD = 16
masked_score = -1e30
VMEM = pl.BlockSpec(memory_space=pltpu.VMEM)
SMEM = pl.BlockSpec(memory_space=pltpu.SMEM)
LIMIT = 16 * 1024 * 1024
bf16, f32 = jnp.bfloat16, jnp.float32


def pack_first_kernel(far, share, rank_ref, *refs):
    arrays, outs, (plain, sems) = refs[:4], refs[4:-2], refs[-2:]
    high = outs[0].shape[1]
    wide = plain.shape[3]
    copies = []
    for place, distance in enumerate(far):
        at = pl.ds(pl.multiple_of((rank_ref[0] ^ distance) * share, 128), wide)
        for which, array in enumerate(arrays):
            copies.append(
                pltpu.make_async_copy(
                    array.at[0, :, at], plain.at[place, which], sems.at[place, which]
                )
            )
            copies[-1].start()
    for index, copy in enumerate(copies):
        copy.wait()
        place, which = divmod(index, 4)
        outs[place][which] = plain[place, which].T[:high]


def pack_kernel(wanted, share, rank_ref, *refs):
    arrays, outs, turned = refs[:4], refs[4:-1], refs[-1]
    high = outs[0].shape[1]
    for which, array in enumerate(arrays):
        turned[which] = array[0].T
        for (chunk, distance), out in zip(wanted, outs):
            first = pl.multiple_of((rank_ref[0] ^ distance) * share + chunk * high, 16)
            out[which] = turned[which, pl.ds(first, high), :]


def pack(rank, arrays, count, chunks):
    _, frames, width = arrays[0].shape
    share = width // count
    high = share // chunks
    piece = jax.ShapeDtypeStruct((4, high, frames), bf16)
    wide = -(-high // 128) * 128
    far = tuple(range(count - 1, 1, -1)) if share % 128 == 0 and wide <= share else ()
    params = pltpu.CompilerParams(vmem_limit_bytes=LIMIT)
    arrays = [pltpu.with_memory_space_constraint(array, pltpu.HBM) for array in arrays]
    found = {}
    if far:
        outs = pl.pallas_call(
            functools.partial(pack_first_kernel, far, share),
            out_shape=(piece,) * len(far),
            in_specs=[SMEM] + [pl.BlockSpec(memory_space=pltpu.HBM)] * 4,
            out_specs=(VMEM,) * len(far),
            scratch_shapes=[
                pltpu.VMEM((len(far), 4, frames, wide), bf16),
                pltpu.SemaphoreType.DMA((len(far), 4)),
            ],
            compiler_params=params,
            cost_estimate=pl.CostEstimate(
                flops=0, bytes_accessed=16 * frames * wide * len(far), transcendentals=0
            ),
        )(rank, *arrays)
        found.update(zip([(0, distance) for distance in far], outs))
    every = [(chunk, distance) for chunk in range(chunks) for distance in range(count)]
    wanted = tuple(key for key in every if key not in found)
    outs = pl.pallas_call(
        functools.partial(pack_kernel, wanted, share),
        out_shape=(piece,) * len(wanted),
        in_specs=[SMEM] + [VMEM] * 4,
        out_specs=(VMEM,) * len(wanted),
        scratch_shapes=[pltpu.VMEM((4, width, frames), bf16)],
        compiler_params=params,
        cost_estimate=pl.CostEstimate(
            flops=0, bytes_accessed=16 * frames * width, transcendentals=0
        ),
    )(rank, *arrays)
    found.update(zip(wanted, outs))
    return [[found[chunk, distance] for distance in range(count)] for chunk in range(chunks)]


def taken(count):
    return [0] + list(range(count - 1, 0, -1))


def returned(count):
    return [0] + list(range(2, count)) + [1]


def unpack_kernel(count, chunks, rank_ref, *refs):
    pieces, refs = refs[: count * chunks], refs[count * chunks :]
    taps_refs, outs = refs[:-7], refs[-7:-4]
    weight_ref, bias_ref, bias_row, turned = refs[-4:]
    rank = rank_ref[0]
    high = pieces[0].shape[1]
    share = high * chunks
    for which, out in enumerate(outs):
        for chunk in range(chunks):
            for place, distance in enumerate(returned(count)):
                first = pl.multiple_of((rank ^ distance) * share + chunk * high, 16)
                turned[which, pl.ds(first, high), :] = pieces[chunk * count + place][which]
        out[0] = turned[which].T
    taps = taps_refs[0][...] + taps_refs[1][...]
    heads, _, depth = taps.shape
    for head in range(heads):
        at = slice(head * depth, (head + 1) * depth)
        weight_ref[:, at] = taps[head, :KERNEL]
        bias_row[:, at] = taps[head, KERNEL:]
    bias_ref[...] = bias_row[0]


def unpack(rank, taps, pieces, count, chunks):
    _, high, frames = pieces[0][0].shape
    width = high * count * chunks
    whole = jax.ShapeDtypeStruct((1, frames, width), bf16)
    return pl.pallas_call(
        functools.partial(unpack_kernel, count, chunks),
        out_shape=(whole,) * 3
        + (
            jax.ShapeDtypeStruct((KERNEL, width // count), f32),
            jax.ShapeDtypeStruct((width // count,), f32),
        ),
        in_specs=[SMEM] + [VMEM] * (count * chunks + len(taps)),
        out_specs=(VMEM,) * 5,
        scratch_shapes=[
            pltpu.VMEM((1, width // count), f32),
            pltpu.VMEM((3, width, frames), bf16),
        ],
        compiler_params=pltpu.CompilerParams(vmem_limit_bytes=LIMIT),
        cost_estimate=pl.CostEstimate(
            flops=0, bytes_accessed=12 * frames * width, transcendentals=0
        ),
    )(rank, *[part[distance] for part in pieces for distance in returned(count)], *taps)


def core_kernel(count, block, scalars, weight_ref, bias_ref, *refs):
    pieces, outs, taps_ref = refs[:count], refs[count : 2 * count], refs[2 * count]
    q_t, k_t, v_t, a_t, q_n, k_n, v_n, g_n, a_n, probs, shifted, padded = refs[2 * count + 1 :]
    heads, rows, depth = q_n.shape
    frames = pieces[0].shape[2]
    blocks = rows // block
    scale = 1.0 / math.sqrt(depth)
    log_scale = scale * math.log2(math.e)
    length, rank = scalars[0], scalars[1]

    def span(head):
        return slice(head * depth, (head + 1) * depth)

    for distance, piece in zip(taken(count), pieces):
        at = pl.ds(pl.multiple_of((rank ^ distance) * frames, 128), frames)
        q_t[:, at] = piece[0]
        k_t[:, at] = piece[1]
        v_t[:, at] = piece[2]
        for head in range(heads):
            q_n[head, at, :] = piece[0, span(head), :].T
            k_n[head, at, :] = piece[1, span(head), :].T
            v_n[head, at, :] = piece[2, span(head), :].T
            g_n[head, at, :] = piece[3, span(head), :].T

    def forward(index, head):
        cols = pl.ds(pl.multiple_of(index * block, block), block)
        scores = jnp.dot(k_n[head], q_t[span(head), cols], preferred_element_type=f32)
        key_at = lax.broadcasted_iota(jnp.int32, scores.shape, 0)
        scores = jnp.where(key_at < length, scores, masked_score)
        exped = jnp.exp2((scores - jnp.max(scores, axis=0, keepdims=True)) * log_scale)
        found = exped * (1.0 / jnp.sum(exped, axis=0, keepdims=True))
        probs[head, :, cols] = found
        out = jnp.dot(v_t[span(head), :], found.astype(bf16), preferred_element_type=f32)
        frame_at = index * block + lax.broadcasted_iota(jnp.int32, out.shape, 1)
        a_t[span(head), cols] = jnp.where(frame_at < length, out, 0.0).astype(bf16)

    def each_block(body):
        if blocks == 1:
            for head in range(heads):
                body(0, head)
        else:

            def step(index, carry):
                for head in range(heads):
                    body(index, head)
                return carry

            lax.fori_loop(0, blocks, step, 0)

    each_block(forward)

    tall = padded.shape[0]
    padded[0:PAD, :] = jnp.zeros((PAD, depth), f32)
    padded[PAD + rows : tall, :] = jnp.zeros((tall - PAD - rows, depth), f32)

    def shift_all():
        for s in range(8):
            shifted[s] = padded[s : s + tall - 8, :].reshape(tall // 8 - 1, 8, depth)

    step_tiles = 4
    step_rows = 8 * step_tiles

    def window(index, offset):
        return shifted[offset % 8, pl.ds(index * step_tiles + offset // 8, step_tiles)]

    def filtered(head, index, reverse):
        total = None
        for offset in range(1, KERNEL + 1):
            tap = KERNEL - offset if reverse else offset - 1
            term = weight_ref[head, tap : tap + 1, :] * window(index, offset)
            total = term if total is None else total + term
        return total

    def loaded(ref, index):
        at = pl.ds(pl.multiple_of(index * step_rows, step_rows), step_rows)
        return ref[at, :].astype(f32).reshape(step_tiles, 8, depth)

    for head in range(heads):
        for first in range(0, rows, frames):
            at = slice(PAD + first, PAD + first + frames)
            padded[at, :] = a_t[span(head), first : first + frames].T.astype(f32)
        shift_all()

        def conv_step(index, carry, head=head):
            conv_pre = filtered(head, index, False) + bias_ref[head]
            sig = 1.0 / (1.0 + jnp.exp(-conv_pre))
            pre = loaded(g_n.at[head], index) * (sig * (1.0 + conv_pre * (1.0 - sig)))
            pre = pre.astype(bf16).astype(f32)
            at = pl.ds(pl.multiple_of(PAD + index * step_rows, PAD), step_rows)
            padded[at, :] = pre.reshape(step_rows, depth)
            new = []
            for offset in range(1, KERNEL + 1):
                new.append(carry[offset - 1] + jnp.sum(pre * window(index, offset), axis=0))
            new.append(carry[KERNEL] + jnp.sum(pre, axis=0))
            return tuple(new)

        zero = jnp.zeros((8, depth), f32)
        sums = lax.fori_loop(0, rows // step_rows, conv_step, (zero,) * (KERNEL + 1))
        for tap in range(KERNEL + 1):
            taps_ref[head, tap : tap + 1, :] = jnp.sum(sums[tap], axis=0, keepdims=True)
        shift_all()

        def back_step(index, carry, head=head):
            total = loaded(g_n.at[head], index) + filtered(head, index, True)
            total = total.reshape(step_rows, depth)
            frame_at = index * step_rows + lax.broadcasted_iota(jnp.int32, total.shape, 0)
            total = jnp.where(frame_at < length, total, 0.0)
            at = pl.ds(pl.multiple_of(index * step_rows, step_rows), step_rows)
            a_n[head, at, :] = total.astype(bf16)
            return carry

        lax.fori_loop(0, rows // step_rows, back_step, 0)
        for first in range(0, rows, frames):
            a_t[span(head), first : first + frames] = a_n[head, first : first + frames, :].T

    def backward(index, head):
        cols = pl.ds(pl.multiple_of(index * block, block), block)
        score_grad = jnp.dot(v_n[head], a_t[span(head), cols], preferred_element_type=f32)
        found = probs[head, :, cols]
        delta = jnp.sum(found * score_grad, axis=0, keepdims=True)
        diff = (found * (score_grad - delta)).astype(bf16)
        value = jnp.dot(found.astype(bf16), a_n[head, cols, :], preferred_element_type=f32)
        key = jnp.dot(diff, q_n[head, cols, :], preferred_element_type=f32)
        query = jnp.dot(k_t[span(head), :], diff, preferred_element_type=f32)
        q_t[span(head), cols] = (query * scale).astype(bf16)
        return key, value

    def finish(head, key, value):
        for first in range(0, rows, frames):
            at = slice(first, first + frames)
            k_t[span(head), at] = (key[at, :] * scale).astype(bf16).T
            v_t[span(head), at] = value[at, :].astype(bf16).T

    for head in range(heads):
        if blocks == 1:
            finish(head, *backward(0, head))
        else:
            zeros = jnp.zeros((rows, depth), f32)

            def step(index, carry, head=head):
                key, value = backward(index, head)
                return carry[0] + key, carry[1] + value

            finish(head, *lax.fori_loop(0, blocks, step, (zeros, zeros)))

    for distance, out in enumerate(outs):
        at = pl.ds(pl.multiple_of((rank ^ distance) * frames, 128), frames)
        out[0] = q_t[:, at]
        out[1] = k_t[:, at]
        out[2] = v_t[:, at]


def core(scalars, weight, bias, pieces):
    count = len(pieces)
    _, high, frames = pieces[0].shape
    heads, _, depth = weight.shape
    rows = count * frames
    block = math.gcd(rows, 512)
    tall = rows + 2 * PAD + 8
    piece = jax.ShapeDtypeStruct((3, high, frames), bf16)
    turned = pltpu.VMEM((high, rows), bf16)
    plain = pltpu.VMEM((heads, rows, depth), bf16)
    outs = pl.pallas_call(
        functools.partial(core_kernel, count, block),
        out_shape=(piece,) * count + (jax.ShapeDtypeStruct((heads, KERNEL + 1, depth), f32),),
        in_specs=[SMEM] + [VMEM] * (2 + count),
        out_specs=(VMEM,) * (count + 1),
        scratch_shapes=[turned] * 4
        + [plain] * 5
        + [
            pltpu.VMEM((heads, rows, rows), f32),
            pltpu.VMEM((8, tall // 8 - 1, 8, depth), f32),
            pltpu.VMEM((tall, depth), f32),
        ],
        compiler_params=pltpu.CompilerParams(
            vmem_limit_bytes=12 * 2**20 + 8 * heads * rows * rows + 4096 * tall
        ),
        cost_estimate=pl.CostEstimate(
            flops=24 * rows * rows * high,
            bytes_accessed=14 * rows * high,
            transcendentals=heads * rows * rows,
        ),
    )(scalars, weight, bias, *[pieces[distance] for distance in taken(count)])
    return outs[:count], outs[count]


def exchanged(pieces, before, farthest_first=True):
    pieces = list(pieces)
    if before is not None and len(pieces) > 2:
        pieces[:1:-1], before[:0:-1] = lax.optimization_barrier((pieces[:1:-1], before[:0:-1]))
    moved = pieces[:1] * len(pieces)
    order = range(1, len(pieces))
    for distance in reversed(order) if farthest_first else [*order[1:], 1]:
        pairs = [(i, i ^ distance) for i in range(len(pieces))]
        moved[distance] = lax.ppermute(pieces[distance], "seq", pairs)
    return moved


def doubled(array, axis):
    count = lax.axis_size(axis)
    pair, distance = (array, jnp.zeros_like(array)), 1
    while distance < count:
        total = array if distance == 1 else pair[0] + pair[1]
        pairs = [(i, i ^ distance) for i in range(count)]
        pair = (total, lax.ppermute(total, axis, pairs))
        distance *= 2
    return pair


def on_device(queries, keys, values, grad_out, conv_weight, conv_bias, lengths):
    count = lax.axis_size("seq")
    rank = lax.axis_index("seq").astype(jnp.int32)
    width = queries.shape[2]
    depth = width // HEADS
    heads = HEADS // count
    chunks = math.gcd(heads, 2)
    step = heads // chunks
    by_head = conv_weight.reshape(KERNEL, HEADS, depth).transpose(1, 0, 2)
    weight = lax.dynamic_slice_in_dim(by_head, rank * heads, heads, axis=0)
    bias = lax.dynamic_slice_in_dim(conv_bias.reshape(HEADS, 1, depth), rank * heads, heads, axis=0)
    scalars = jnp.stack([lengths[0], rank])
    sent = pack(rank[None], (queries, keys, values, grad_out), count, chunks)
    order = []
    for pieces in sent:
        order.append(exchanged(pieces, order[-1] if order else None))
    taps = []
    for chunk in range(chunks):
        at = slice(chunk * step, (chunk + 1) * step)
        grads, part = core(scalars, weight[at], bias[at], order[chunk])
        taps.append(part)
        if chunk < chunks - 1:
            order.append(exchanged(grads, order[-1], False))
    before, grads, taps = order[-1], list(grads), jnp.concatenate(taps, axis=0)
    last = count - 1
    grads[last - 1], before[1] = lax.optimization_barrier((grads[last - 1], before[1]))
    if last > 2:
        (grads[1], taps), before[2] = lax.optimization_barrier(((grads[1], taps), before[2]))
        grads[last], before[last] = lax.optimization_barrier((grads[last], before[last]))
    order.append(exchanged(grads, None, False))
    return unpack(rank[None], doubled(taps, "dp"), order[chunks:], count, chunks)


def solution(mesh):
    return jax.shard_map(
        on_device,
        mesh=mesh,
        in_specs=(
            P("dp", "seq", None),
            P("dp", "seq", None),
            P("dp", "seq", None),
            P("dp", "seq", None),
            P(),
            P(),
            P("dp"),
        ),
        out_specs=(
            P("dp", "seq", None),
            P("dp", "seq", None),
            P("dp", "seq", None),
            P(None, "seq"),
            P("seq"),
        ),
        check_vma=False,
    )
```
